256 devices in a mesh: row: 8 (over z_hi, core), col: 32 (over z_lo, x, y).
Axes of the slice: x: 4, y: 4, z: 8 (z_hi: 4, z_lo: 2; z = z_hi * 2 + z_lo), core: 2. Of those that a mesh axis runs over, the one named last changes fastest.
Arguments:
- features: bfloat16 [32768, 512], P(('row', 'col')), may hold values from -6 to 6
- cotangent: bfloat16 [32768, 512], P(('row', 'col')), may hold values from -6 to 6
- w_self: bfloat16 [512, 512], replicated, may hold values from -0.25 to 0.25
- w_neigh: bfloat16 [512, 512], replicated, may hold values from -0.75 to 0.75
- out_bias: float32 [512], replicated, may hold values from -4 to 4
- block_vals: bfloat16 [12288, 128, 128], P(('row', 'col')), as said below
- block_rows: int32 [12288], P(('row', 'col')), may hold values from 0 to 31, as said below
- block_cols: int32 [12288], P(('row', 'col')), may hold values from 0 to 7
- block_count: int32 [256], P(('row', 'col')), may hold values from 1 to 48, as said below
Outputs:
- layer_out: bfloat16 [32768, 512], P(('row', 'col'))
- feature_grad: float32 [32768, 512], P(('row', 'col'))
- self_grad: float32 [512, 512], replicated
- neigh_grad: float32 [512, 512], replicated
- bias_grad: float32 [512], replicated
The draws below stay inside these ranges and needn't reach their ends.
Inputs may be any that keep to these rules, and one draw needn't show every extreme that they name: `block_rows`: within one device the live slots name distinct blocks. `block_count`: some device has all 48 slots live. `block_vals`: edge weights are non-negative.
All inputs are finite; a program needn't handle non-finite values.
Results may differ from the reference program's by a relative error of at most 0.0075.
Values may be sent and summed in bfloat16 or wider, within the bound.
No kernel may reach another device: no remote copies, remote signals or barrier semaphores. Data moves between devices by JAX's collectives and lax.ppermute only.
A program may use at most 64 MiB of HBM per device.

```python
import math
import jax
import jax.numpy as jnp
from jax import lax

F = 512
BLOCK = 128
NODE_DEV = 128
TILE_ROWS = 4096
TILE_COLS = 1024
SLOTS = 48
NODES = 32768
DEVICES = 256


def slot_places(key):
    tile_blocks = TILE_ROWS // BLOCK * (TILE_COLS // BLOCK)
    device_keys = jax.random.split(key, DEVICES)

    def chosen_of(device_key):
        return jax.random.permutation(device_key, tile_blocks)[:SLOTS]
    return jax.vmap(chosen_of)(device_keys).reshape(-1).astype(jnp.int32)


def draw_block_rows(key, part):
    places = slot_places(key)
    return (places // (TILE_COLS // BLOCK)).astype(jnp.int32)


def draw_block_cols(key, part):
    places = slot_places(key)
    return (places % (TILE_COLS // BLOCK)).astype(jnp.int32)


def draw_block_count(key, part):
    key = jax.random.fold_in(key, 3)
    key_draw, key_top = jax.random.split(key)
    picked = jax.random.randint(key_draw, (DEVICES,), 0, SLOTS + 1)
    counts = jnp.maximum(1, picked * picked // SLOTS)
    busiest = jax.random.randint(key_top, (), 0, DEVICES)
    return jnp.where(jnp.arange(DEVICES) == busiest, SLOTS, counts).astype(jnp.int32)


def draw_block_vals(key, part):
    key = jax.random.fold_in(key, 4)
    key_mask, key_base, key_rowsc, key_colsc = jax.random.split(key, 4)
    shape = (DEVICES * SLOTS, BLOCK, BLOCK)
    present = jax.random.uniform(key_mask, shape) < 0.5
    base = jnp.exp(0.4 * jax.random.normal(key_base, shape, jnp.float32))
    row_scale = jnp.exp(jax.random.uniform(key_rowsc, (DEVICES * SLOTS, BLOCK, 1), jnp.float32, math.log(0.3), math.log(3.0)))
    col_scale = jnp.exp(jax.random.uniform(key_colsc, (DEVICES * SLOTS, 1, BLOCK), jnp.float32, math.log(0.3), math.log(3.0)))
    values = jnp.where(present, base * row_scale * col_scale, 0.0)
    return values.astype(jnp.bfloat16)


def shard_levels(rng, extent, pieces, least, top_value):
    factor_of = 1.0
    for position, shards_of in pieces:
        steps = jax.random.uniform(jax.random.fold_in(jax.random.fold_in(rng, 6), position), (shards_of,), jnp.float32, least / len(pieces), top_value / len(pieces))
        factor_of = factor_of * jnp.repeat(jnp.exp(steps), extent[position] // shards_of).reshape((-1,) + (1,) * (len(extent) - 1 - position))
    return factor_of


def bell_draw(stream_key, shape, deviation, bound, pieces=(), dtype=jnp.bfloat16):
    result = deviation * jax.random.normal(stream_key, shape, jnp.float32)
    if pieces:
        result = result * shard_levels(stream_key, shape, pieces, -0.22, 0.18)
    return jnp.clip(result, -bound, bound).astype(dtype)


def setup_inputs(seed: int = 0) -> dict:
    key_of = jax.random.split(jax.random.key(seed), 10)
    return {
        "features": bell_draw(key_of[0], (NODES, F), 1.0, 6.0, ((0, 256),)),
        "cotangent": bell_draw(key_of[1], (NODES, F), 1.0, 6.0, ((0, 256),)),
        "w_self": bell_draw(key_of[2], (F, F), F ** -0.5, 0.25),
        "w_neigh": bell_draw(key_of[3], (F, F), (F // 8) ** -0.5, 0.75),
        "out_bias": bell_draw(key_of[4], (F,), 1.0, 4.0, (), jnp.float32),
        "block_vals": draw_block_vals(jax.random.fold_in(key_of[9], 71), 0),
        "block_rows": draw_block_rows(jax.random.fold_in(key_of[9], 71), 0),
        "block_cols": draw_block_cols(jax.random.fold_in(key_of[9], 71), 0),
        "block_count": draw_block_count(jax.random.fold_in(key_of[9], 71), 0),
    }


def place_of(flat_index, block_rows, block_cols):
    device = flat_index // SLOTS
    col_groups = TILE_ROWS // NODE_DEV
    row_begin = device // col_groups * TILE_ROWS + block_rows[flat_index] * BLOCK
    local_col = block_cols[flat_index] * BLOCK
    col_begin = (local_col // NODE_DEV * col_groups + device % col_groups) * NODE_DEV + local_col % NODE_DEV
    return (row_begin.astype(jnp.int32), col_begin.astype(jnp.int32))

def reference(features, cotangent, w_self, w_neigh, out_bias, block_vals, block_rows, block_cols, block_count):

    def forward_device(device, carry):

        def forward_slot(slot_index, inner):
            partial_value, totals = inner
            flat_index = (device * SLOTS + slot_index).astype(jnp.int32)
            row_begin, col_begin = place_of(flat_index, block_rows, block_cols)
            block_tile = block_vals[flat_index]
            source = lax.dynamic_slice_in_dim(features, col_begin, BLOCK, 0)
            block_term = jnp.dot(block_tile, source, preferred_element_type=jnp.float32)
            row_weight = lax.optimization_barrier(jnp.sum(block_tile.astype(jnp.float32), axis=1))
            partial_value = lax.dynamic_update_slice_in_dim(partial_value, lax.dynamic_slice_in_dim(partial_value, row_begin, BLOCK, 0) + block_term, row_begin, 0)
            totals = lax.dynamic_update_slice_in_dim(totals, lax.dynamic_slice_in_dim(totals, row_begin, BLOCK, 0) + row_weight, row_begin, 0)
            return (partial_value, totals)
        return lax.fori_loop(0, block_count[device], forward_slot, carry)
    start_carry = (jnp.zeros((NODES, F), jnp.float32), jnp.zeros((NODES,), jnp.float32))
    neigh_sum, totals = lax.fori_loop(0, DEVICES, forward_device, start_carry)
    degree = 1.0 + totals
    mean_agg = (neigh_sum / degree[:, None]).astype(jnp.bfloat16)
    pre_act = jnp.dot(features, w_self, preferred_element_type=jnp.float32) + jnp.dot(mean_agg, w_neigh, preferred_element_type=jnp.float32) + out_bias
    layer_out = jax.nn.silu(pre_act).astype(jnp.bfloat16)
    sigmoid_val = jax.nn.sigmoid(pre_act)
    grad_pre = (cotangent.astype(jnp.float32) * sigmoid_val * (1.0 + pre_act * (1.0 - sigmoid_val))).astype(jnp.bfloat16)
    grad_scale = 1.0 / math.sqrt(NODES)
    self_grad = jnp.dot(features.T, grad_pre, preferred_element_type=jnp.float32) * grad_scale
    neigh_grad = jnp.dot(mean_agg.T, grad_pre, preferred_element_type=jnp.float32) * grad_scale
    bias_grad = lax.optimization_barrier(jnp.sum(grad_pre.astype(jnp.float32), axis=0)) * grad_scale
    back_mean = jnp.dot(grad_pre, w_neigh.T, preferred_element_type=jnp.float32)
    back_scaled = (back_mean / degree[:, None]).astype(jnp.bfloat16)

    def backward_device(device, spread):

        def backward_slot(slot_index, current):
            flat_index = (device * SLOTS + slot_index).astype(jnp.int32)
            row_begin, col_begin = place_of(flat_index, block_rows, block_cols)
            grad_rows = lax.dynamic_slice_in_dim(back_scaled, row_begin, BLOCK, 0)
            block_term = lax.dot_general(block_vals[flat_index], grad_rows, (((0,), (0,)), ((), ())), preferred_element_type=jnp.float32)
            return lax.dynamic_update_slice_in_dim(current, lax.dynamic_slice_in_dim(current, col_begin, BLOCK, 0) + block_term, col_begin, 0)
        return lax.fori_loop(0, block_count[device], backward_slot, spread)
    spread = lax.fori_loop(0, DEVICES, backward_device, jnp.zeros((NODES, F), jnp.float32))
    feature_grad = jnp.dot(grad_pre, w_self.T, preferred_element_type=jnp.float32) + spread
    return (layer_out, feature_grad, self_grad, neigh_grad, bias_grad)
```

```python
import functools
import math

import jax
import jax.numpy as jnp
from jax import lax
from jax.experimental import pallas as pl
from jax.experimental.pallas import tpu as pltpu
from jax.sharding import PartitionSpec as P

BF = jnp.bfloat16
F32 = jnp.float32
AXES = ("row", "col")
ZH, CORE, ZL, X, Y = 4, 2, 2, 4, 4
DEVICES = ZH * CORE * ZL * X * Y
VMEM = pl.BlockSpec(memory_space=pltpu.VMEM)
SMEM = pl.BlockSpec(memory_space=pltpu.SMEM)
ANY = pl.BlockSpec(memory_space=pl.ANY)
CONTRACT_ROWS = (((0,), (0,)), ((), ()))
CONTRACT_COLS = (((1,), (1,)), ((), ()))
LIMIT = 48 * 1024 * 1024


def coords(device):
    y = device % Y
    x = device // Y % X
    zl = device // (Y * X) % ZL
    core = device // (Y * X * ZL) % CORE
    zh = device // (Y * X * ZL * CORE)
    return zh, core, zl, x, y


def shift(value, zh=0, core=0, zl=0, x=0, y=0):
    pairs = []
    for device in range(DEVICES):
        a, b, c, d, e = coords(device)
        a, b, c, d, e = (a + zh) % ZH, (b + core) % CORE, (c + zl) % ZL, (d + x) % X, (e + y) % Y
        pairs.append((device, (((a * CORE + b) * ZL + c) * X + d) * Y + e))
    return lax.ppermute(value, AXES, pairs)


def others(axis):
    return (1, 3, 2)


def call(kernel, outs, args, specs, scratch=(), flops=0, out_specs=None):
    size = sum(math.prod(o.shape) * o.dtype.itemsize for o in outs)
    size += sum(math.prod(a.shape) * a.dtype.itemsize for a in args)
    return pl.pallas_call(
        kernel,
        out_shape=tuple(outs),
        in_specs=list(specs),
        out_specs=tuple(out_specs or [VMEM] * len(outs)),
        scratch_shapes=list(scratch),
        compiler_params=pltpu.CompilerParams(vmem_limit_bytes=LIMIT),
        cost_estimate=pl.CostEstimate(flops=flops, bytes_accessed=size, transcendentals=0),
    )(*args)


def shaped(shape, dtype):
    return jax.ShapeDtypeStruct(shape, dtype)


def prepare_kernel(place, vals, weights, turned):
    slots = vals.shape[0]
    weights[...] = jnp.zeros_like(weights)
    ones = jnp.ones((8, 128), BF)

    def step(slot, carry):
        block = vals[slot]
        sums = lax.dot_general(ones, block, CONTRACT_COLS, preferred_element_type=F32)
        weights[place[slot]] += sums
        turned[slot] = block.T
        return carry

    lax.fori_loop(0, slots, step, 0)


def prepare(place, vals):
    slots = vals.shape[0]
    return call(
        prepare_kernel,
        [shaped((33, 8, 128), F32), shaped(vals.shape, BF)],
        (place, vals),
        [SMEM, VMEM],
    )


GROUP = 4


def forward_kernel(half, count, place, source, vals, *refs):
    pieces, outs, (panel, total, sems) = refs[:8], refs[8:12], refs[12:]
    copies = [
        pltpu.make_async_copy(piece.at[:, pl.ds(256 * half, 256)], panel.at[k], sems.at[k])
        for k, piece in enumerate(pieces)
    ]
    for copy in copies:
        copy.start()

    def clear(k, carry):
        total[k] = jnp.zeros((128, 256), F32)
        return carry

    lax.fori_loop(0, 33, clear, 0)
    for copy in copies:
        copy.wait()

    def step(i, carry):
        slots = [i * GROUP + u for u in range(GROUP)]
        terms = [
            jnp.dot(vals[s], panel[source[s]], preferred_element_type=F32) for s in slots
        ]
        for s, term in zip(slots, terms):
            total[place[s]] += term
        return carry

    lax.fori_loop(0, (count[0] + GROUP - 1) // GROUP, step, 0)

    def finish(k, carry):
        for part, out in enumerate(outs):
            out[k] = total[part * 8 + k].astype(out.dtype)
        return carry

    lax.fori_loop(0, 8, finish, 0)


def forward(half, count, place, source, vals, pieces):
    return call(
        functools.partial(forward_kernel, half),
        [shaped((8, 128, 256), F32)] + [shaped((8, 128, 256), BF)] * 3,
        (count, place, source, vals, *pieces),
        [SMEM, SMEM, SMEM, VMEM] + [ANY] * 8,
        [
            pltpu.VMEM((8, 128, 256), BF),
            pltpu.VMEM((33, 128, 256), F32),
            pltpu.SemaphoreType.DMA((8,)),
        ],
        flops=2 * 48 * 128 * 128 * 256,
    )


def merge_kernel(own, a, b, c, *outs):
    step = outs[0].shape[0]
    for part, out in enumerate(outs):
        for k in range(step):
            at = part * step + k
            total = own[at] + a[at].astype(F32) + b[at].astype(F32) + c[at].astype(F32)
            out[k] = total.astype(out.dtype)


def merge(own, a, b, c):
    lead, rows, width = own.shape
    piece = (lead // 4, rows, width)
    return call(
        merge_kernel,
        [shaped(piece, F32)] + [shaped(piece, BF)] * 3,
        (own, a, b, c),
        [VMEM] * 4,
    )


def backward_kernel(count, from_a, from_b, place, vals, *refs):
    parts_a, parts_b, outs = refs[:4], refs[4:8], refs[8:10]
    panel_a, panel_b, total, sems = refs[10:]
    copies = []
    for k in range(4):
        copies.append(
            pltpu.make_async_copy(parts_a[k], panel_a.at[pl.ds(8 * k, 8)], sems.at[k])
        )
        copies.append(
            pltpu.make_async_copy(parts_b[k], panel_b.at[pl.ds(8 * k, 8)], sems.at[4 + k])
        )
    for copy in copies:
        copy.start()

    def clear(k, carry):
        total[k] = jnp.zeros((128, 512), F32)
        return carry

    lax.fori_loop(0, 9, clear, 0)
    for copy in copies:
        copy.wait()

    def step(i, carry):
        for u in range(GROUP):
            s = i * GROUP + u
            block = vals[s]
            first = jnp.dot(block, panel_a[from_a[s]], preferred_element_type=F32)
            second = jnp.dot(block, panel_b[from_b[s]], preferred_element_type=F32)
            total[place[s], :, :256] += first
            total[place[s], :, 256:] += second
        return carry

    lax.fori_loop(0, (count[0] + GROUP - 1) // GROUP, step, 0)

    def finish(k, carry):
        for part, out in enumerate(outs):
            out[k] = total[part * 4 + k].astype(out.dtype)
        return carry

    lax.fori_loop(0, 4, finish, 0)


def backward(count, from_a, from_b, place, turned, parts_a, parts_b):
    return call(
        backward_kernel,
        [shaped((4, 128, 512), F32), shaped((4, 128, 512), F32)],
        (count, from_a, from_b, place, turned, *parts_a, *parts_b),
        [SMEM] * 4 + [VMEM] + [ANY] * 8,
        [
            pltpu.VMEM((32, 128, 256), BF),
            pltpu.VMEM((32, 128, 256), BF),
            pltpu.VMEM((9, 128, 512), F32),
            pltpu.SemaphoreType.DMA((8,)),
        ],
        flops=2 * 48 * 128 * 128 * 512,
    )


def pair_kernel(own, got, *outs):
    for k, out in enumerate(outs):
        out[...] = (own[k] + got[k].astype(F32)).astype(out.dtype)


def pair(own, got):
    piece = own.shape[1:]
    return call(
        pair_kernel,
        [shaped(piece, F32)] + [shaped(piece, BF)] * 3,
        (own, got),
        [VMEM] * 2,
    )


BIAS_ROWS = 16


def weights_kernel(keep, give, grad, keep_out, give_out):
    grads = grad[...]
    bias = jnp.sum(grads.astype(F32), axis=0, keepdims=True)
    bias = jnp.broadcast_to(bias, (BIAS_ROWS, 512))
    for lhs, out in ((keep, keep_out), (give, give_out)):
        for k in range(4):
            out[k, :128, :] = lax.dot_general(
                lhs[:, 128 * k : 128 * (k + 1)], grads, CONTRACT_ROWS, preferred_element_type=F32
            )
            out[k, 128:, :] = bias


def weights(keep, give, grad):
    out = shaped((4, 128 + BIAS_ROWS, 512), F32)
    return call(weights_kernel, [out, out], (keep, give, grad), [VMEM] * 3, flops=4 * 128 * 512 * 512)


def local(
    features, cotangent, w_self, w_neigh, out_bias, block_vals, block_rows, block_cols, block_count
):
    device = lax.axis_index("row") * 32 + lax.axis_index("col")
    my_zh, my_core, my_zl, my_x, my_y = coords(device)
    slots = block_vals.shape[0]
    live = jnp.arange(slots, dtype=jnp.int32) < block_count[0]
    rel_z = (block_rows // 16 - my_zl) % ZL
    rel_x = (block_rows // 4 % 4 - my_x) % X
    rel_y = (block_rows % 4 - my_y) % Y
    rows_a = rel_x * 8 + rel_y * 2 + rel_z
    rows_b = rel_y * 8 + rel_x * 2 + rel_z
    place_a = jnp.where(live, rows_a, 32)
    place_b = jnp.where(live, rows_b, 32)
    rel_h = (block_cols // 2 - my_zh) % ZH
    rel_c = (block_cols % 2 - my_core) % CORE
    source = rel_h * 2 + rel_c
    back_place = jnp.where(live, rel_c * 4 + rel_h, 8)

    ahead = {k: shift(features, zh=-k) for k in others("zh")}
    ahead[0] = features
    pieces = []
    for k in range(4):
        pieces += [ahead[k], shift(ahead[k], core=1)]

    weight_parts, turned = prepare(place_a, block_vals)
    weight = weight_parts[0:8]
    for k in others("x"):
        weight = weight + shift(weight_parts[8 * k : 8 * k + 8], x=k)
    weight_own = weight[0:2]
    for k in others("y"):
        weight_own = weight_own + shift(weight[2 * k : 2 * k + 2], y=k)
    degree = 1.0 + weight_own[0, 0] + shift(weight_own[1], zl=1)[0]
    inverse = (1.0 / degree)[:, None]

    self_pre = jnp.dot(features, w_self, preferred_element_type=F32) + out_bias

    parts = forward(0, block_count, place_a, source, block_vals, pieces)
    got_a = [shift(parts[k], x=k) for k in others("x")]
    own_a = parts[0]
    parts = forward(1, block_count, place_b, source, block_vals, pieces)
    got_b = [shift(parts[k], y=k) for k in others("y")]
    own_b = parts[0]
    parts = merge(own_a, *got_a)
    got_a = [shift(parts[k], y=k) for k in others("y")]
    own_a = parts[0]
    parts = merge(own_b, *got_b)
    got_b = [shift(parts[k], x=k) for k in others("x")]
    own_b = parts[0]
    sums = []
    for own, got in ((own_a, got_a), (own_b, got_b)):
        for part in got:
            own = own + part.astype(F32)
        sums.append(own)
    sums = jnp.concatenate(sums, axis=2)
    neigh_sum = sums[0] + shift(sums[1], zl=1)

    mean_agg = (neigh_sum * inverse).astype(BF)
    pre_act = self_pre + jnp.dot(mean_agg, w_neigh, preferred_element_type=F32)
    sigmoid_val = jax.nn.sigmoid(pre_act)
    layer_out = (pre_act * sigmoid_val).astype(BF)
    grad_pre = (
        cotangent.astype(F32) * sigmoid_val * (1.0 + pre_act * (1.0 - sigmoid_val))
    ).astype(BF)
    back_mean = lax.dot_general(grad_pre, w_neigh, CONTRACT_COLS, preferred_element_type=F32)
    back_scaled = (back_mean * inverse).astype(BF)

    both = jnp.stack([back_scaled, shift(back_scaled, zl=1)])
    near_a = {0: both[:, :, :256]}
    near_b = {0: both[:, :, 256:]}
    for k in others("y"):
        near_a[k] = shift(near_a[0], y=-k)
        near_b[k] = shift(near_b[0], x=-k)
    far_a = {0: jnp.concatenate([near_a[k] for k in range(4)])}
    far_b = {0: jnp.concatenate([near_b[k] for k in range(4)])}
    for k in others("x"):
        far_a[k] = shift(far_a[0], x=-k)
        far_b[k] = shift(far_b[0], y=-k)

    turn = my_x * 128
    feat_turn = lax.dynamic_slice_in_dim(jnp.concatenate([features, features], 1), turn, 512, 1)
    mean_turn = lax.dynamic_slice_in_dim(jnp.concatenate([mean_agg, mean_agg], 1), turn, 512, 1)
    first = my_core == 0
    keep = jnp.where(first, feat_turn, mean_turn)
    give = jnp.where(first, mean_turn, feat_turn)
    keep_part, give_part = weights(keep, give, grad_pre)
    parts = pair(keep_part, shift(give_part, core=1))
    got = [shift(parts[k], x=k) for k in others("x")]
    chunk = parts[0]
    for part in got:
        chunk = chunk + part.astype(F32)

    def y_part(k):
        begin = (my_y + k) % 4 * 32
        rows = lax.dynamic_slice_in_dim(chunk, begin, 32, 0)
        return jnp.concatenate([rows, chunk[128:136]])

    strip = y_part(0)
    for k in others("y"):
        strip = strip + shift(y_part(k), y=k)
    strip = strip + shift(strip, zl=1)
    for_zh = strip
    for k in others("zh"):
        strip = strip + shift(for_zh, zh=k)
    scale = 1.0 / math.sqrt(128 * DEVICES)
    bias_grad = strip[32] * scale
    strip_out = (strip[:32] * scale).astype(BF)
    strips = {0: strip_out}
    for k in others("y"):
        strips[k] = shift(strip_out, y=-k)
    chunk_out = jnp.concatenate([strips[k] for k in range(4)])
    chunk_out = jnp.concatenate([chunk_out, chunk_out])
    chunk_out = lax.dynamic_slice_in_dim(chunk_out, (4 - my_y) % 4 * 32, 128, 0)
    chunks = {0: chunk_out}
    for k in others("x"):
        chunks[k] = shift(chunk_out, x=-k)
    matrix = jnp.concatenate([chunks[k] for k in range(4)])
    matrix = jnp.concatenate([matrix, matrix])
    matrix = lax.dynamic_slice_in_dim(matrix, (4 - my_x) % 4 * 128, 512, 0)
    other = shift(matrix, core=1)
    self_grad = jnp.where(first, matrix, other).astype(F32)
    neigh_grad = jnp.where(first, other, matrix).astype(F32)

    grad_self = lax.dot_general(grad_pre, w_self, CONTRACT_COLS, preferred_element_type=F32)
    own, give = backward(
        block_count,
        rows_a,
        rows_b,
        back_place,
        turned,
        [far_a[k] for k in range(4)],
        [far_b[k] for k in range(4)],
    )
    parts = pair(own, shift(give, core=1))
    spread = parts[0]
    for k in others("zh"):
        spread = spread + shift(parts[k], zh=k).astype(F32)
    feature_grad = grad_self + spread
    return layer_out, feature_grad, self_grad, neigh_grad, bias_grad


def solution(mesh):
    return jax.shard_map(
        local,
        mesh=mesh,
        in_specs=(
            P(("row", "col"), None),
            P(("row", "col"), None),
            P(),
            P(),
            P(),
            P(("row", "col"), None, None),
            P(("row", "col")),
            P(("row", "col")),
            P(("row", "col")),
        ),
        out_specs=(P(("row", "col"), None), P(("row", "col"), None), P(), P(), P()),
        check_vma=False,
    )
```

```python
import functools
import math

import jax
import jax.numpy as jnp
from jax import lax
from jax.experimental import pallas as pl
from jax.experimental.pallas import tpu as pltpu
from jax.sharding import PartitionSpec as P

BF = jnp.bfloat16
F32 = jnp.float32
AXES = ("row", "col")
ZH, CORE, ZL, X, Y = 4, 2, 2, 4, 4
DEVICES = ZH * CORE * ZL * X * Y
VMEM = pl.BlockSpec(memory_space=pltpu.VMEM)
SMEM = pl.BlockSpec(memory_space=pltpu.SMEM)
ANY = pl.BlockSpec(memory_space=pl.ANY)
CONTRACT_ROWS = (((0,), (0,)), ((), ()))
CONTRACT_COLS = (((1,), (1,)), ((), ()))
LIMIT = 48 * 1024 * 1024


def coords(device):
    y = device % Y
    x = device // Y % X
    zl = device // (Y * X) % ZL
    core = device // (Y * X * ZL) % CORE
    zh = device // (Y * X * ZL * CORE)
    return zh, core, zl, x, y


def shift(value, zh=0, core=0, zl=0, x=0, y=0):
    pairs = []
    for device in range(DEVICES):
        a, b, c, d, e = coords(device)
        a, b, c, d, e = (a + zh) % ZH, (b + core) % CORE, (c + zl) % ZL, (d + x) % X, (e + y) % Y
        pairs.append((device, (((a * CORE + b) * ZL + c) * X + d) * Y + e))
    return lax.ppermute(value, AXES, pairs)


def others(axis):
    return (1, 3, 2)


def call(kernel, outs, args, specs, scratch=(), flops=0, out_specs=None):
    size = sum(math.prod(o.shape) * o.dtype.itemsize for o in outs)
    size += sum(math.prod(a.shape) * a.dtype.itemsize for a in args)
    return pl.pallas_call(
        kernel,
        out_shape=tuple(outs),
        in_specs=list(specs),
        out_specs=tuple(out_specs or [VMEM] * len(outs)),
        scratch_shapes=list(scratch),
        compiler_params=pltpu.CompilerParams(vmem_limit_bytes=LIMIT),
        cost_estimate=pl.CostEstimate(flops=flops, bytes_accessed=size, transcendentals=0),
    )(*args)


def shaped(shape, dtype):
    return jax.ShapeDtypeStruct(shape, dtype)


def row_weights_kernel(count, place, vals, weights):
    weights[...] = jnp.zeros_like(weights)
    ones = jnp.ones((8, 128), BF)

    def step(i, carry):
        slots = [i * GROUP + u for u in range(GROUP)]
        sums = [
            lax.dot_general(ones, vals[s], CONTRACT_COLS, preferred_element_type=F32) for s in slots
        ]
        for s, term in zip(slots, sums):
            weights[place[s]] += term
        return carry

    lax.fori_loop(0, (count[0] + GROUP - 1) // GROUP, step, 0)


def row_weights(count, place, vals):
    return call(
        row_weights_kernel,
        [shaped((33, 8, 128), F32)],
        (count, place, vals),
        [SMEM, SMEM, VMEM],
    )[0]


def turn_kernel(vals, turned):
    def step(i, carry):
        for u in range(GROUP):
            turned[i * GROUP + u] = vals[i * GROUP + u].T
        return carry

    lax.fori_loop(0, vals.shape[0] // GROUP, step, 0)


def turn(vals):
    return call(turn_kernel, [shaped(vals.shape, BF)], (vals,), [VMEM], flops=6 * 10**9)[0]


GROUP = 4
PAD = 16


def put_weights(out, rows, value):
    count = value.shape[0]
    if out.dtype == F32:
        out[rows : rows + count, :128] = value
        return
    out[rows:, :] = jnp.zeros((PAD, out.shape[1]), out.dtype)
    lead = value.astype(BF)
    trail = (value - lead.astype(F32)).astype(BF)
    both = jnp.concatenate([lead.astype(F32), trail.astype(F32)], axis=1)
    both = jnp.concatenate([both, jnp.zeros((PAD - count, 256), F32)], axis=0)
    out[rows:, :256] = both.astype(BF)


def get_weights(ref, rows, count):
    got = ref[rows : rows + PAD, :256].astype(F32)[:count]
    if ref.dtype == F32:
        return got[:, :128]
    return got[:, :128] + got[:, 128:]


def forward_kernel(half, count, place, source, vals, *refs):
    weights = None
    if half == 0:
        weights, refs = refs[0], refs[1:]
    pieces, outs, (panel, total, sems) = refs[:8], refs[8:12], refs[12:]
    copies = [
        pltpu.make_async_copy(piece.at[:, pl.ds(256 * half, 256)], panel.at[k], sems.at[k])
        for k, piece in enumerate(pieces)
    ]
    for copy in copies:
        copy.start()

    def clear(k, carry):
        total[k] = jnp.zeros((128, 256), F32)
        return carry

    lax.fori_loop(0, 33, clear, 0)
    for copy in copies:
        copy.wait()

    def step(i, carry):
        slots = [i * GROUP + u for u in range(GROUP)]
        terms = [
            jnp.dot(vals[s], panel[source[s]], preferred_element_type=F32) for s in slots
        ]
        for s, term in zip(slots, terms):
            total[place[s]] += term
        return carry

    lax.fori_loop(0, (count[0] + GROUP - 1) // GROUP, step, 0)

    def finish(k, carry):
        for part, out in enumerate(outs):
            begin = pl.multiple_of(k * 128, 128)
            out[pl.ds(begin, 128), :] = total[part * 8 + k].astype(out.dtype)
        return carry

    lax.fori_loop(0, 8, finish, 0)
    if weights is not None:
        for part, out in enumerate(outs):
            rows = [weights[part * 8 + k, 0:1, :] for k in range(8)]
            put_weights(out, 1024, jnp.concatenate(rows, axis=0))


def forward(half, count, place, source, vals, pieces, weights=None):
    rows = 1024 + (PAD if half == 0 else 0)
    extra = [weights] if half == 0 else []
    return call(
        functools.partial(forward_kernel, half),
        [shaped((rows, 256), F32)] + [shaped((rows, 256), BF)] * 3,
        (count, place, source, vals, *extra, *pieces),
        [SMEM, SMEM, SMEM, VMEM] + [VMEM] * len(extra) + [ANY] * 8,
        [
            pltpu.VMEM((8, 128, 256), BF),
            pltpu.VMEM((33, 128, 256), F32),
            pltpu.SemaphoreType.DMA((8,)),
        ],
        flops=2 * 48 * 128 * 128 * 256,
    )


def merge_kernel(carries, own, a, b, c, *outs):
    for part, out in enumerate(outs):
        rows = pl.ds(256 * part, 256)
        total = own[rows] + a[rows].astype(F32) + b[rows].astype(F32) + c[rows].astype(F32)
        out[:256] = total.astype(out.dtype)
    if carries:
        weight = sum(get_weights(ref, 1024, 8) for ref in (own, a, b, c))
        for part, out in enumerate(outs):
            put_weights(out, 256, weight[2 * part : 2 * part + 2])


def merge(carries, own, a, b, c):
    rows = 256 + (PAD if carries else 0)
    return call(
        functools.partial(merge_kernel, carries),
        [shaped((rows, 256), F32)] + [shaped((rows, 256), BF)] * 3,
        (own, a, b, c),
        [VMEM] * 4,
    )


def join_kernel(*refs):
    parts_a, parts_b, (keep, weight_out, give) = refs[:4], refs[4:8], refs[8:]
    for at, parts in ((0, parts_a), (256, parts_b)):
        total = parts[0][:256]
        for part in parts[1:]:
            total += part[:256].astype(F32)
        keep[:, at : at + 256] = total
        give[:256, at : at + 256] = total.astype(BF)
    weight = sum(get_weights(ref, 256, 2) for ref in parts_a)
    weight_out[0:2, :] = weight
    put_weights(give, 256, weight)


def join(parts_a, parts_b):
    return call(
        join_kernel,
        [shaped((256, 512), F32), shaped((8, 128), F32), shaped((256 + PAD, 512), BF)],
        (*parts_a, *parts_b),
        [VMEM] * 8,
    )


def node_kernel(
    keep, weight, got, self_pre, cot, w_neigh, layer_out, mean_out, grad_out, back_a, back_b
):
    came = get_weights(got, 256, 2)
    for k in range(2):
        rows, back = slice(128 * k, 128 * k + 128), slice(128 - 128 * k, 256 - 128 * k)
        degree = 1.0 + weight[k : k + 1, :] + came[1 - k : 2 - k, :]
        inverse = 1.0 / jnp.broadcast_to(degree, (128, 128)).T
        inverse = jnp.concatenate([inverse] * 4, axis=1)
        mean = ((keep[rows] + got[back].astype(F32)) * inverse).astype(BF)
        pre_act = self_pre[rows] + jnp.dot(mean, w_neigh[...], preferred_element_type=F32)
        sigmoid_val = jax.nn.sigmoid(pre_act)
        grad = cot[rows].astype(F32) * sigmoid_val * (1.0 + pre_act * (1.0 - sigmoid_val))
        grad = grad.astype(BF)
        back_mean = lax.dot_general(
            grad, w_neigh[...], CONTRACT_COLS, preferred_element_type=F32
        )
        scaled = (back_mean * inverse).astype(BF)
        back_a[rows, :] = scaled[:, :256]
        back_b[rows, :] = scaled[:, 256:]
        if k == 0:
            layer_out[...] = (pre_act * sigmoid_val).astype(BF)
            mean_out[...] = mean
            grad_out[...] = grad


def node(keep, weight, got, self_pre, cot, w_neigh):
    wide = shaped((128, 512), BF)
    half = shaped((256, 256), BF)
    return call(
        node_kernel,
        [wide, wide, wide, half, half],
        (keep, weight, got, self_pre, cot, w_neigh),
        [VMEM] * 6,
        flops=8 * 128 * 512 * 512,
    )


def backward_kernel(count, from_a, from_b, place, vals, *refs):
    parts_a, parts_b, outs = refs[:4], refs[4:8], refs[8:10]
    panel_a, panel_b, total, sems = refs[10:]
    copies = []
    for k in range(4):
        rows = pl.ds(1024 * k, 1024)
        copies.append(pltpu.make_async_copy(parts_a[k], panel_a.at[rows], sems.at[k]))
        copies.append(pltpu.make_async_copy(parts_b[k], panel_b.at[rows], sems.at[4 + k]))
    for copy in copies:
        copy.start()

    def clear(k, carry):
        total[k] = jnp.zeros((128, 512), F32)
        return carry

    lax.fori_loop(0, 9, clear, 0)
    for copy in copies:
        copy.wait()

    def step(i, carry):
        for u in range(GROUP):
            s = i * GROUP + u
            block = vals[s]
            rows_a = pl.ds(pl.multiple_of(from_a[s] * 128, 128), 128)
            rows_b = pl.ds(pl.multiple_of(from_b[s] * 128, 128), 128)
            first = jnp.dot(block, panel_a[rows_a, :], preferred_element_type=F32)
            second = jnp.dot(block, panel_b[rows_b, :], preferred_element_type=F32)
            total[place[s], :, :256] += first
            total[place[s], :, 256:] += second
        return carry

    lax.fori_loop(0, (count[0] + GROUP - 1) // GROUP, step, 0)

    def finish(k, carry):
        for part, out in enumerate(outs):
            out[k] = total[part * 4 + k].astype(out.dtype)
        return carry

    lax.fori_loop(0, 4, finish, 0)


def backward(count, from_a, from_b, place, turned, parts_a, parts_b):
    return call(
        backward_kernel,
        [shaped((4, 128, 512), F32), shaped((4, 128, 512), BF)],
        (count, from_a, from_b, place, turned, *parts_a, *parts_b),
        [SMEM] * 4 + [VMEM] + [ANY] * 8,
        [
            pltpu.VMEM((4096, 256), BF),
            pltpu.VMEM((4096, 256), BF),
            pltpu.VMEM((9, 128, 512), F32),
            pltpu.SemaphoreType.DMA((8,)),
        ],
        flops=2 * 48 * 128 * 128 * 512,
    )


def pair_kernel(own, got, *outs):
    for k, out in enumerate(outs):
        out[...] = (own[k] + got[k].astype(F32)).astype(out.dtype)


def pair(own, got):
    piece = own.shape[1:]
    return call(
        pair_kernel,
        [shaped(piece, F32)] + [shaped(piece, BF)] * 3,
        (own, got),
        [VMEM] * 2,
    )


BIAS_ROWS = 16


def weights_kernel(keep, give, grad, keep_out, give_out):
    grads = grad[...]
    bias = jnp.sum(grads.astype(F32), axis=0, keepdims=True)
    bias = jnp.broadcast_to(bias, (BIAS_ROWS, 512))
    for lhs, out in ((keep, keep_out), (give, give_out)):
        for k in range(4):
            out[k, :128, :] = lax.dot_general(
                lhs[:, 128 * k : 128 * (k + 1)], grads, CONTRACT_ROWS, preferred_element_type=F32
            )
            out[k, 128:, :] = bias


def weights(keep, give, grad):
    out = shaped((4, 128 + BIAS_ROWS, 512), F32)
    return call(weights_kernel, [out, out], (keep, give, grad), [VMEM] * 3, flops=4 * 128 * 512 * 512)


def ring_sum(value, **axis):
    (name,) = axis
    sent = value.astype(BF)
    got = {k: shift(sent, **{name: k}).astype(F32) for k in others(name)}
    return (sent.astype(F32) + got[2]) + (got[1] + got[3])


def local(
    features, cotangent, w_self, w_neigh, out_bias, block_vals, block_rows, block_cols, block_count
):
    device = lax.axis_index("row") * 32 + lax.axis_index("col")
    my_zh, my_core, my_zl, my_x, my_y = coords(device)
    slots = block_vals.shape[0]
    live = jnp.arange(slots, dtype=jnp.int32) < block_count[0]
    rel_z = (block_rows // 16 - my_zl) % ZL
    rel_x = (block_rows // 4 % 4 - my_x) % X
    rel_y = (block_rows % 4 - my_y) % Y
    rows_a = rel_x * 8 + rel_y * 2 + rel_z
    rows_b = rel_y * 8 + rel_x * 2 + rel_z
    place_a = jnp.where(live, rows_a, 32)
    place_b = jnp.where(live, rows_b, 32)
    rel_h = (block_cols // 2 - my_zh) % ZH
    rel_c = (block_cols % 2 - my_core) % CORE
    source = rel_h * 2 + rel_c
    back_place = jnp.where(live, rel_c * 4 + rel_h, 8)

    ahead = {k: shift(features, zh=-k) for k in others("zh")}
    ahead[0] = features
    pieces = []
    for k in range(4):
        pieces += [ahead[k], shift(ahead[k], core=1)]

    weight = row_weights(block_count, place_a, block_vals)

    parts_a = forward(0, block_count, place_a, source, block_vals, pieces, weight)
    got_a = [shift(parts_a[k], x=k) for k in others("x")]
    parts_b = forward(1, block_count, place_b, source, block_vals, pieces)
    got_b = [shift(parts_b[k], y=k) for k in others("y")]

    later, _ = lax.optimization_barrier(((features, cotangent, block_vals), parts_b[3]))
    feat_late, cot_late, vals_late = later
    both_feat = jnp.concatenate([feat_late, shift(feat_late, zl=1)])
    both_cot = jnp.concatenate([cot_late, shift(cot_late, zl=1)])
    self_pre = jnp.dot(both_feat, w_self, preferred_element_type=F32) + out_bias
    turned = turn(vals_late)

    parts_a = merge(True, parts_a[0], *got_a)
    got_a = [shift(parts_a[k], y=k) for k in others("y")]
    parts_b = merge(False, parts_b[0], *got_b)
    got_b = [shift(parts_b[k], x=k) for k in others("x")]
    kept, weight, given = join([parts_a[0], *got_a], [parts_b[0], *got_b])
    layer_out, mean_agg, grad_pre, back_a, back_b = node(
        kept, weight, shift(given, zl=1), self_pre, both_cot, w_neigh
    )

    near_a, near_b = {0: back_a}, {0: back_b}
    for k in others("y"):
        near_a[k] = shift(back_a, y=-k)
        near_b[k] = shift(back_b, x=-k)

    begin = my_x * 128
    feat_turn = lax.dynamic_slice_in_dim(jnp.concatenate([features, features], 1), begin, 512, 1)
    mean_turn = lax.dynamic_slice_in_dim(jnp.concatenate([mean_agg, mean_agg], 1), begin, 512, 1)
    first = my_core == 0
    keep = jnp.where(first, feat_turn, mean_turn)
    give = jnp.where(first, mean_turn, feat_turn)
    keep_part, give_part = weights(keep, give, grad_pre)
    parts = pair(keep_part, shift(give_part, core=1))

    far_a = {0: jnp.concatenate([near_a[k] for k in range(4)])}
    far_b = {0: jnp.concatenate([near_b[k] for k in range(4)])}
    parts, far_a[0], far_b[0] = lax.optimization_barrier((parts, far_a[0], far_b[0]))
    got = [shift(parts[k], x=k) for k in others("x")]
    for k in others("x"):
        far_a[k] = shift(far_a[0], x=-k)
        far_b[k] = shift(far_b[0], y=-k)
    chunk = parts[0] + got[0].astype(F32) + got[1].astype(F32) + got[2].astype(F32)
    chunk = chunk + shift(chunk, zl=1)
    chunk = ring_sum(chunk, zh=1)
    chunk, far_a, far_b = lax.optimization_barrier((chunk, far_a, far_b))
    chunk = ring_sum(chunk, y=1)
    scale = 1.0 / math.sqrt(128 * DEVICES)
    bias_grad = chunk[128] * scale
    chunk_out = (chunk[:128] * scale).astype(BF)
    chunks = {0: chunk_out}
    for k in others("x"):
        chunks[k] = shift(chunk_out, x=-k)
    matrix = jnp.concatenate([chunks[k] for k in range(4)])
    matrix = jnp.concatenate([matrix, matrix])
    matrix = lax.dynamic_slice_in_dim(matrix, (4 - my_x) % 4 * 128, 512, 0)
    other = shift(matrix, core=1)
    self_grad = jnp.where(first, matrix, other).astype(F32)
    neigh_grad = jnp.where(first, other, matrix).astype(F32)

    grad_self = lax.dot_general(grad_pre, w_self, CONTRACT_COLS, preferred_element_type=F32)
    own, give = backward(
        block_count,
        rows_a,
        rows_b,
        back_place,
        turned,
        [far_a[k] for k in range(4)],
        [far_b[k] for k in range(4)],
    )
    parts = pair(own, shift(give, core=1))
    spread = parts[0]
    for k in others("zh"):
        spread = spread + shift(parts[k], zh=k).astype(F32)
    feature_grad = grad_self + spread
    return layer_out, feature_grad, self_grad, neigh_grad, bias_grad


def solution(mesh):
    return jax.shard_map(
        local,
        mesh=mesh,
        in_specs=(
            P(("row", "col"), None),
            P(("row", "col"), None),
            P(),
            P(),
            P(),
            P(("row", "col"), None, None),
            P(("row", "col")),
            P(("row", "col")),
            P(("row", "col")),
        ),
        out_specs=(P(("row", "col"), None), P(("row", "col"), None), P(), P(), P()),
        check_vma=False,
    )
```

```python
import functools
import math

import jax
import jax.numpy as jnp
from jax import lax
from jax.experimental import pallas as pl
from jax.experimental.pallas import tpu as pltpu
from jax.sharding import PartitionSpec as P

BF = jnp.bfloat16
F32 = jnp.float32
AXES = ("row", "col")
ZH, CORE, ZL, X, Y = 4, 2, 2, 4, 4
DEVICES = ZH * CORE * ZL * X * Y
VMEM = pl.BlockSpec(memory_space=pltpu.VMEM)
SMEM = pl.BlockSpec(memory_space=pltpu.SMEM)
ANY = pl.BlockSpec(memory_space=pl.ANY)
CONTRACT_ROWS = (((0,), (0,)), ((), ()))
CONTRACT_COLS = (((1,), (1,)), ((), ()))
MIB = 1 << 20


def coords(device):
    y = device % Y
    x = device // Y % X
    zl = device // (Y * X) % ZL
    core = device // (Y * X * ZL) % CORE
    zh = device // (Y * X * ZL * CORE)
    return zh, core, zl, x, y


def shift(value, zh=0, core=0, zl=0, x=0, y=0):
    pairs = []
    for device in range(DEVICES):
        a, b, c, d, e = coords(device)
        a, b, c, d, e = (a + zh) % ZH, (b + core) % CORE, (c + zl) % ZL, (d + x) % X, (e + y) % Y
        pairs.append((device, (((a * CORE + b) * ZL + c) * X + d) * Y + e))
    return lax.ppermute(value, AXES, pairs)


def meet(value, **axis):
    ((name, bit),) = axis.items()
    at = ("zh", "core", "zl", "x", "y").index(name)
    pairs = []
    for device in range(DEVICES):
        place = list(coords(device))
        place[at] ^= bit
        a, b, c, d, e = place
        pairs.append((device, (((a * CORE + b) * ZL + c) * X + d) * Y + e))
    return lax.ppermute(value, AXES, pairs)


def others(axis):
    return (1, 3, 2)


def call(kernel, outs, args, specs, scratch=(), flops=0, own=0):
    size = sum(math.prod(o.shape) * o.dtype.itemsize for o in outs)
    size += sum(math.prod(a.shape) * a.dtype.itemsize for a in args)
    return pl.pallas_call(
        kernel,
        out_shape=tuple(outs),
        in_specs=list(specs),
        out_specs=(VMEM,) * len(outs),
        scratch_shapes=list(scratch),
        compiler_params=pltpu.CompilerParams(vmem_limit_bytes=size + own + 3 * MIB),
        cost_estimate=pl.CostEstimate(flops=flops, bytes_accessed=size, transcendentals=0),
    )(*args)


def shaped(shape, dtype):
    return jax.ShapeDtypeStruct(shape, dtype)


def row_weights_kernel(count, place, vals, weights):
    weights[...] = jnp.zeros_like(weights)
    ones = jnp.ones((8, 128), BF)

    def step(i, carry):
        slots = [i * GROUP + u for u in range(GROUP)]
        sums = [
            lax.dot_general(ones, vals[s], CONTRACT_COLS, preferred_element_type=F32) for s in slots
        ]
        for s, term in zip(slots, sums):
            weights[place[s]] += term
        return carry

    lax.fori_loop(0, (count[0] + GROUP - 1) // GROUP, step, 0)


def row_weights(count, place, vals):
    return call(
        row_weights_kernel,
        [shaped((33, 8, 128), F32)],
        (count, place, vals),
        [SMEM, SMEM, VMEM],
    )[0]


def turn_kernel(vals, turned):
    def step(i, carry):
        for u in range(GROUP):
            turned[i * GROUP + u] = vals[i * GROUP + u].T
        return carry

    lax.fori_loop(0, vals.shape[0] // GROUP, step, 0)


def turn(vals):
    return call(turn_kernel, [shaped(vals.shape, BF)], (vals,), [VMEM], flops=6 * 10**9)[0]


GROUP = 4
PAD = 16


def put_weights(out, rows, value):
    count = value.shape[0]
    if out.dtype == F32:
        out[rows : rows + count, :128] = value
        return
    out[rows:, :] = jnp.zeros((PAD, out.shape[1]), out.dtype)
    lead = value.astype(BF)
    trail = (value - lead.astype(F32)).astype(BF)
    both = jnp.concatenate([lead.astype(F32), trail.astype(F32)], axis=1)
    both = jnp.concatenate([both, jnp.zeros((PAD - count, 256), F32)], axis=0)
    out[rows:, :256] = both.astype(BF)


def get_weights(ref, rows, count):
    got = ref[rows : rows + PAD, :256].astype(F32)[:count]
    if ref.dtype == F32:
        return got[:, :128]
    return got[:, :128] + got[:, 128:]


def forward_kernel(half, count, place, source, vals, *refs):
    weights = None
    if half == 0:
        weights, refs = refs[0], refs[1:]
    pieces, outs, (panel, total, sems) = refs[:8], refs[8:13], refs[13:]
    copies = [
        pltpu.make_async_copy(piece.at[:, pl.ds(256 * half, 256)], panel.at[k], sems.at[k])
        for k, piece in enumerate(pieces)
    ]
    for copy in copies:
        copy.start()

    def clear(k, carry):
        total[k] = jnp.zeros((128, 256), F32)
        return carry

    lax.fori_loop(0, 33, clear, 0)
    for copy in copies:
        copy.wait()

    def step(i, carry):
        slots = [i * GROUP + u for u in range(GROUP)]
        terms = [
            jnp.dot(vals[s], panel[source[s]], preferred_element_type=F32) for s in slots
        ]
        for s, term in zip(slots, terms):
            total[place[s]] += term
        return carry

    lax.fori_loop(0, (count[0] + GROUP - 1) // GROUP, step, 0)

    own, ahead, low, high, behind = outs

    def finish(k, carry):
        rows = pl.ds(pl.multiple_of(k * 128, 128), 128)
        own[rows, :] = total[k]
        ahead[rows, :] = total[8 + k]
        behind[rows, :] = total[24 + k]
        return carry

    def finish_half(k, carry):
        rows = pl.ds(pl.multiple_of(k * 128, 128), 128)
        low[rows, :] = total[16 + k].astype(BF)
        high[rows, :] = total[20 + k].astype(BF)
        return carry

    lax.fori_loop(0, 8, finish, 0)
    lax.fori_loop(0, 4, finish_half, 0)
    if weights is not None:
        rows = [weights[k, 0:1, :] for k in range(32)]
        put_weights(own, 1024, jnp.concatenate(rows[0:8], axis=0))
        put_weights(ahead, 1024, jnp.concatenate(rows[8:16], axis=0))
        put_weights(low, 512, jnp.concatenate(rows[16:20], axis=0))
        put_weights(high, 512, jnp.concatenate(rows[20:24], axis=0))
        put_weights(behind, 1024, jnp.concatenate(rows[24:32], axis=0))


def forward(half, count, place, source, vals, pieces, weights=None):
    pad = PAD if half == 0 else 0
    extra = [weights] if half == 0 else []
    full = shaped((1024 + pad, 256), F32)
    cut = shaped((512 + pad, 256), BF)
    return call(
        functools.partial(forward_kernel, half),
        [full, full, cut, cut, full],
        (count, place, source, vals, *extra, *pieces),
        [SMEM, SMEM, SMEM, VMEM] + [VMEM] * len(extra) + [ANY] * 8,
        [
            pltpu.VMEM((8, 128, 256), BF),
            pltpu.VMEM((33, 128, 256), F32),
            pltpu.SemaphoreType.DMA((8,)),
        ],
        flops=2 * 48 * 128 * 128 * 256,
        own=5 * MIB,
    )


def pass_kernel(carries, ahead, low, behind, high, ahead_out, behind_out):
    ahead_out[:512] = (ahead[:512] + low[:512].astype(F32)).astype(BF)
    ahead_out[512:1024] = ahead[512:1024].astype(BF)
    behind_out[:512] = behind[:512].astype(BF)
    behind_out[512:1024] = (behind[512:1024] + high[:512].astype(F32)).astype(BF)
    if carries:
        none = jnp.zeros((4, 128), F32)
        low_weight = jnp.concatenate([get_weights(low, 512, 4), none], axis=0)
        high_weight = jnp.concatenate([none, get_weights(high, 512, 4)], axis=0)
        put_weights(ahead_out, 1024, get_weights(ahead, 1024, 8) + low_weight)
        put_weights(behind_out, 1024, get_weights(behind, 1024, 8) + high_weight)


def pass_on(carries, ahead, low, behind, high):
    out = shaped(ahead.shape, BF)
    return call(
        functools.partial(pass_kernel, carries),
        [out, out],
        (ahead, low, behind, high),
        [VMEM] * 4,
    )


def ring_scatter(carries, parts, axis):
    own, ahead, low, high, behind = parts
    came_low, came_high = shift(low, **{axis: 1}), shift(high, **{axis: -1})
    return own, ahead, came_low, behind, came_high


def merge_kernel(carries, own, a, b, *outs):
    for part, out in enumerate(outs):
        rows = pl.ds(256 * part, 256)
        total = own[rows] + a[rows].astype(F32) + b[rows].astype(F32)
        out[:256] = total.astype(out.dtype)
    if carries:
        weight = sum(get_weights(ref, 1024, 8) for ref in (own, a, b))
        for part, out in enumerate(outs):
            put_weights(out, 256, weight[2 * part : 2 * part + 2])


def merge(carries, own, a, b):
    rows = 256 + (PAD if carries else 0)
    return call(
        functools.partial(merge_kernel, carries),
        [shaped((rows, 256), F32)] + [shaped((rows, 256), BF)] * 3,
        (own, a, b),
        [VMEM] * 3,
    )


def join_kernel(*refs):
    parts_a, parts_b, (keep, weight_out, give) = refs[:4], refs[4:8], refs[8:]
    for at, parts in ((0, parts_a), (256, parts_b)):
        total = parts[0][:256]
        for part in parts[1:]:
            total += part[:256].astype(F32)
        keep[:, at : at + 256] = total
        give[:256, at : at + 256] = total.astype(BF)
    weight = sum(get_weights(ref, 256, 2) for ref in parts_a)
    weight_out[0:2, :] = weight
    put_weights(give, 256, weight)


def join(parts_a, parts_b):
    return call(
        join_kernel,
        [shaped((256, 512), F32), shaped((8, 128), F32), shaped((256 + PAD, 512), BF)],
        (*parts_a, *parts_b),
        [VMEM] * 8,
    )


def node_kernel(
    keep, weight, got, self_pre, cot, w_neigh, layer_out, mean_out, grad_out, back_a, back_b
):
    came = get_weights(got, 256, 2)
    for k in range(2):
        rows, back = slice(128 * k, 128 * k + 128), slice(128 - 128 * k, 256 - 128 * k)
        degree = 1.0 + weight[k : k + 1, :] + came[1 - k : 2 - k, :]
        inverse = 1.0 / jnp.broadcast_to(degree, (128, 128)).T
        inverse = jnp.concatenate([inverse] * 4, axis=1)
        mean = ((keep[rows] + got[back].astype(F32)) * inverse).astype(BF)
        pre_act = self_pre[rows] + jnp.dot(mean, w_neigh[...], preferred_element_type=F32)
        sigmoid_val = jax.nn.sigmoid(pre_act)
        grad = cot[rows].astype(F32) * sigmoid_val * (1.0 + pre_act * (1.0 - sigmoid_val))
        grad = grad.astype(BF)
        back_mean = lax.dot_general(
            grad, w_neigh[...], CONTRACT_COLS, preferred_element_type=F32
        )
        scaled = (back_mean * inverse).astype(BF)
        back_a[rows, :] = scaled[:, :256]
        back_b[rows, :] = scaled[:, 256:]
        if k == 0:
            layer_out[...] = (pre_act * sigmoid_val).astype(BF)
            mean_out[...] = mean
            grad_out[...] = grad


def node(keep, weight, got, self_pre, cot, w_neigh):
    wide = shaped((128, 512), BF)
    half = shaped((256, 256), BF)
    return call(
        node_kernel,
        [wide, wide, wide, half, half],
        (keep, weight, got, self_pre, cot, w_neigh),
        [VMEM] * 6,
        flops=8 * 128 * 512 * 512,
    )


def backward_kernel(count, from_a, from_b, place, vals, *refs):
    parts_a, parts_b, outs = refs[:5], refs[5:10], refs[10:12]
    panel_a, panel_b, total, sems = refs[12:]
    copies = []
    begin = 0
    for k, (part_a, part_b) in enumerate(zip(parts_a, parts_b)):
        rows = pl.ds(begin, part_a.shape[0])
        begin += part_a.shape[0]
        copies.append(pltpu.make_async_copy(part_a, panel_a.at[rows], sems.at[k]))
        copies.append(pltpu.make_async_copy(part_b, panel_b.at[rows], sems.at[5 + k]))
    for copy in copies:
        copy.start()

    def clear(k, carry):
        total[k] = jnp.zeros((128, 512), F32)
        return carry

    lax.fori_loop(0, 9, clear, 0)
    for copy in copies:
        copy.wait()

    def step(i, carry):
        for u in range(GROUP):
            s = i * GROUP + u
            block = vals[s]
            rows_a = pl.ds(pl.multiple_of(from_a[s] * 128, 128), 128)
            rows_b = pl.ds(pl.multiple_of(from_b[s] * 128, 128), 128)
            first = jnp.dot(block, panel_a[rows_a, :], preferred_element_type=F32)
            second = jnp.dot(block, panel_b[rows_b, :], preferred_element_type=F32)
            total[place[s], :, :256] += first
            total[place[s], :, 256:] += second
        return carry

    lax.fori_loop(0, (count[0] + GROUP - 1) // GROUP, step, 0)

    def finish(k, carry):
        for part, out in enumerate(outs):
            out[k] = total[part * 4 + k].astype(out.dtype)
        return carry

    lax.fori_loop(0, 4, finish, 0)


def backward(count, from_a, from_b, place, turned, parts_a, parts_b):
    return call(
        backward_kernel,
        [shaped((4, 128, 512), F32), shaped((4, 128, 512), BF)],
        (count, from_a, from_b, place, turned, *parts_a, *parts_b),
        [SMEM] * 4 + [VMEM] + [ANY] * 10,
        [
            pltpu.VMEM((4096, 256), BF),
            pltpu.VMEM((4096, 256), BF),
            pltpu.VMEM((9, 128, 512), F32),
            pltpu.SemaphoreType.DMA((10,)),
        ],
        flops=2 * 48 * 128 * 128 * 512,
        own=4 * MIB,
    )


def pair_kernel(own, got, *outs):
    for k, out in enumerate(outs):
        out[...] = (own[k] + got[k].astype(F32)).astype(out.dtype)


def pair(own, got):
    piece = own.shape[1:]
    return call(
        pair_kernel,
        [shaped(piece, F32)] + [shaped(piece, BF)] * 3,
        (own, got),
        [VMEM] * 2,
    )


BIAS_ROWS = 16
CHUNK = 128 + BIAS_ROWS


def weights_kernel(place, feat, mean, grad, keep_out, give_out):
    grads = grad[...]
    bias = jnp.sum(grads.astype(F32), axis=0, keepdims=True)
    bias = jnp.broadcast_to(bias, (BIAS_ROWS, 512))

    def emit(lhs, out):
        for m in range(4):
            begin = pl.multiple_of((place[0] ^ m) * 128, 128)
            out[m, :128, :] = lax.dot_general(
                lhs[:, pl.ds(begin, 128)], grads, CONTRACT_ROWS, preferred_element_type=F32
            )
            out[m, 128:, :] = bias

    @pl.when(place[1] == 0)
    def _():
        emit(feat, keep_out)
        emit(mean, give_out)

    @pl.when(place[1] != 0)
    def _():
        emit(mean, keep_out)
        emit(feat, give_out)


def weights(place, feat, mean, grad):
    out = shaped((4, CHUNK, 512), F32)
    return call(
        weights_kernel,
        [out, out],
        (place, feat, mean, grad),
        [SMEM] + [VMEM] * 3,
        flops=4 * 128 * 512 * 512,
    )


def halve_kernel(own, got, keep, give):
    half = keep.shape[0]
    for k in range(half):
        keep[k] = own[k] + got[k].astype(F32)
        give[k] = (own[half + k] + got[half + k].astype(F32)).astype(BF)


def halve(own, got):
    piece = (own.shape[0] // 2,) + own.shape[1:]
    return call(halve_kernel, [shaped(piece, F32), shaped(piece, BF)], (own, got), [VMEM] * 2)


def arrange_kernel(place, mine, other, self_out, neigh_out):
    def emit(first, second):
        for m in range(4):
            rows = pl.ds(pl.multiple_of((place[0] ^ m) * 128, 128), 128)
            self_out[rows, :] = first[128 * m : 128 * m + 128].astype(F32)
            neigh_out[rows, :] = second[128 * m : 128 * m + 128].astype(F32)

    @pl.when(place[1] == 0)
    def _():
        emit(mine, other)

    @pl.when(place[1] != 0)
    def _():
        emit(other, mine)


def arrange(place, mine, other):
    out = shaped((512, 512), F32)
    return call(arrange_kernel, [out, out], (place, mine, other), [SMEM, VMEM, VMEM])


def meet_sum(value, **axis):
    sent = value.astype(BF)
    return sent.astype(F32) + meet(sent, **axis).astype(F32)


def local(
    features, cotangent, w_self, w_neigh, out_bias, block_vals, block_rows, block_cols, block_count
):
    device = lax.axis_index("row") * 32 + lax.axis_index("col")
    my_zh, my_core, my_zl, my_x, my_y = coords(device)
    slots = block_vals.shape[0]
    live = jnp.arange(slots, dtype=jnp.int32) < block_count[0]
    rel_z = (block_rows // 16 - my_zl) % ZL
    rel_x = (block_rows // 4 % 4 - my_x) % X
    rel_y = (block_rows % 4 - my_y) % Y
    rows_a = rel_x * 8 + rel_y * 2 + rel_z
    rows_b = rel_y * 8 + rel_x * 2 + rel_z
    place_a = jnp.where(live, rows_a, 32)
    place_b = jnp.where(live, rows_b, 32)
    rel_h = (block_cols // 2 - my_zh) % ZH
    rel_c = (block_cols % 2 - my_core) % CORE
    source = rel_h * 2 + rel_c
    back_place = jnp.where(live, rel_c * 4 + rel_h, 8)

    ahead = {k: shift(features, zh=-k) for k in others("zh")}
    ahead[0] = features
    pieces = []
    for k in range(4):
        pieces += [ahead[k], shift(ahead[k], core=1)]

    weight = row_weights(block_count, place_a, block_vals)

    parts_a = forward(0, block_count, place_a, source, block_vals, pieces, weight)
    parts_a = ring_scatter(True, parts_a, "x")
    parts_b = forward(1, block_count, place_b, source, block_vals, pieces)
    parts_b = ring_scatter(False, parts_b, "y")
    ahead_a, behind_a = pass_on(True, *parts_a[1:])
    ahead_b, behind_b = pass_on(False, *parts_b[1:])
    got_a = [shift(ahead_a, x=1), shift(behind_a, x=-1)]
    got_b = [shift(ahead_b, y=1), shift(behind_b, y=-1)]

    later, _ = lax.optimization_barrier(((features, cotangent, block_vals), ahead_a))
    feat_late, cot_late, vals_late = later
    late = shift(jnp.concatenate([feat_late, cot_late]), zl=1)
    both_feat = jnp.concatenate([feat_late, late[:128]])
    both_cot = jnp.concatenate([cot_late, late[128:]])
    self_pre = jnp.dot(both_feat, w_self, preferred_element_type=F32) + out_bias
    turned = turn(vals_late)
    (got_a, got_b), self_pre, both_cot, turned = lax.optimization_barrier(
        ((got_a, got_b), self_pre, both_cot, turned)
    )

    parts_a = merge(True, parts_a[0], *got_a)
    got_a = [shift(parts_a[k], y=k) for k in others("y")]
    parts_b = merge(False, parts_b[0], *got_b)
    got_b = [shift(parts_b[k], x=k) for k in others("x")]
    kept, weight, given = join([parts_a[0], *got_a], [parts_b[0], *got_b])
    layer_out, mean_agg, grad_pre, back_a, back_b = node(
        kept, weight, shift(given, zl=1), self_pre, both_cot, w_neigh
    )

    near_a, near_b = {0: back_a}, {0: back_b}
    for k in others("y"):
        near_a[k] = shift(back_a, y=-k)
        near_b[k] = shift(back_b, x=-k)
    own_a = jnp.concatenate([near_a[k] for k in range(4)])
    own_b = jnp.concatenate([near_b[k] for k in range(4)])
    next_a, last_a = shift(own_a, x=-1), shift(own_a, x=1)
    next_b, last_b = shift(own_b, y=-1), shift(own_b, y=1)
    low_a, high_a = shift(last_a[:512], x=1), shift(next_a[512:], x=-1)
    low_b, high_b = shift(last_b[:512], y=1), shift(next_b[512:], y=-1)

    place = jnp.stack([my_x, my_core]).astype(jnp.int32)
    keep_part, give_part = weights(place, features, mean_agg, grad_pre)
    keep_part, give_part = halve(keep_part, shift(give_part, core=1))
    keep_part, give_part = halve(keep_part, meet(give_part, x=2))
    chunk = keep_part[0] + meet(give_part[0], x=1).astype(F32)
    chunk = chunk + shift(chunk, zl=1)
    chunk = meet_sum(chunk, zh=1)
    chunk = meet_sum(chunk, zh=2)

    grad_self = lax.dot_general(grad_pre, w_self, CONTRACT_COLS, preferred_element_type=F32)
    own, give = backward(
        block_count,
        rows_a,
        rows_b,
        back_place,
        turned,
        [own_a, next_a, low_a, high_a, last_a],
        [own_b, next_b, low_b, high_b, last_b],
    )
    (own, give), chunk = lax.optimization_barrier(((own, give), chunk))
    parts = pair(own, shift(give, core=1))
    spread = parts[0]
    for k in others("zh"):
        spread = spread + shift(parts[k], zh=k).astype(F32)
    feature_grad = grad_self + spread

    chunk = chunk + meet(chunk, y=1)
    chunk = chunk + meet(chunk, y=2)
    scale = 1.0 / math.sqrt(128 * DEVICES)
    bias_grad = chunk[128] * scale
    block = (chunk[:128] * scale).astype(BF)
    block = jnp.concatenate([block, meet(block, x=1)])
    block = jnp.concatenate([block, meet(block, x=2)])
    self_grad, neigh_grad = arrange(place, block, shift(block, core=1))
    return layer_out, feature_grad, self_grad, neigh_grad, bias_grad


def solution(mesh):
    return jax.shard_map(
        local,
        mesh=mesh,
        in_specs=(
            P(("row", "col"), None),
            P(("row", "col"), None),
            P(),
            P(),
            P(),
            P(("row", "col"), None, None),
            P(("row", "col")),
            P(("row", "col")),
            P(("row", "col")),
        ),
        out_specs=(P(("row", "col"), None), P(("row", "col"), None), P(), P(), P()),
        check_vma=False,
    )
```

```python
import functools
import math

import jax
import jax.numpy as jnp
from jax import lax
from jax.experimental import pallas as pl
from jax.experimental.pallas import tpu as pltpu
from jax.sharding import PartitionSpec as P

BF = jnp.bfloat16
F32 = jnp.float32
AXES = ("row", "col")
ZH, CORE, ZL, X, Y = 4, 2, 2, 4, 4
DEVICES = ZH * CORE * ZL * X * Y
VMEM = pl.BlockSpec(memory_space=pltpu.VMEM)
SMEM = pl.BlockSpec(memory_space=pltpu.SMEM)
ANY = pl.BlockSpec(memory_space=pl.ANY)
CONTRACT_ROWS = (((0,), (0,)), ((), ()))
CONTRACT_COLS = (((1,), (1,)), ((), ()))
MIB = 1 << 20


def coords(device):
    y = device % Y
    x = device // Y % X
    zl = device // (Y * X) % ZL
    core = device // (Y * X * ZL) % CORE
    zh = device // (Y * X * ZL * CORE)
    return zh, core, zl, x, y


def shift(value, zh=0, core=0, zl=0, x=0, y=0):
    pairs = []
    for device in range(DEVICES):
        a, b, c, d, e = coords(device)
        a, b, c, d, e = (a + zh) % ZH, (b + core) % CORE, (c + zl) % ZL, (d + x) % X, (e + y) % Y
        pairs.append((device, (((a * CORE + b) * ZL + c) * X + d) * Y + e))
    return lax.ppermute(value, AXES, pairs)


def meet(value, **axis):
    ((name, bit),) = axis.items()
    at = ("zh", "core", "zl", "x", "y").index(name)
    pairs = []
    for device in range(DEVICES):
        place = list(coords(device))
        place[at] ^= bit
        a, b, c, d, e = place
        pairs.append((device, (((a * CORE + b) * ZL + c) * X + d) * Y + e))
    return lax.ppermute(value, AXES, pairs)


def others(axis):
    return (1, 3, 2)


def call(kernel, outs, args, specs, scratch=(), flops=0, own=0):
    size = sum(math.prod(o.shape) * o.dtype.itemsize for o in outs)
    size += sum(math.prod(a.shape) * a.dtype.itemsize for a in args)
    return pl.pallas_call(
        kernel,
        out_shape=tuple(outs),
        in_specs=list(specs),
        out_specs=(VMEM,) * len(outs),
        scratch_shapes=list(scratch),
        compiler_params=pltpu.CompilerParams(vmem_limit_bytes=size + own + 3 * MIB),
        cost_estimate=pl.CostEstimate(flops=flops, bytes_accessed=size, transcendentals=0),
    )(*args)


def shaped(shape, dtype):
    return jax.ShapeDtypeStruct(shape, dtype)


def row_weights_kernel(count, place, vals, weights):
    weights[...] = jnp.zeros_like(weights)
    ones = jnp.ones((8, 128), BF)

    def step(i, carry):
        slots = [i * GROUP + u for u in range(GROUP)]
        sums = [
            lax.dot_general(ones, vals[s], CONTRACT_COLS, preferred_element_type=F32) for s in slots
        ]
        for s, term in zip(slots, sums):
            weights[place[s]] += term
        return carry

    lax.fori_loop(0, (count[0] + GROUP - 1) // GROUP, step, 0)


def row_weights(count, place, vals):
    return call(
        row_weights_kernel,
        [shaped((33, 8, 128), F32)],
        (count, place, vals),
        [SMEM, SMEM, VMEM],
    )[0]


def turn_kernel(vals, turned):
    def step(i, carry):
        for u in range(GROUP):
            turned[i * GROUP + u] = vals[i * GROUP + u].T
        return carry

    lax.fori_loop(0, vals.shape[0] // GROUP, step, 0)


def turn(vals):
    return call(turn_kernel, [shaped(vals.shape, BF)], (vals,), [VMEM], flops=6 * 10**9)[0]


GROUP = 4
BACKWARD_COST = 20 * 10**9
PAIR_COST = 5 * 10**9
TOTAL_COST = 5 * 10**9
PAD = 16


def put_weights(out, rows, value):
    count = value.shape[0]
    if out.dtype == F32:
        out[rows : rows + count, :128] = value
        return
    out[rows:, :] = jnp.zeros((PAD, out.shape[1]), out.dtype)
    lead = value.astype(BF)
    trail = (value - lead.astype(F32)).astype(BF)
    both = jnp.concatenate([lead.astype(F32), trail.astype(F32)], axis=1)
    both = jnp.concatenate([both, jnp.zeros((PAD - count, 256), F32)], axis=0)
    out[rows:, :256] = both.astype(BF)


def get_weights(ref, rows, count):
    got = ref[rows : rows + PAD, :256].astype(F32)[:count]
    if ref.dtype == F32:
        return got[:, :128]
    return got[:, :128] + got[:, 128:]


def forward_kernel(half, count, place, source, vals, *refs):
    weights = None
    if half == 0:
        weights, refs = refs[0], refs[1:]
    pieces, outs, (panel, total, sems) = refs[:8], refs[8:13], refs[13:]
    copies = [
        pltpu.make_async_copy(piece.at[:, pl.ds(256 * half, 256)], panel.at[k], sems.at[k])
        for k, piece in enumerate(pieces)
    ]
    for copy in copies:
        copy.start()

    def clear(k, carry):
        total[k] = jnp.zeros((128, 256), F32)
        return carry

    lax.fori_loop(0, 33, clear, 0)
    for copy in copies:
        copy.wait()

    def step(i, carry):
        slots = [i * GROUP + u for u in range(GROUP)]
        terms = [
            jnp.dot(vals[s], panel[source[s]], preferred_element_type=F32) for s in slots
        ]
        for s, term in zip(slots, terms):
            total[place[s]] += term
        return carry

    lax.fori_loop(0, (count[0] + GROUP - 1) // GROUP, step, 0)

    own, ahead, low, high, behind = outs

    def finish(k, carry):
        rows = pl.ds(pl.multiple_of(k * 128, 128), 128)
        own[rows, :] = total[k]
        ahead[rows, :] = total[8 + k]
        behind[rows, :] = total[24 + k]
        return carry

    def finish_half(k, carry):
        rows = pl.ds(pl.multiple_of(k * 128, 128), 128)
        low[rows, :] = total[16 + k].astype(BF)
        high[rows, :] = total[20 + k].astype(BF)
        return carry

    lax.fori_loop(0, 8, finish, 0)
    lax.fori_loop(0, 4, finish_half, 0)
    if weights is not None:
        rows = [weights[k, 0:1, :] for k in range(32)]
        put_weights(own, 1024, jnp.concatenate(rows[0:8], axis=0))
        put_weights(ahead, 1024, jnp.concatenate(rows[8:16], axis=0))
        put_weights(low, 512, jnp.concatenate(rows[16:20], axis=0))
        put_weights(high, 512, jnp.concatenate(rows[20:24], axis=0))
        put_weights(behind, 1024, jnp.concatenate(rows[24:32], axis=0))


def forward(half, count, place, source, vals, pieces, weights=None):
    pad = PAD if half == 0 else 0
    extra = [weights] if half == 0 else []
    full = shaped((1024 + pad, 256), F32)
    cut = shaped((512 + pad, 256), BF)
    return call(
        functools.partial(forward_kernel, half),
        [full, full, cut, cut, full],
        (count, place, source, vals, *extra, *pieces),
        [SMEM, SMEM, SMEM, VMEM] + [VMEM] * len(extra) + [ANY] * 8,
        [
            pltpu.VMEM((8, 128, 256), BF),
            pltpu.VMEM((33, 128, 256), F32),
            pltpu.SemaphoreType.DMA((8,)),
        ],
        flops=2 * 48 * 128 * 128 * 256,
        own=5 * MIB,
    )


def pass_kernel(carries, ahead, low, behind, high, ahead_out, behind_out):
    ahead_out[:512] = (ahead[:512] + low[:512].astype(F32)).astype(BF)
    ahead_out[512:1024] = ahead[512:1024].astype(BF)
    behind_out[:512] = behind[:512].astype(BF)
    behind_out[512:1024] = (behind[512:1024] + high[:512].astype(F32)).astype(BF)
    if carries:
        none = jnp.zeros((4, 128), F32)
        low_weight = jnp.concatenate([get_weights(low, 512, 4), none], axis=0)
        high_weight = jnp.concatenate([none, get_weights(high, 512, 4)], axis=0)
        put_weights(ahead_out, 1024, get_weights(ahead, 1024, 8) + low_weight)
        put_weights(behind_out, 1024, get_weights(behind, 1024, 8) + high_weight)


def pass_on(carries, ahead, low, behind, high):
    out = shaped(ahead.shape, BF)
    return call(
        functools.partial(pass_kernel, carries),
        [out, out],
        (ahead, low, behind, high),
        [VMEM] * 4,
    )


def ring_scatter(carries, parts, axis):
    own, ahead, low, high, behind = parts
    came_low, came_high = shift(low, **{axis: 1}), shift(high, **{axis: -1})
    return own, ahead, came_low, behind, came_high


def merge_kernel(carries, own, a, b, *outs):
    for part, out in enumerate(outs):
        rows = pl.ds(256 * part, 256)
        total = own[rows] + a[rows].astype(F32) + b[rows].astype(F32)
        out[:256] = total.astype(out.dtype)
    if carries:
        weight = sum(get_weights(ref, 1024, 8) for ref in (own, a, b))
        for part, out in enumerate(outs):
            put_weights(out, 256, weight[2 * part : 2 * part + 2])


def merge(carries, own, a, b):
    rows = 256 + (PAD if carries else 0)
    return call(
        functools.partial(merge_kernel, carries),
        [shaped((rows, 256), F32)] + [shaped((rows, 256), BF)] * 3,
        (own, a, b),
        [VMEM] * 3,
    )


def join_kernel(*refs):
    parts_a, parts_b, give = refs[:4], refs[4:8], refs[8]
    for at, parts in ((0, parts_a), (256, parts_b)):
        total = parts[0][:256]
        for part in parts[1:]:
            total += part[:256].astype(F32)
        give[:256, at : at + 256] = total.astype(BF)
    put_weights(give, 256, sum(get_weights(ref, 256, 2) for ref in parts_a))


def join(parts_a, parts_b):
    return call(
        join_kernel,
        [shaped((256 + PAD, 512), BF)],
        (*parts_a, *parts_b),
        [VMEM] * 8,
    )[0]


def node_kernel(given, got, self_pre, cot, w_neigh, layer_out, mean_out, grad_out, back_a, back_b):
    weight, came = get_weights(given, 256, 2), get_weights(got, 256, 2)
    for k in range(2):
        rows, back = slice(128 * k, 128 * k + 128), slice(128 - 128 * k, 256 - 128 * k)
        degree = 1.0 + (weight[k : k + 1, :] + came[1 - k : 2 - k, :])
        inverse = 1.0 / jnp.broadcast_to(degree, (128, 128)).T
        inverse = jnp.concatenate([inverse] * 4, axis=1)
        mean = ((given[rows].astype(F32) + got[back].astype(F32)) * inverse).astype(BF)
        pre_act = self_pre[rows] + jnp.dot(mean, w_neigh[...], preferred_element_type=F32)
        sigmoid_val = jax.nn.sigmoid(pre_act)
        grad = cot[rows].astype(F32) * sigmoid_val * (1.0 + pre_act * (1.0 - sigmoid_val))
        grad = grad.astype(BF)
        back_mean = lax.dot_general(
            grad, w_neigh[...], CONTRACT_COLS, preferred_element_type=F32
        )
        scaled = (back_mean * inverse).astype(BF)
        back_a[rows, :] = scaled[:, :256]
        back_b[rows, :] = scaled[:, 256:]
        mean_out[rows, :] = mean
        grad_out[rows, :] = grad
        if k == 0:
            layer_out[...] = (pre_act * sigmoid_val).astype(BF)


def node(given, got, self_pre, cot, w_neigh):
    wide = shaped((256, 512), BF)
    half = shaped((256, 256), BF)
    return call(
        node_kernel,
        [shaped((128, 512), BF), wide, wide, half, half],
        (given, got, self_pre, cot, w_neigh),
        [VMEM] * 5,
        flops=8 * 128 * 512 * 512,
    )


def backward_kernel(count, from_a, from_b, place, vals, *refs):
    parts_a, parts_b, outs = refs[:5], refs[5:10], refs[10:12]
    panel_a, panel_b, total, sems = refs[12:]
    copies = []
    begin = 0
    for k, (part_a, part_b) in enumerate(zip(parts_a, parts_b)):
        rows = pl.ds(begin, part_a.shape[0])
        begin += part_a.shape[0]
        copies.append(pltpu.make_async_copy(part_a, panel_a.at[rows], sems.at[k]))
        copies.append(pltpu.make_async_copy(part_b, panel_b.at[rows], sems.at[5 + k]))
    for copy in copies:
        copy.start()

    def clear(k, carry):
        total[k] = jnp.zeros((128, 512), F32)
        return carry

    lax.fori_loop(0, 9, clear, 0)
    for copy in copies:
        copy.wait()

    def step(i, carry):
        for u in range(GROUP):
            s = i * GROUP + u
            block = vals[s]
            rows_a = pl.ds(pl.multiple_of(from_a[s] * 128, 128), 128)
            rows_b = pl.ds(pl.multiple_of(from_b[s] * 128, 128), 128)
            first = jnp.dot(block, panel_a[rows_a, :], preferred_element_type=F32)
            second = jnp.dot(block, panel_b[rows_b, :], preferred_element_type=F32)
            total[place[s], :, :256] += first
            total[place[s], :, 256:] += second
        return carry

    lax.fori_loop(0, (count[0] + GROUP - 1) // GROUP, step, 0)

    def finish(k, carry):
        for part, out in enumerate(outs):
            out[k] = total[part * 4 + k].astype(out.dtype)
        return carry

    lax.fori_loop(0, 4, finish, 0)


def backward(count, from_a, from_b, place, turned, parts_a, parts_b):
    return call(
        backward_kernel,
        [shaped((4, 128, 512), F32), shaped((4, 128, 512), BF)],
        (count, from_a, from_b, place, turned, *parts_a, *parts_b),
        [SMEM] * 4 + [VMEM] + [ANY] * 10,
        [
            pltpu.VMEM((4096, 256), BF),
            pltpu.VMEM((4096, 256), BF),
            pltpu.VMEM((9, 128, 512), F32),
            pltpu.SemaphoreType.DMA((10,)),
        ],
        flops=BACKWARD_COST,
        own=4 * MIB,
    )


def pair_kernel(own, got, *outs):
    for k, out in enumerate(outs):
        out[...] = (own[k] + got[k].astype(F32)).astype(out.dtype)


def pair(own, got):
    piece = own.shape[1:]
    return call(
        pair_kernel,
        [shaped(piece, F32)] + [shaped(piece, BF)] * 3,
        (own, got),
        [VMEM] * 2,
        flops=PAIR_COST,
    )


def total_kernel(product, own, a, b, c, out):
    total = own[...] + a[...].astype(F32) + b[...].astype(F32) + c[...].astype(F32)
    out[...] = product[...] + total


def total(product, own, got):
    return call(
        total_kernel,
        [shaped((128, 512), F32)],
        (product, own, *got),
        [VMEM] * 5,
        flops=TOTAL_COST,
    )[0]


BIAS_ROWS = 16
CHUNK = 128 + BIAS_ROWS


def weights_kernel(place, feat, mean, grad, keep_out, give_out):
    nodes = (slice(0, 128), slice(128, 256))
    bias = [jnp.sum(grad[n].astype(F32), axis=0, keepdims=True) for n in nodes]
    bias = jnp.broadcast_to(bias[0] + bias[1], (BIAS_ROWS, 512))

    def emit(lhs, out):
        for m in range(4):
            begin = pl.multiple_of((place[0] ^ m) * 128, 128)
            terms = [
                lax.dot_general(
                    lhs[n, pl.ds(begin, 128)], grad[n], CONTRACT_ROWS, preferred_element_type=F32
                )
                for n in nodes
            ]
            out[m, :128, :] = terms[0] + terms[1]
            out[m, 128:, :] = bias

    @pl.when(place[1] == 0)
    def _():
        emit(feat, keep_out)
        emit(mean, give_out)

    @pl.when(place[1] != 0)
    def _():
        emit(mean, keep_out)
        emit(feat, give_out)


def weights(place, feat, mean, grad):
    out = shaped((4, CHUNK, 512), F32)
    return call(
        weights_kernel,
        [out, out],
        (place, feat, mean, grad),
        [SMEM] + [VMEM] * 3,
        flops=4 * 128 * 512 * 512,
    )


def halve_kernel(own, got, keep, give):
    half = keep.shape[0]
    for k in range(half):
        keep[k] = own[k] + got[k].astype(F32)
        give[k] = (own[half + k] + got[half + k].astype(F32)).astype(BF)


def halve(own, got):
    piece = (own.shape[0] // 2,) + own.shape[1:]
    return call(halve_kernel, [shaped(piece, F32), shaped(piece, BF)], (own, got), [VMEM] * 2)


def arrange_kernel(place, mine, other, self_out, neigh_out):
    def emit(first, second):
        for m in range(4):
            rows = pl.ds(pl.multiple_of((place[0] ^ m) * 128, 128), 128)
            self_out[rows, :] = first[128 * m : 128 * m + 128].astype(F32)
            neigh_out[rows, :] = second[128 * m : 128 * m + 128].astype(F32)

    @pl.when(place[1] == 0)
    def _():
        emit(mine, other)

    @pl.when(place[1] != 0)
    def _():
        emit(other, mine)


def arrange(place, mine, other):
    out = shaped((512, 512), F32)
    return call(arrange_kernel, [out, out], (place, mine, other), [SMEM, VMEM, VMEM])


def meet_sum(value, **axis):
    sent = value.astype(BF)
    return sent.astype(F32) + meet(sent, **axis).astype(F32)


def local(
    features, cotangent, w_self, w_neigh, out_bias, block_vals, block_rows, block_cols, block_count
):
    device = lax.axis_index("row") * 32 + lax.axis_index("col")
    my_zh, my_core, my_zl, my_x, my_y = coords(device)
    slots = block_vals.shape[0]
    live = jnp.arange(slots, dtype=jnp.int32) < block_count[0]
    rel_z = (block_rows // 16 - my_zl) % ZL
    rel_x = (block_rows // 4 % 4 - my_x) % X
    rel_y = (block_rows % 4 - my_y) % Y
    rows_a = rel_x * 8 + rel_y * 2 + rel_z
    rows_b = rel_y * 8 + rel_x * 2 + rel_z
    place_a = jnp.where(live, rows_a, 32)
    place_b = jnp.where(live, rows_b, 32)
    rel_h = (block_cols // 2 - my_zh) % ZH
    rel_c = (block_cols % 2 - my_core) % CORE
    source = rel_h * 2 + rel_c
    back_place = jnp.where(live, rel_c * 4 + rel_h, 8)

    ahead = {k: shift(features, zh=-k) for k in others("zh")}
    ahead[0] = features
    pieces = []
    for k in range(4):
        pieces += [ahead[k], shift(ahead[k], core=1)]

    weight = row_weights(block_count, place_a, block_vals)

    parts_a = forward(0, block_count, place_a, source, block_vals, pieces, weight)
    parts_a = ring_scatter(True, parts_a, "x")
    parts_b = forward(1, block_count, place_b, source, block_vals, pieces)
    parts_b = ring_scatter(False, parts_b, "y")
    ahead_a, behind_a = pass_on(True, *parts_a[1:])
    ahead_b, behind_b = pass_on(False, *parts_b[1:])
    got_a = [shift(ahead_a, x=1), shift(behind_a, x=-1)]
    got_b = [shift(ahead_b, y=1), shift(behind_b, y=-1)]

    later, _ = lax.optimization_barrier(((features, cotangent, block_vals), ahead_a))
    feat_late, cot_late, vals_late = later
    late = shift(jnp.concatenate([feat_late, cot_late]), zl=1)
    both_feat = jnp.concatenate([feat_late, late[:128]])
    both_cot = jnp.concatenate([cot_late, late[128:]])
    self_pre = jnp.dot(both_feat, w_self, preferred_element_type=F32) + out_bias
    turned = turn(vals_late)
    (got_a, got_b), self_pre, both_cot, turned = lax.optimization_barrier(
        ((got_a, got_b), self_pre, both_cot, turned)
    )

    parts_a = merge(True, parts_a[0], *got_a)
    got_a = [shift(parts_a[k], y=k) for k in others("y")]
    parts_b = merge(False, parts_b[0], *got_b)
    got_b = [shift(parts_b[k], x=k) for k in others("x")]
    given = join([parts_a[0], *got_a], [parts_b[0], *got_b])
    layer_out, mean_agg, grad_pre, back_a, back_b = node(
        given, shift(given, zl=1), self_pre, both_cot, w_neigh
    )

    near_a, near_b = {0: back_a}, {0: back_b}
    for k in others("y"):
        near_a[k] = shift(back_a, y=-k)
        near_b[k] = shift(back_b, x=-k)
    own_a = jnp.concatenate([near_a[k] for k in range(4)])
    own_b = jnp.concatenate([near_b[k] for k in range(4)])
    next_a, last_a = shift(own_a, x=-1), shift(own_a, x=1)
    next_b, last_b = shift(own_b, y=-1), shift(own_b, y=1)
    low_a, high_a = shift(last_a[:512], x=1), shift(next_a[512:], x=-1)
    low_b, high_b = shift(last_b[:512], y=1), shift(next_b[512:], y=-1)

    place = jnp.stack([my_x, my_core]).astype(jnp.int32)
    keep_part, give_part = weights(place, both_feat, mean_agg, grad_pre)
    keep_part, give_part = halve(keep_part, shift(give_part, core=1))
    keep_part, give_part = halve(keep_part, meet(give_part, x=2))
    chunk = keep_part[0] + meet(give_part[0], x=1).astype(F32)
    chunk = meet_sum(chunk, zh=1)
    chunk = meet_sum(chunk, zh=2)

    grad_self = lax.dot_general(grad_pre[:128], w_self, CONTRACT_COLS, preferred_element_type=F32)
    own, give = backward(
        block_count,
        rows_a,
        rows_b,
        back_place,
        turned,
        [own_a, next_a, low_a, high_a, last_a],
        [own_b, next_b, low_b, high_b, last_b],
    )
    parts = pair(own, shift(give, core=1))
    feature_grad = total(grad_self, parts[0], [shift(parts[k], zh=k) for k in others("zh")])

    chunk = chunk + meet(chunk, y=1)
    chunk = chunk + meet(chunk, y=2)
    scale = 1.0 / math.sqrt(128 * DEVICES)
    bias_grad = chunk[128] * scale
    block = (chunk[:128] * scale).astype(BF)
    block = jnp.concatenate([block, meet(block, x=1)])
    block = jnp.concatenate([block, meet(block, x=2)])
    self_grad, neigh_grad = arrange(place, block, shift(block, core=1))
    return layer_out, feature_grad, self_grad, neigh_grad, bias_grad


def solution(mesh):
    return jax.shard_map(
        local,
        mesh=mesh,
        in_specs=(
            P(("row", "col"), None),
            P(("row", "col"), None),
            P(),
            P(),
            P(),
            P(("row", "col"), None, None),
            P(("row", "col")),
            P(("row", "col")),
            P(("row", "col")),
        ),
        out_specs=(P(("row", "col"), None), P(("row", "col"), None), P(), P(), P()),
        check_vma=False,
    )
```

```python
import functools
import math

import jax
import jax.numpy as jnp
from jax import lax
from jax.experimental import pallas as pl
from jax.experimental.pallas import tpu as pltpu
from jax.sharding import PartitionSpec as P

BF = jnp.bfloat16
F32 = jnp.float32
AXES = ("row", "col")
ZH, CORE, ZL, X, Y = 4, 2, 2, 4, 4
DEVICES = ZH * CORE * ZL * X * Y
VMEM = pl.BlockSpec(memory_space=pltpu.VMEM)
SMEM = pl.BlockSpec(memory_space=pltpu.SMEM)
ANY = pl.BlockSpec(memory_space=pl.ANY)
CONTRACT_ROWS = (((0,), (0,)), ((), ()))
CONTRACT_COLS = (((1,), (1,)), ((), ()))
MIB = 1 << 20


def coords(device):
    y = device % Y
    x = device // Y % X
    zl = device // (Y * X) % ZL
    core = device // (Y * X * ZL) % CORE
    zh = device // (Y * X * ZL * CORE)
    return zh, core, zl, x, y


def shift(value, zh=0, core=0, zl=0, x=0, y=0):
    pairs = []
    for device in range(DEVICES):
        a, b, c, d, e = coords(device)
        a, b, c, d, e = (a + zh) % ZH, (b + core) % CORE, (c + zl) % ZL, (d + x) % X, (e + y) % Y
        pairs.append((device, (((a * CORE + b) * ZL + c) * X + d) * Y + e))
    return lax.ppermute(value, AXES, pairs)


def meet(value, **axis):
    ((name, bit),) = axis.items()
    at = ("zh", "core", "zl", "x", "y").index(name)
    pairs = []
    for device in range(DEVICES):
        place = list(coords(device))
        place[at] ^= bit
        a, b, c, d, e = place
        pairs.append((device, (((a * CORE + b) * ZL + c) * X + d) * Y + e))
    return lax.ppermute(value, AXES, pairs)


def others(axis):
    return (1, 3, 2)


def call(kernel, outs, args, specs, scratch=(), flops=0, own=0):
    size = sum(math.prod(o.shape) * o.dtype.itemsize for o in outs)
    size += sum(math.prod(a.shape) * a.dtype.itemsize for a in args)
    return pl.pallas_call(
        kernel,
        out_shape=tuple(outs),
        in_specs=list(specs),
        out_specs=(VMEM,) * len(outs),
        scratch_shapes=list(scratch),
        compiler_params=pltpu.CompilerParams(vmem_limit_bytes=size + own + 3 * MIB),
        cost_estimate=pl.CostEstimate(flops=flops, bytes_accessed=size, transcendentals=0),
    )(*args)


def shaped(shape, dtype):
    return jax.ShapeDtypeStruct(shape, dtype)


def row_weights_kernel(count, place, vals, weights):
    weights[...] = jnp.zeros_like(weights)
    ones = jnp.ones((8, 128), BF)

    def step(i, carry):
        slots = [i * GROUP + u for u in range(GROUP)]
        sums = [
            lax.dot_general(ones, vals[s], CONTRACT_COLS, preferred_element_type=F32) for s in slots
        ]
        for s, term in zip(slots, sums):
            weights[place[s]] += term
        return carry

    lax.fori_loop(0, (count[0] + GROUP - 1) // GROUP, step, 0)


def row_weights(count, place, vals):
    return call(
        row_weights_kernel,
        [shaped((33, 8, 128), F32)],
        (count, place, vals),
        [SMEM, SMEM, VMEM],
    )[0]


def turn_kernel(vals, turned):
    def step(i, carry):
        for u in range(GROUP):
            turned[i * GROUP + u] = vals[i * GROUP + u].T
        return carry

    lax.fori_loop(0, vals.shape[0] // GROUP, step, 0)


def turn(vals):
    return call(turn_kernel, [shaped(vals.shape, BF)], (vals,), [VMEM], flops=6 * 10**9)[0]


GROUP = 4
BACKWARD_COST = 20 * 10**9
PAIR_COST = 5 * 10**9
TOTAL_COST = 5 * 10**9
PAD = 16


def put_weights(out, rows, value):
    count = value.shape[0]
    if out.dtype == F32:
        out[rows : rows + count, :128] = value
        return
    out[rows:, :] = jnp.zeros((PAD, out.shape[1]), out.dtype)
    lead = value.astype(BF)
    trail = (value - lead.astype(F32)).astype(BF)
    both = jnp.concatenate([lead.astype(F32), trail.astype(F32)], axis=1)
    both = jnp.concatenate([both, jnp.zeros((PAD - count, 256), F32)], axis=0)
    out[rows:, :256] = both.astype(BF)


def get_weights(ref, rows, count):
    got = ref[rows : rows + PAD, :256].astype(F32)[:count]
    if ref.dtype == F32:
        return got[:, :128]
    return got[:, :128] + got[:, 128:]


def forward_kernel(half, count, place, source, vals, *refs):
    weights = None
    if half == 0:
        weights, refs = refs[0], refs[1:]
    pieces, outs, (panel, total, sems) = refs[:8], refs[8:13], refs[13:]
    copies = [
        pltpu.make_async_copy(piece.at[:, pl.ds(256 * half, 256)], panel.at[k], sems.at[k])
        for k, piece in enumerate(pieces)
    ]
    for copy in copies:
        copy.start()

    def clear(k, carry):
        total[k] = jnp.zeros((128, 256), F32)
        return carry

    lax.fori_loop(0, 33, clear, 0)
    for copy in copies:
        copy.wait()

    def step(i, carry):
        slots = [i * GROUP + u for u in range(GROUP)]
        terms = [
            jnp.dot(vals[s], panel[source[s]], preferred_element_type=F32) for s in slots
        ]
        for s, term in zip(slots, terms):
            total[place[s]] += term
        return carry

    lax.fori_loop(0, (count[0] + GROUP - 1) // GROUP, step, 0)

    own, ahead, low, high, behind = outs

    def finish(k, carry):
        rows = pl.ds(pl.multiple_of(k * 128, 128), 128)
        own[rows, :] = total[k]
        ahead[rows, :] = total[8 + k]
        behind[rows, :] = total[24 + k]
        return carry

    def finish_half(k, carry):
        rows = pl.ds(pl.multiple_of(k * 128, 128), 128)
        low[rows, :] = total[16 + k].astype(BF)
        high[rows, :] = total[20 + k].astype(BF)
        return carry

    lax.fori_loop(0, 8, finish, 0)
    lax.fori_loop(0, 4, finish_half, 0)
    if weights is not None:
        rows = [weights[k, 0:1, :] for k in range(32)]
        put_weights(own, 1024, jnp.concatenate(rows[0:8], axis=0))
        put_weights(ahead, 1024, jnp.concatenate(rows[8:16], axis=0))
        put_weights(low, 512, jnp.concatenate(rows[16:20], axis=0))
        put_weights(high, 512, jnp.concatenate(rows[20:24], axis=0))
        put_weights(behind, 1024, jnp.concatenate(rows[24:32], axis=0))


def forward(half, count, place, source, vals, pieces, weights=None):
    pad = PAD if half == 0 else 0
    extra = [weights] if half == 0 else []
    full = shaped((1024 + pad, 256), F32)
    cut = shaped((512 + pad, 256), BF)
    return call(
        functools.partial(forward_kernel, half),
        [full, full, cut, cut, full],
        (count, place, source, vals, *extra, *pieces),
        [SMEM, SMEM, SMEM, VMEM] + [VMEM] * len(extra) + [ANY] * 8,
        [
            pltpu.VMEM((8, 128, 256), BF),
            pltpu.VMEM((33, 128, 256), F32),
            pltpu.SemaphoreType.DMA((8,)),
        ],
        flops=2 * 48 * 128 * 128 * 256,
        own=5 * MIB,
    )


def pass_kernel(carries, ahead, low, behind, high, ahead_out, behind_out):
    ahead_out[:512] = (ahead[:512] + low[:512].astype(F32)).astype(BF)
    ahead_out[512:1024] = ahead[512:1024].astype(BF)
    behind_out[:512] = behind[:512].astype(BF)
    behind_out[512:1024] = (behind[512:1024] + high[:512].astype(F32)).astype(BF)
    if carries:
        none = jnp.zeros((4, 128), F32)
        low_weight = jnp.concatenate([get_weights(low, 512, 4), none], axis=0)
        high_weight = jnp.concatenate([none, get_weights(high, 512, 4)], axis=0)
        put_weights(ahead_out, 1024, get_weights(ahead, 1024, 8) + low_weight)
        put_weights(behind_out, 1024, get_weights(behind, 1024, 8) + high_weight)


def pass_on(carries, ahead, low, behind, high):
    out = shaped(ahead.shape, BF)
    return call(
        functools.partial(pass_kernel, carries),
        [out, out],
        (ahead, low, behind, high),
        [VMEM] * 4,
    )


def ring_scatter(carries, parts, axis):
    own, ahead, low, high, behind = parts
    came_low, came_high = shift(low, **{axis: 1}), shift(high, **{axis: -1})
    return own, ahead, came_low, behind, came_high


def merge_kernel(carries, own, a, b, *outs):
    for part, out in enumerate(outs):
        rows = pl.ds(256 * part, 256)
        total = own[rows] + a[rows].astype(F32) + b[rows].astype(F32)
        out[:256] = total.astype(out.dtype)
    if carries:
        weight = sum(get_weights(ref, 1024, 8) for ref in (own, a, b))
        for part, out in enumerate(outs):
            put_weights(out, 256, weight[2 * part : 2 * part + 2])


def merge(carries, own, a, b):
    rows = 256 + (PAD if carries else 0)
    return call(
        functools.partial(merge_kernel, carries),
        [shaped((rows, 256), F32)] + [shaped((rows, 256), BF)] * 3,
        (own, a, b),
        [VMEM] * 3,
    )


def join_kernel(*refs):
    parts_a, parts_b, give = refs[:4], refs[4:8], refs[8]
    for at, parts in ((0, parts_a), (256, parts_b)):
        total = parts[0][:256]
        for part in parts[1:]:
            total += part[:256].astype(F32)
        give[:256, at : at + 256] = total.astype(BF)
    put_weights(give, 256, sum(get_weights(ref, 256, 2) for ref in parts_a))


def join(parts_a, parts_b):
    return call(
        join_kernel,
        [shaped((256 + PAD, 512), BF)],
        (*parts_a, *parts_b),
        [VMEM] * 8,
    )[0]


def node_kernel(
    place, given, got, feat, self_pre, cot, w_neigh, layer_out, mean_out, grad_out, back_a, back_b, send
):
    @pl.when(place[1] != 0)
    def _():
        send[:256, :] = feat[...]

    weight, came = get_weights(given, 256, 2), get_weights(got, 256, 2)
    for k in range(2):
        rows, back = slice(128 * k, 128 * k + 128), slice(128 - 128 * k, 256 - 128 * k)
        degree = 1.0 + (weight[k : k + 1, :] + came[1 - k : 2 - k, :])
        inverse = 1.0 / jnp.broadcast_to(degree, (128, 128)).T
        inverse = jnp.concatenate([inverse] * 4, axis=1)
        mean = ((given[rows].astype(F32) + got[back].astype(F32)) * inverse).astype(BF)
        pre_act = self_pre[rows] + jnp.dot(mean, w_neigh[...], preferred_element_type=F32)
        sigmoid_val = jax.nn.sigmoid(pre_act)
        grad = cot[rows].astype(F32) * sigmoid_val * (1.0 + pre_act * (1.0 - sigmoid_val))
        grad = grad.astype(BF)
        back_mean = lax.dot_general(
            grad, w_neigh[...], CONTRACT_COLS, preferred_element_type=F32
        )
        scaled = (back_mean * inverse).astype(BF)
        back_a[rows, :] = scaled[:, :256]
        back_b[rows, :] = scaled[:, 256:]
        mean_out[rows, :] = mean
        grad_out[rows, :] = grad
        send[256 + 128 * k : 384 + 128 * k, :] = grad

        @pl.when(place[1] == 0)
        def _():
            send[rows, :] = mean

        if k == 0:
            layer_out[...] = (pre_act * sigmoid_val).astype(BF)


def node(place, given, got, feat, self_pre, cot, w_neigh):
    wide = shaped((256, 512), BF)
    half = shaped((256, 256), BF)
    return call(
        node_kernel,
        [shaped((128, 512), BF), wide, wide, half, half, shaped((512, 512), BF)],
        (place, given, got, feat, self_pre, cot, w_neigh),
        [SMEM] + [VMEM] * 6,
        flops=8 * 128 * 512 * 512,
    )


def backward_kernel(count, from_a, from_b, place, vals, *refs):
    parts_a, parts_b, outs = refs[:5], refs[5:10], refs[10:12]
    panel_a, panel_b, total, sems = refs[12:]
    copies = []
    begin = 0
    for k, (part_a, part_b) in enumerate(zip(parts_a, parts_b)):
        rows = pl.ds(begin, part_a.shape[0])
        begin += part_a.shape[0]
        copies.append(pltpu.make_async_copy(part_a, panel_a.at[rows], sems.at[k]))
        copies.append(pltpu.make_async_copy(part_b, panel_b.at[rows], sems.at[5 + k]))
    for copy in copies:
        copy.start()

    def clear(k, carry):
        total[k] = jnp.zeros((128, 512), F32)
        return carry

    lax.fori_loop(0, 9, clear, 0)
    for copy in copies:
        copy.wait()

    def step(i, carry):
        for u in range(GROUP):
            s = i * GROUP + u
            block = vals[s]
            rows_a = pl.ds(pl.multiple_of(from_a[s] * 128, 128), 128)
            rows_b = pl.ds(pl.multiple_of(from_b[s] * 128, 128), 128)
            first = jnp.dot(block, panel_a[rows_a, :], preferred_element_type=F32)
            second = jnp.dot(block, panel_b[rows_b, :], preferred_element_type=F32)
            total[place[s], :, :256] += first
            total[place[s], :, 256:] += second
        return carry

    lax.fori_loop(0, (count[0] + GROUP - 1) // GROUP, step, 0)

    def finish(k, carry):
        for part, out in enumerate(outs):
            out[k] = total[part * 4 + k].astype(out.dtype)
        return carry

    lax.fori_loop(0, 4, finish, 0)


def backward(count, from_a, from_b, place, turned, parts_a, parts_b):
    return call(
        backward_kernel,
        [shaped((4, 128, 512), F32), shaped((4, 128, 512), BF)],
        (count, from_a, from_b, place, turned, *parts_a, *parts_b),
        [SMEM] * 4 + [VMEM] + [ANY] * 10,
        [
            pltpu.VMEM((4096, 256), BF),
            pltpu.VMEM((4096, 256), BF),
            pltpu.VMEM((9, 128, 512), F32),
            pltpu.SemaphoreType.DMA((10,)),
        ],
        flops=BACKWARD_COST,
        own=4 * MIB,
    )


def pair_kernel(own, got, *outs):
    for k, out in enumerate(outs):
        out[...] = (own[k] + got[k].astype(F32)).astype(out.dtype)


def pair(own, got):
    piece = own.shape[1:]
    return call(
        pair_kernel,
        [shaped(piece, F32)] + [shaped(piece, BF)] * 3,
        (own, got),
        [VMEM] * 2,
        flops=PAIR_COST,
    )


def total_kernel(product, own, a, b, c, out):
    total = own[...] + a[...].astype(F32) + b[...].astype(F32) + c[...].astype(F32)
    out[...] = product[...] + total


def total(product, own, got):
    return call(
        total_kernel,
        [shaped((128, 512), F32)],
        (product, own, *got),
        [VMEM] * 5,
        flops=TOTAL_COST,
    )[0]


BIAS_ROWS = 16
CHUNK = 128 + BIAS_ROWS


def weights_kernel(place, feat, mean, grad, got, keep_out, give_out):
    nodes = (slice(0, 128), slice(128, 256))
    came = tuple(slice(n.start + 256, n.stop + 256) for n in nodes)
    bias = [jnp.sum(grad[n].astype(F32), axis=0, keepdims=True) for n in nodes]
    bias += [jnp.sum(got[n].astype(F32), axis=0, keepdims=True) for n in came]
    bias = (bias[0] + bias[1]) + (bias[2] + bias[3])
    bias = jnp.broadcast_to(bias, (BIAS_ROWS, 512))

    def emit(lhs):
        for m in range(4):
            begin = pl.multiple_of((place[0] ^ m) * 128, 128)
            columns = pl.ds(begin, 128)
            mine = [
                lax.dot_general(
                    lhs[n, columns], grad[n], CONTRACT_ROWS, preferred_element_type=F32
                )
                for n in nodes
            ]
            theirs = [
                lax.dot_general(got[n, columns], got[g], CONTRACT_ROWS, preferred_element_type=F32)
                for n, g in zip(nodes, came)
            ]
            out = keep_out if m < 2 else give_out
            out[m % 2, :128, :] = ((mine[0] + mine[1]) + (theirs[0] + theirs[1])).astype(out.dtype)
            out[m % 2, 128:, :] = bias.astype(out.dtype)

    @pl.when(place[1] == 0)
    def _():
        emit(feat)

    @pl.when(place[1] != 0)
    def _():
        emit(mean)


def weights(place, feat, mean, grad, got):
    piece = (2, CHUNK, 512)
    return call(
        weights_kernel,
        [shaped(piece, F32), shaped(piece, BF)],
        (place, feat, mean, grad, got),
        [SMEM] + [VMEM] * 4,
        flops=4 * 128 * 512 * 512,
    )


def halve_kernel(own, got, keep, give):
    half = keep.shape[0]
    for k in range(half):
        keep[k] = own[k] + got[k].astype(F32)
        give[k] = (own[half + k] + got[half + k].astype(F32)).astype(BF)


def halve(own, got):
    piece = (own.shape[0] // 2,) + own.shape[1:]
    return call(halve_kernel, [shaped(piece, F32), shaped(piece, BF)], (own, got), [VMEM] * 2)


def arrange_kernel(place, mine, other, self_out, neigh_out):
    def emit(first, second):
        for m in range(4):
            rows = pl.ds(pl.multiple_of((place[0] ^ m) * 128, 128), 128)
            self_out[rows, :] = first[128 * m : 128 * m + 128].astype(F32)
            neigh_out[rows, :] = second[128 * m : 128 * m + 128].astype(F32)

    @pl.when(place[1] == 0)
    def _():
        emit(mine, other)

    @pl.when(place[1] != 0)
    def _():
        emit(other, mine)


def arrange(place, mine, other):
    out = shaped((512, 512), F32)
    return call(arrange_kernel, [out, out], (place, mine, other), [SMEM, VMEM, VMEM])


def meet_sum(value, **axis):
    sent = value.astype(BF)
    return sent.astype(F32) + meet(sent, **axis).astype(F32)


def local(
    features, cotangent, w_self, w_neigh, out_bias, block_vals, block_rows, block_cols, block_count
):
    device = lax.axis_index("row") * 32 + lax.axis_index("col")
    my_zh, my_core, my_zl, my_x, my_y = coords(device)
    slots = block_vals.shape[0]
    live = jnp.arange(slots, dtype=jnp.int32) < block_count[0]
    rel_z = (block_rows // 16 - my_zl) % ZL
    rel_x = (block_rows // 4 % 4 - my_x) % X
    rel_y = (block_rows % 4 - my_y) % Y
    rows_a = rel_x * 8 + rel_y * 2 + rel_z
    rows_b = rel_y * 8 + rel_x * 2 + rel_z
    place_a = jnp.where(live, rows_a, 32)
    place_b = jnp.where(live, rows_b, 32)
    rel_h = (block_cols // 2 - my_zh) % ZH
    rel_c = (block_cols % 2 - my_core) % CORE
    source = rel_h * 2 + rel_c
    back_place = jnp.where(live, rel_c * 4 + rel_h, 8)

    place = jnp.stack([my_x, my_core]).astype(jnp.int32)

    ahead = {k: shift(features, zh=-k) for k in others("zh")}
    ahead[0] = features
    weight = row_weights(block_count, place_a, block_vals)
    ahead[1], weight = lax.optimization_barrier((ahead[1], weight))
    pieces = []
    for k in range(4):
        pieces += [ahead[k], shift(ahead[k], core=1)]

    parts_a = forward(0, block_count, place_a, source, block_vals, pieces, weight)
    parts_a = ring_scatter(True, parts_a, "x")
    parts_b = forward(1, block_count, place_b, source, block_vals, pieces)
    parts_b = ring_scatter(False, parts_b, "y")
    ahead_a, behind_a = pass_on(True, *parts_a[1:])
    ahead_b, behind_b = pass_on(False, *parts_b[1:])
    got_a = [shift(ahead_a, x=1), shift(behind_a, x=-1)]
    got_b = [shift(ahead_b, y=1), shift(behind_b, y=-1)]

    later, _ = lax.optimization_barrier(((features, cotangent, block_vals), ahead_a))
    feat_late, cot_late, vals_late = later
    late = shift(jnp.concatenate([feat_late, cot_late]), zl=1)
    both_feat = jnp.concatenate([feat_late, late[:128]])
    both_cot = jnp.concatenate([cot_late, late[128:]])
    self_pre = jnp.dot(both_feat, w_self, preferred_element_type=F32) + out_bias
    turned = turn(vals_late)
    (got_a, got_b), self_pre, both_cot, turned = lax.optimization_barrier(
        ((got_a, got_b), self_pre, both_cot, turned)
    )

    parts_a = merge(True, parts_a[0], *got_a)
    got_a = [shift(parts_a[k], y=k) for k in others("y")]
    parts_b = merge(False, parts_b[0], *got_b)
    got_b = [shift(parts_b[k], x=k) for k in others("x")]
    given = join([parts_a[0], *got_a], [parts_b[0], *got_b])
    layer_out, mean_agg, grad_pre, back_a, back_b, send = node(
        place, given, shift(given, zl=1), both_feat, self_pre, both_cot, w_neigh
    )

    near_a, near_b = {0: back_a}, {0: back_b}
    for k in others("y"):
        near_a[k] = shift(back_a, y=-k)
        near_b[k] = shift(back_b, x=-k)
    own_a = jnp.concatenate([near_a[k] for k in range(4)])
    own_b = jnp.concatenate([near_b[k] for k in range(4)])
    next_a, last_a = shift(own_a, x=-1), shift(own_a, x=1)
    next_b, last_b = shift(own_b, y=-1), shift(own_b, y=1)
    low_a, high_a = shift(last_a[:512], x=1), shift(next_a[512:], x=-1)
    low_b, high_b = shift(last_b[:512], y=1), shift(next_b[512:], y=-1)

    got = shift(send, core=1)
    keep_part, give_part = weights(place, both_feat, mean_agg, grad_pre, got)
    keep_part, give_part = halve(keep_part, meet(give_part, x=2))
    chunk = keep_part[0] + meet(give_part[0], x=1).astype(F32)
    chunk = meet_sum(chunk, zh=1)
    chunk = meet_sum(chunk, zh=2)

    grad_self = lax.dot_general(grad_pre[:128], w_self, CONTRACT_COLS, preferred_element_type=F32)
    own, give = backward(
        block_count,
        rows_a,
        rows_b,
        back_place,
        turned,
        [own_a, next_a, low_a, high_a, last_a],
        [own_b, next_b, low_b, high_b, last_b],
    )
    parts = pair(own, shift(give, core=1))
    feature_grad = total(grad_self, parts[0], [shift(parts[k], zh=k) for k in others("zh")])

    chunk = chunk + meet(chunk, y=1)
    chunk = chunk + meet(chunk, y=2)
    scale = 1.0 / math.sqrt(128 * DEVICES)
    bias_grad = chunk[128] * scale
    block = (chunk[:128] * scale).astype(BF)
    block = jnp.concatenate([block, meet(block, x=1)])
    block = jnp.concatenate([block, meet(block, x=2)])
    self_grad, neigh_grad = arrange(place, block, shift(block, core=1))
    return layer_out, feature_grad, self_grad, neigh_grad, bias_grad


def solution(mesh):
    return jax.shard_map(
        local,
        mesh=mesh,
        in_specs=(
            P(("row", "col"), None),
            P(("row", "col"), None),
            P(),
            P(),
            P(),
            P(("row", "col"), None, None),
            P(("row", "col")),
            P(("row", "col")),
            P(("row", "col")),
        ),
        out_specs=(P(("row", "col"), None), P(("row", "col"), None), P(), P(), P()),
        check_vma=False,
    )
```

```python
import functools
import math

import jax
import jax.numpy as jnp
from jax import lax
from jax.experimental import pallas as pl
from jax.experimental.pallas import tpu as pltpu
from jax.sharding import PartitionSpec as P

BF = jnp.bfloat16
F32 = jnp.float32
AXES = ("row", "col")
ZH, CORE, ZL, X, Y = 4, 2, 2, 4, 4
DEVICES = ZH * CORE * ZL * X * Y
VMEM = pl.BlockSpec(memory_space=pltpu.VMEM)
SMEM = pl.BlockSpec(memory_space=pltpu.SMEM)
ANY = pl.BlockSpec(memory_space=pl.ANY)
CONTRACT_ROWS = (((0,), (0,)), ((), ()))
CONTRACT_COLS = (((1,), (1,)), ((), ()))
MIB = 1 << 20


def coords(device):
    y = device % Y
    x = device // Y % X
    zl = device // (Y * X) % ZL
    core = device // (Y * X * ZL) % CORE
    zh = device // (Y * X * ZL * CORE)
    return zh, core, zl, x, y


def shift(value, zh=0, core=0, zl=0, x=0, y=0):
    pairs = []
    for device in range(DEVICES):
        a, b, c, d, e = coords(device)
        a, b, c, d, e = (a + zh) % ZH, (b + core) % CORE, (c + zl) % ZL, (d + x) % X, (e + y) % Y
        pairs.append((device, (((a * CORE + b) * ZL + c) * X + d) * Y + e))
    return lax.ppermute(value, AXES, pairs)


def meet(value, **axis):
    ((name, bit),) = axis.items()
    at = ("zh", "core", "zl", "x", "y").index(name)
    pairs = []
    for device in range(DEVICES):
        place = list(coords(device))
        place[at] ^= bit
        a, b, c, d, e = place
        pairs.append((device, (((a * CORE + b) * ZL + c) * X + d) * Y + e))
    return lax.ppermute(value, AXES, pairs)


def others(axis):
    return (1, 3, 2)


def call(kernel, outs, args, specs, scratch=(), flops=0, own=0):
    size = sum(math.prod(o.shape) * o.dtype.itemsize for o in outs)
    size += sum(math.prod(a.shape) * a.dtype.itemsize for a in args)
    return pl.pallas_call(
        kernel,
        out_shape=tuple(outs),
        in_specs=list(specs),
        out_specs=(VMEM,) * len(outs),
        scratch_shapes=list(scratch),
        compiler_params=pltpu.CompilerParams(vmem_limit_bytes=size + own + 3 * MIB),
        cost_estimate=pl.CostEstimate(flops=flops, bytes_accessed=size, transcendentals=0),
    )(*args)


def shaped(shape, dtype):
    return jax.ShapeDtypeStruct(shape, dtype)


def row_weights_kernel(count, place, vals, weights):
    weights[...] = jnp.zeros_like(weights)
    ones = jnp.ones((8, 128), BF)

    def step(i, carry):
        slots = [i * GROUP + u for u in range(GROUP)]
        sums = [
            lax.dot_general(ones, vals[s], CONTRACT_COLS, preferred_element_type=F32) for s in slots
        ]
        for s, term in zip(slots, sums):
            weights[place[s]] += term
        return carry

    lax.fori_loop(0, (count[0] + GROUP - 1) // GROUP, step, 0)


def row_weights(count, place, vals):
    return call(
        row_weights_kernel,
        [shaped((33, 8, 128), F32)],
        (count, place, vals),
        [SMEM, SMEM, VMEM],
    )[0]


def turn_kernel(vals, turned):
    def step(i, carry):
        for u in range(GROUP):
            turned[i * GROUP + u] = vals[i * GROUP + u].T
        return carry

    lax.fori_loop(0, vals.shape[0] // GROUP, step, 0)


def turn(vals):
    return call(turn_kernel, [shaped(vals.shape, BF)], (vals,), [VMEM], flops=6 * 10**9)[0]


GROUP = 4
TURN = 16
BACKWARD_COST = 20 * 10**9
PAIR_COST = 5 * 10**9
TOTAL_COST = 5 * 10**9
PAD = 16


def put_weights(out, rows, value):
    count = value.shape[0]
    if out.dtype == F32:
        out[rows : rows + count, :128] = value
        return
    out[rows:, :] = jnp.zeros((PAD, out.shape[1]), out.dtype)
    lead = value.astype(BF)
    trail = (value - lead.astype(F32)).astype(BF)
    both = jnp.concatenate([lead.astype(F32), trail.astype(F32)], axis=1)
    both = jnp.concatenate([both, jnp.zeros((PAD - count, 256), F32)], axis=0)
    out[rows:, :256] = both.astype(BF)


def get_weights(ref, rows, count):
    got = ref[rows : rows + PAD, :256].astype(F32)[:count]
    if ref.dtype == F32:
        return got[:, :128]
    return got[:, :128] + got[:, 128:]


def forward_kernel(count, place_a, place_b, source, vals, weights, *refs):
    pieces, (total_a, low_a, high_a, total_b, low_b, high_b), (panel, sems) = (
        refs[:8],
        refs[8:14],
        refs[14:],
    )
    copies = [
        pltpu.make_async_copy(piece, panel.at[k], sems.at[k]) for k, piece in enumerate(pieces)
    ]
    for copy in copies:
        copy.start()

    def clear(k, carry):
        total_a[k] = jnp.zeros((128, 256), F32)
        total_b[k] = jnp.zeros((128, 256), F32)
        return carry

    lax.fori_loop(0, 33, clear, 0)
    for copy in copies:
        copy.wait()

    def step(i, carry):
        for u in range(TURN):
            s = i * TURN + u
            term = jnp.dot(vals[s], panel[source[s]], preferred_element_type=F32)
            total_a[place_a[s]] += term[:, :256]
            total_b[place_b[s]] += term[:, 256:]
        return carry

    lax.fori_loop(0, (count[0] + TURN - 1) // TURN, step, 0)

    def finish(k, carry):
        rows = pl.ds(pl.multiple_of(k * 128, 128), 128)
        low_a[rows, :] = total_a[16 + k].astype(BF)
        high_a[rows, :] = total_a[20 + k].astype(BF)
        low_b[rows, :] = total_b[16 + k].astype(BF)
        high_b[rows, :] = total_b[20 + k].astype(BF)
        return carry

    lax.fori_loop(0, 4, finish, 0)
    put_weights(low_a, 512, rows_of(weights, 16, 4))
    put_weights(high_a, 512, rows_of(weights, 20, 4))


def rows_of(weights, begin, count):
    return jnp.concatenate([weights[begin + k, 0:1, :] for k in range(count)], axis=0)


def forward(count, place_a, place_b, source, vals, weights, pieces):
    full = shaped((33, 128, 256), F32)
    cut = shaped((512 + PAD, 256), BF)
    plain = shaped((512, 256), BF)
    return call(
        forward_kernel,
        [full, cut, cut, full, plain, plain],
        (count, place_a, place_b, source, vals, weights, *pieces),
        [SMEM] * 4 + [VMEM] * 2 + [ANY] * 8,
        [pltpu.VMEM((8, 128, 512), BF), pltpu.SemaphoreType.DMA((8,))],
        flops=2 * 48 * 128 * 128 * 512,
        own=4 * MIB,
    )


def pass_kernel(carries, total, weights, low, high, ahead_out, behind_out):
    def first(k, carry):
        rows = pl.ds(pl.multiple_of(k * 128, 128), 128)
        later = pl.ds(pl.multiple_of(512 + k * 128, 128), 128)
        ahead_out[rows, :] = (total[8 + k] + low[rows, :].astype(F32)).astype(BF)
        ahead_out[later, :] = total[12 + k].astype(BF)
        behind_out[rows, :] = total[24 + k].astype(BF)
        behind_out[later, :] = (total[28 + k] + high[rows, :].astype(F32)).astype(BF)
        return carry

    lax.fori_loop(0, 4, first, 0)
    if carries:
        none = jnp.zeros((4, 128), F32)
        low_weight = jnp.concatenate([get_weights(low, 512, 4), none], axis=0)
        high_weight = jnp.concatenate([none, get_weights(high, 512, 4)], axis=0)
        put_weights(ahead_out, 1024, rows_of(weights, 8, 8) + low_weight)
        put_weights(behind_out, 1024, rows_of(weights, 24, 8) + high_weight)


def pass_on(carries, total, weights, low, high):
    out = shaped((1024 + (PAD if carries else 0), 256), BF)
    return call(
        functools.partial(pass_kernel, carries),
        [out, out],
        (total, weights, low, high),
        [VMEM] * 4,
    )


def merge_kernel(carries, own, weights, a, b, *outs):
    for part, out in enumerate(outs):
        for k in range(2):
            rows = slice(256 * part + 128 * k, 256 * part + 128 * k + 128)
            total = own[2 * part + k] + a[rows].astype(F32) + b[rows].astype(F32)
            out[128 * k : 128 * k + 128] = total.astype(out.dtype)
    if carries:
        weight = rows_of(weights, 0, 8) + get_weights(a, 1024, 8) + get_weights(b, 1024, 8)
        for part, out in enumerate(outs):
            put_weights(out, 256, weight[2 * part : 2 * part + 2])


def merge(carries, own, weights, a, b):
    rows = 256 + (PAD if carries else 0)
    return call(
        functools.partial(merge_kernel, carries),
        [shaped((rows, 256), F32)] + [shaped((rows, 256), BF)] * 3,
        (own, weights, a, b),
        [VMEM] * 4,
    )


def join_kernel(*refs):
    parts_a, parts_b, give = refs[:4], refs[4:8], refs[8]
    for at, parts in ((0, parts_a), (256, parts_b)):
        total = parts[0][:256]
        for part in parts[1:]:
            total += part[:256].astype(F32)
        give[:256, at : at + 256] = total.astype(BF)
    put_weights(give, 256, sum(get_weights(ref, 256, 2) for ref in parts_a))


def join(parts_a, parts_b):
    return call(
        join_kernel,
        [shaped((256 + PAD, 512), BF)],
        (*parts_a, *parts_b),
        [VMEM] * 8,
    )[0]


def node_kernel(
    place, given, got, feat, self_pre, cot, w_neigh, layer_out, mean_out, grad_out, back_a, back_b, send
):
    @pl.when(place[1] != 0)
    def _():
        send[:256, :] = feat[...]

    weight, came = get_weights(given, 256, 2), get_weights(got, 256, 2)
    for k in range(2):
        rows, back = slice(128 * k, 128 * k + 128), slice(128 - 128 * k, 256 - 128 * k)
        degree = 1.0 + (weight[k : k + 1, :] + came[1 - k : 2 - k, :])
        inverse = 1.0 / jnp.broadcast_to(degree, (128, 128)).T
        inverse = jnp.concatenate([inverse] * 4, axis=1)
        mean = ((given[rows].astype(F32) + got[back].astype(F32)) * inverse).astype(BF)
        pre_act = self_pre[rows] + jnp.dot(mean, w_neigh[...], preferred_element_type=F32)
        sigmoid_val = jax.nn.sigmoid(pre_act)
        grad = cot[rows].astype(F32) * sigmoid_val * (1.0 + pre_act * (1.0 - sigmoid_val))
        grad = grad.astype(BF)
        back_mean = lax.dot_general(
            grad, w_neigh[...], CONTRACT_COLS, preferred_element_type=F32
        )
        scaled = (back_mean * inverse).astype(BF)
        back_a[rows, :] = scaled[:, :256]
        back_b[rows, :] = scaled[:, 256:]
        mean_out[rows, :] = mean
        grad_out[rows, :] = grad
        send[256 + 128 * k : 384 + 128 * k, :] = grad

        @pl.when(place[1] == 0)
        def _():
            send[rows, :] = mean

        if k == 0:
            layer_out[...] = (pre_act * sigmoid_val).astype(BF)


def node(place, given, got, feat, self_pre, cot, w_neigh):
    wide = shaped((256, 512), BF)
    half = shaped((256, 256), BF)
    return call(
        node_kernel,
        [shaped((128, 512), BF), wide, wide, half, half, shaped((512, 512), BF)],
        (place, given, got, feat, self_pre, cot, w_neigh),
        [SMEM] + [VMEM] * 6,
        flops=8 * 128 * 512 * 512,
    )


def backward_kernel(count, from_a, from_b, place, vals, *refs):
    parts_a, parts_b, outs = refs[:5], refs[5:10], refs[10:12]
    panel_a, panel_b, total, sems = refs[12:]
    copies = []
    begin = 0
    for k, (part_a, part_b) in enumerate(zip(parts_a, parts_b)):
        rows = pl.ds(begin, part_a.shape[0])
        begin += part_a.shape[0]
        copies.append(pltpu.make_async_copy(part_a, panel_a.at[rows], sems.at[k]))
        copies.append(pltpu.make_async_copy(part_b, panel_b.at[rows], sems.at[5 + k]))
    for copy in copies:
        copy.start()

    def clear(k, carry):
        total[k] = jnp.zeros((128, 512), F32)
        return carry

    lax.fori_loop(0, 9, clear, 0)
    for copy in copies:
        copy.wait()

    def step(i, carry):
        for u in range(TURN):
            s = i * TURN + u
            block = vals[s]
            rows_a = pl.ds(pl.multiple_of(from_a[s] * 128, 128), 128)
            rows_b = pl.ds(pl.multiple_of(from_b[s] * 128, 128), 128)
            first = jnp.dot(block, panel_a[rows_a, :], preferred_element_type=F32)
            second = jnp.dot(block, panel_b[rows_b, :], preferred_element_type=F32)
            total[place[s], :, :256] += first
            total[place[s], :, 256:] += second
        return carry

    lax.fori_loop(0, (count[0] + TURN - 1) // TURN, step, 0)

    def finish(k, carry):
        for part, out in enumerate(outs):
            out[k] = total[part * 4 + k].astype(out.dtype)
        return carry

    lax.fori_loop(0, 4, finish, 0)


def backward(count, from_a, from_b, place, turned, parts_a, parts_b):
    return call(
        backward_kernel,
        [shaped((4, 128, 512), F32), shaped((4, 128, 512), BF)],
        (count, from_a, from_b, place, turned, *parts_a, *parts_b),
        [SMEM] * 4 + [VMEM] + [ANY] * 10,
        [
            pltpu.VMEM((4096, 256), BF),
            pltpu.VMEM((4096, 256), BF),
            pltpu.VMEM((9, 128, 512), F32),
            pltpu.SemaphoreType.DMA((10,)),
        ],
        flops=BACKWARD_COST,
        own=4 * MIB,
    )


def pair_kernel(own, got, *outs):
    for k, out in enumerate(outs):
        out[...] = (own[k] + got[k].astype(F32)).astype(out.dtype)


def pair(own, got):
    piece = own.shape[1:]
    return call(
        pair_kernel,
        [shaped(piece, F32)] + [shaped(piece, BF)] * 3,
        (own, got),
        [VMEM] * 2,
        flops=PAIR_COST,
    )


def total_kernel(product, own, a, b, c, out):
    total = own[...] + a[...].astype(F32) + b[...].astype(F32) + c[...].astype(F32)
    out[...] = product[...] + total


def total(product, own, got):
    return call(
        total_kernel,
        [shaped((128, 512), F32)],
        (product, own, *got),
        [VMEM] * 5,
        flops=TOTAL_COST,
    )[0]


BIAS_ROWS = 16
CHUNK = 128 + BIAS_ROWS


def weights_kernel(place, feat, mean, grad, got, keep_out, give_out):
    nodes = (slice(0, 128), slice(128, 256))
    came = tuple(slice(n.start + 256, n.stop + 256) for n in nodes)
    bias = [jnp.sum(grad[n].astype(F32), axis=0, keepdims=True) for n in nodes]
    bias += [jnp.sum(got[n].astype(F32), axis=0, keepdims=True) for n in came]
    bias = (bias[0] + bias[1]) + (bias[2] + bias[3])
    bias = jnp.broadcast_to(bias, (BIAS_ROWS, 512))

    def emit(lhs):
        for m in range(4):
            begin = pl.multiple_of((place[0] ^ m) * 128, 128)
            columns = pl.ds(begin, 128)
            mine = [
                lax.dot_general(
                    lhs[n, columns], grad[n], CONTRACT_ROWS, preferred_element_type=F32
                )
                for n in nodes
            ]
            theirs = [
                lax.dot_general(got[n, columns], got[g], CONTRACT_ROWS, preferred_element_type=F32)
                for n, g in zip(nodes, came)
            ]
            out = keep_out if m < 2 else give_out
            out[m % 2, :128, :] = ((mine[0] + mine[1]) + (theirs[0] + theirs[1])).astype(out.dtype)
            out[m % 2, 128:, :] = bias.astype(out.dtype)

    @pl.when(place[1] == 0)
    def _():
        emit(feat)

    @pl.when(place[1] != 0)
    def _():
        emit(mean)


def weights(place, feat, mean, grad, got):
    piece = (2, CHUNK, 512)
    return call(
        weights_kernel,
        [shaped(piece, F32), shaped(piece, BF)],
        (place, feat, mean, grad, got),
        [SMEM] + [VMEM] * 4,
        flops=4 * 128 * 512 * 512,
    )


def halve_kernel(own, got, keep, give):
    half = keep.shape[0]
    for k in range(half):
        keep[k] = own[k] + got[k].astype(F32)
        give[k] = (own[half + k] + got[half + k].astype(F32)).astype(BF)


def halve(own, got):
    piece = (own.shape[0] // 2,) + own.shape[1:]
    return call(halve_kernel, [shaped(piece, F32), shaped(piece, BF)], (own, got), [VMEM] * 2)


def arrange_kernel(place, mine, other, self_out, neigh_out):
    def emit(first, second):
        for m in range(4):
            rows = pl.ds(pl.multiple_of((place[0] ^ m) * 128, 128), 128)
            self_out[rows, :] = first[128 * m : 128 * m + 128].astype(F32)
            neigh_out[rows, :] = second[128 * m : 128 * m + 128].astype(F32)

    @pl.when(place[1] == 0)
    def _():
        emit(mine, other)

    @pl.when(place[1] != 0)
    def _():
        emit(other, mine)


def arrange(place, mine, other):
    out = shaped((512, 512), F32)
    return call(arrange_kernel, [out, out], (place, mine, other), [SMEM, VMEM, VMEM])


def ring_sum(value, **axis):
    (name,) = axis
    sent = value.astype(BF)
    got = {k: shift(sent, **{name: k}).astype(F32) for k in others(name)}
    return (sent.astype(F32) + got[2]) + (got[1] + got[3])


def meet_sum(value, **axis):
    sent = value.astype(BF)
    return sent.astype(F32) + meet(sent, **axis).astype(F32)


def local(
    features, cotangent, w_self, w_neigh, out_bias, block_vals, block_rows, block_cols, block_count
):
    device = lax.axis_index("row") * 32 + lax.axis_index("col")
    my_zh, my_core, my_zl, my_x, my_y = coords(device)
    slots = block_vals.shape[0]
    live = jnp.arange(slots, dtype=jnp.int32) < block_count[0]
    rel_z = (block_rows // 16 - my_zl) % ZL
    rel_x = (block_rows // 4 % 4 - my_x) % X
    rel_y = (block_rows % 4 - my_y) % Y
    rows_a = rel_x * 8 + rel_y * 2 + rel_z
    rows_b = rel_y * 8 + rel_x * 2 + rel_z
    place_a = jnp.where(live, rows_a, 32)
    place_b = jnp.where(live, rows_b, 32)
    rel_h = (block_cols // 2 - my_zh) % ZH
    rel_c = (block_cols % 2 - my_core) % CORE
    source = rel_h * 2 + rel_c
    back_place = jnp.where(live, rel_c * 4 + rel_h, 8)

    place = jnp.stack([my_x, my_core]).astype(jnp.int32)

    ahead = {k: shift(features, zh=-k) for k in others("zh")}
    ahead[0] = features
    weight = row_weights(block_count, place_a, block_vals)
    ahead[1], weight = lax.optimization_barrier((ahead[1], weight))
    pieces = []
    for k in range(4):
        pieces += [ahead[k], shift(ahead[k], core=1)]

    total_a, low_a, high_a, total_b, low_b, high_b = forward(
        block_count, place_a, place_b, source, block_vals, weight, pieces
    )
    low_a, high_a = shift(low_a, x=1), shift(high_a, x=-1)
    low_b, high_b = shift(low_b, y=1), shift(high_b, y=-1)
    ahead_a, behind_a = pass_on(True, total_a, weight, low_a, high_a)
    ahead_b, behind_b = pass_on(False, total_b, weight, low_b, high_b)
    got_a = [shift(ahead_a, x=1), shift(behind_a, x=-1)]
    got_b = [shift(ahead_b, y=1), shift(behind_b, y=-1)]

    later, _ = lax.optimization_barrier(((features, cotangent, block_vals), ahead_a))
    feat_late, cot_late, vals_late = later
    late = shift(jnp.concatenate([feat_late, cot_late]), zl=1)
    both_feat = jnp.concatenate([feat_late, late[:128]])
    both_cot = jnp.concatenate([cot_late, late[128:]])
    self_pre = jnp.dot(both_feat, w_self, preferred_element_type=F32) + out_bias
    turned = turn(vals_late)
    (got_a, got_b), self_pre, both_cot, turned = lax.optimization_barrier(
        ((got_a, got_b), self_pre, both_cot, turned)
    )

    parts_a = merge(True, total_a, weight, *got_a)
    got_a = [shift(parts_a[k], y=k) for k in others("y")]
    parts_b = merge(False, total_b, weight, *got_b)
    got_b = [shift(parts_b[k], x=k) for k in others("x")]
    given = join([parts_a[0], *got_a], [parts_b[0], *got_b])
    layer_out, mean_agg, grad_pre, back_a, back_b, send = node(
        place, given, shift(given, zl=1), both_feat, self_pre, both_cot, w_neigh
    )

    near_a, near_b = {0: back_a}, {0: back_b}
    for k in others("y"):
        near_a[k] = shift(back_a, y=-k)
        near_b[k] = shift(back_b, x=-k)
    own_a = jnp.concatenate([near_a[k] for k in range(4)])
    own_b = jnp.concatenate([near_b[k] for k in range(4)])

    got = shift(send, core=1)
    keep_part, give_part = weights(place, both_feat, mean_agg, grad_pre, got)
    came, own_b = lax.optimization_barrier((meet(give_part, x=2), own_b))
    keep_part, give_part = halve(keep_part, came)
    next_a, last_a = shift(own_a, x=-1), shift(own_a, x=1)
    next_b, last_b = shift(own_b, y=-1), shift(own_b, y=1)
    low_a, high_a = shift(last_a[:512], x=1), shift(next_a[512:], x=-1)
    low_b, high_b = shift(last_b[:512], y=1), shift(next_b[512:], y=-1)
    chunk = keep_part[0] + meet(give_part[0], x=1).astype(F32)
    chunk = meet_sum(chunk, zh=1)
    chunk = meet_sum(chunk, zh=2)

    grad_self = lax.dot_general(grad_pre[:128], w_self, CONTRACT_COLS, preferred_element_type=F32)
    own, give = backward(
        block_count,
        rows_a,
        rows_b,
        back_place,
        turned,
        [own_a, next_a, low_a, high_a, last_a],
        [own_b, next_b, low_b, high_b, last_b],
    )
    parts = pair(own, shift(give, core=1))
    chunk = ring_sum(chunk, y=1)
    scale = 1.0 / math.sqrt(128 * DEVICES)
    bias_grad = chunk[128] * scale
    block = (chunk[:128] * scale).astype(BF)
    block = jnp.concatenate([block, meet(block, x=1)])
    block, parts = lax.optimization_barrier((block, parts))
    block = jnp.concatenate([block, meet(block, x=2)])
    feature_grad = total(grad_self, parts[0], [shift(parts[k], zh=k) for k in others("zh")])
    self_grad, neigh_grad = arrange(place, block, shift(block, core=1))
    return layer_out, feature_grad, self_grad, neigh_grad, bias_grad


def solution(mesh):
    return jax.shard_map(
        local,
        mesh=mesh,
        in_specs=(
            P(("row", "col"), None),
            P(("row", "col"), None),
            P(),
            P(),
            P(),
            P(("row", "col"), None, None),
            P(("row", "col")),
            P(("row", "col")),
            P(("row", "col")),
        ),
        out_specs=(P(("row", "col"), None), P(("row", "col"), None), P(), P(), P()),
        check_vma=False,
    )
```

```python
import functools
import math

import jax
import jax.numpy as jnp
from jax import lax
from jax.experimental import pallas as pl
from jax.experimental.pallas import tpu as pltpu
from jax.sharding import PartitionSpec as P

BF = jnp.bfloat16
F32 = jnp.float32
AXES = ("row", "col")
ZH, CORE, ZL, X, Y = 4, 2, 2, 4, 4
DEVICES = ZH * CORE * ZL * X * Y
VMEM = pl.BlockSpec(memory_space=pltpu.VMEM)
SMEM = pl.BlockSpec(memory_space=pltpu.SMEM)
ANY = pl.BlockSpec(memory_space=pl.ANY)
CONTRACT_ROWS = (((0,), (0,)), ((), ()))
CONTRACT_COLS = (((1,), (1,)), ((), ()))
MIB = 1 << 20


def coords(device):
    y = device % Y
    x = device // Y % X
    zl = device // (Y * X) % ZL
    core = device // (Y * X * ZL) % CORE
    zh = device // (Y * X * ZL * CORE)
    return zh, core, zl, x, y


def shift(value, zh=0, core=0, zl=0, x=0, y=0):
    pairs = []
    for device in range(DEVICES):
        a, b, c, d, e = coords(device)
        a, b, c, d, e = (a + zh) % ZH, (b + core) % CORE, (c + zl) % ZL, (d + x) % X, (e + y) % Y
        pairs.append((device, (((a * CORE + b) * ZL + c) * X + d) * Y + e))
    return lax.ppermute(value, AXES, pairs)


def meet(value, **axis):
    ((name, bit),) = axis.items()
    at = ("zh", "core", "zl", "x", "y").index(name)
    pairs = []
    for device in range(DEVICES):
        place = list(coords(device))
        place[at] ^= bit
        a, b, c, d, e = place
        pairs.append((device, (((a * CORE + b) * ZL + c) * X + d) * Y + e))
    return lax.ppermute(value, AXES, pairs)


def others(axis):
    return (1, 3, 2)


def call(kernel, outs, args, specs, scratch=(), flops=0, own=0):
    size = sum(math.prod(o.shape) * o.dtype.itemsize for o in outs)
    size += sum(math.prod(a.shape) * a.dtype.itemsize for a in args)
    return pl.pallas_call(
        kernel,
        out_shape=tuple(outs),
        in_specs=list(specs),
        out_specs=(VMEM,) * len(outs),
        scratch_shapes=list(scratch),
        compiler_params=pltpu.CompilerParams(vmem_limit_bytes=size + own + 3 * MIB),
        cost_estimate=pl.CostEstimate(flops=flops, bytes_accessed=size, transcendentals=0),
    )(*args)


def shaped(shape, dtype):
    return jax.ShapeDtypeStruct(shape, dtype)


def row_weights_kernel(count, place, vals, feat, weights, vals_out, feat_out):
    feat_out[...] = feat[...]

    def keep(i, carry):
        for u in range(GROUP):
            vals_out[i * GROUP + u] = vals[i * GROUP + u]
        return carry

    lax.fori_loop(0, vals.shape[0] // GROUP, keep, 0)
    weights[...] = jnp.zeros_like(weights)
    ones = jnp.ones((8, 128), BF)

    def step(i, carry):
        slots = [i * GROUP + u for u in range(GROUP)]
        sums = [
            lax.dot_general(ones, vals[s], CONTRACT_COLS, preferred_element_type=F32) for s in slots
        ]
        for s, term in zip(slots, sums):
            weights[place[s]] += term
        return carry

    lax.fori_loop(0, (count[0] + GROUP - 1) // GROUP, step, 0)


def row_weights(count, place, vals, feat):
    return call(
        row_weights_kernel,
        [shaped((33, 8, 128), F32), shaped(vals.shape, BF), shaped(feat.shape, BF)],
        (count, place, vals, feat),
        [SMEM, SMEM, VMEM, VMEM],
    )


def turn_kernel(vals, turned):
    def step(i, carry):
        for u in range(GROUP):
            turned[i * GROUP + u] = vals[i * GROUP + u].T
        return carry

    lax.fori_loop(0, vals.shape[0] // GROUP, step, 0)


def turn(vals):
    return call(turn_kernel, [shaped(vals.shape, BF)], (vals,), [VMEM], flops=6 * 10**9)[0]


GROUP = 4
TURN = 16
BACKWARD_COST = 20 * 10**9
PAIR_COST = 5 * 10**9
TOTAL_COST = 5 * 10**9
PAD = 16


def put_weights(out, rows, value):
    count = value.shape[0]
    if out.dtype == F32:
        out[rows : rows + count, :128] = value
        return
    out[rows:, :] = jnp.zeros((PAD, out.shape[1]), out.dtype)
    lead = value.astype(BF)
    trail = (value - lead.astype(F32)).astype(BF)
    both = jnp.concatenate([lead.astype(F32), trail.astype(F32)], axis=1)
    both = jnp.concatenate([both, jnp.zeros((PAD - count, 256), F32)], axis=0)
    out[rows:, :256] = both.astype(BF)


def get_weights(ref, rows, count):
    got = ref[rows : rows + PAD, :256].astype(F32)[:count]
    if ref.dtype == F32:
        return got[:, :128]
    return got[:, :128] + got[:, 128:]


def forward_kernel(count, place_a, place_b, source, vals, weights, *refs):
    pieces, (total_a, low_a, high_a, total_b, low_b, high_b), (panel, sems) = (
        refs[:8],
        refs[8:14],
        refs[14:],
    )
    copies = [
        pltpu.make_async_copy(piece, panel.at[k], sems.at[k]) for k, piece in enumerate(pieces)
    ]
    for copy in copies:
        copy.start()

    def clear(k, carry):
        total_a[k] = jnp.zeros((128, 256), F32)
        total_b[k] = jnp.zeros((128, 256), F32)
        return carry

    lax.fori_loop(0, 33, clear, 0)
    for copy in copies:
        copy.wait()

    def step(i, carry):
        for u in range(TURN):
            s = i * TURN + u
            term = jnp.dot(vals[s], panel[source[s]], preferred_element_type=F32)
            total_a[place_a[s]] += term[:, :256]
            total_b[place_b[s]] += term[:, 256:]
        return carry

    lax.fori_loop(0, (count[0] + TURN - 1) // TURN, step, 0)

    def finish(k, carry):
        rows = pl.ds(pl.multiple_of(k * 128, 128), 128)
        low_a[rows, :] = total_a[16 + k].astype(BF)
        high_a[rows, :] = total_a[20 + k].astype(BF)
        low_b[rows, :] = total_b[16 + k].astype(BF)
        high_b[rows, :] = total_b[20 + k].astype(BF)
        return carry

    lax.fori_loop(0, 4, finish, 0)
    put_weights(low_a, 512, rows_of(weights, 16, 4))
    put_weights(high_a, 512, rows_of(weights, 20, 4))


def rows_of(weights, begin, count):
    return jnp.concatenate([weights[begin + k, 0:1, :] for k in range(count)], axis=0)


def forward(count, place_a, place_b, source, vals, weights, pieces):
    full = shaped((33, 128, 256), F32)
    cut = shaped((512 + PAD, 256), BF)
    plain = shaped((512, 256), BF)
    return call(
        forward_kernel,
        [full, cut, cut, full, plain, plain],
        (count, place_a, place_b, source, vals, weights, *pieces),
        [SMEM] * 4 + [VMEM] * 2 + [ANY] * 8,
        [pltpu.VMEM((8, 128, 512), BF), pltpu.SemaphoreType.DMA((8,))],
        flops=2 * 48 * 128 * 128 * 512,
        own=4 * MIB,
    )


def pass_kernel(carries, total, weights, low, high, ahead_out, behind_out):
    def first(k, carry):
        rows = pl.ds(pl.multiple_of(k * 128, 128), 128)
        later = pl.ds(pl.multiple_of(512 + k * 128, 128), 128)
        ahead_out[rows, :] = (total[8 + k] + low[rows, :].astype(F32)).astype(BF)
        ahead_out[later, :] = total[12 + k].astype(BF)
        behind_out[rows, :] = total[24 + k].astype(BF)
        behind_out[later, :] = (total[28 + k] + high[rows, :].astype(F32)).astype(BF)
        return carry

    lax.fori_loop(0, 4, first, 0)
    if carries:
        none = jnp.zeros((4, 128), F32)
        low_weight = jnp.concatenate([get_weights(low, 512, 4), none], axis=0)
        high_weight = jnp.concatenate([none, get_weights(high, 512, 4)], axis=0)
        put_weights(ahead_out, 1024, rows_of(weights, 8, 8) + low_weight)
        put_weights(behind_out, 1024, rows_of(weights, 24, 8) + high_weight)


def pass_on(carries, total, weights, low, high):
    out = shaped((1024 + (PAD if carries else 0), 256), BF)
    return call(
        functools.partial(pass_kernel, carries),
        [out, out],
        (total, weights, low, high),
        [VMEM] * 4,
    )


def merge_kernel(carries, own, weights, a, b, *outs):
    for part, out in enumerate(outs):
        for k in range(2):
            rows = slice(256 * part + 128 * k, 256 * part + 128 * k + 128)
            total = own[2 * part + k] + a[rows].astype(F32) + b[rows].astype(F32)
            out[128 * k : 128 * k + 128] = total.astype(out.dtype)
    if carries:
        weight = rows_of(weights, 0, 8) + get_weights(a, 1024, 8) + get_weights(b, 1024, 8)
        for part, out in enumerate(outs):
            put_weights(out, 256, weight[2 * part : 2 * part + 2])


def merge(carries, own, weights, a, b):
    rows = 256 + (PAD if carries else 0)
    return call(
        functools.partial(merge_kernel, carries),
        [shaped((rows, 256), F32)] + [shaped((rows, 256), BF)] * 3,
        (own, weights, a, b),
        [VMEM] * 4,
    )


def join_kernel(*refs):
    parts_a, parts_b, give = refs[:4], refs[4:8], refs[8]
    for at, parts in ((0, parts_a), (256, parts_b)):
        total = parts[0][:256]
        for part in parts[1:]:
            total += part[:256].astype(F32)
        give[:256, at : at + 256] = total.astype(BF)
    put_weights(give, 256, sum(get_weights(ref, 256, 2) for ref in parts_a))


def join(parts_a, parts_b):
    return call(
        join_kernel,
        [shaped((256 + PAD, 512), BF)],
        (*parts_a, *parts_b),
        [VMEM] * 8,
    )[0]


def node_kernel(
    place, given, got, feat, self_pre, cot, w_neigh, layer_out, mean_out, grad_out, back_a, back_b, send
):
    @pl.when(place[1] != 0)
    def _():
        send[:256, :] = feat[...]

    weight, came = get_weights(given, 256, 2), get_weights(got, 256, 2)
    for k in range(2):
        rows, back = slice(128 * k, 128 * k + 128), slice(128 - 128 * k, 256 - 128 * k)
        degree = 1.0 + (weight[k : k + 1, :] + came[1 - k : 2 - k, :])
        inverse = 1.0 / jnp.broadcast_to(degree, (128, 128)).T
        inverse = jnp.concatenate([inverse] * 4, axis=1)
        mean = ((given[rows].astype(F32) + got[back].astype(F32)) * inverse).astype(BF)
        pre_act = self_pre[rows] + jnp.dot(mean, w_neigh[...], preferred_element_type=F32)
        sigmoid_val = jax.nn.sigmoid(pre_act)
        grad = cot[rows].astype(F32) * sigmoid_val * (1.0 + pre_act * (1.0 - sigmoid_val))
        grad = grad.astype(BF)
        back_mean = lax.dot_general(
            grad, w_neigh[...], CONTRACT_COLS, preferred_element_type=F32
        )
        scaled = (back_mean * inverse).astype(BF)
        back_a[rows, :] = scaled[:, :256]
        back_b[rows, :] = scaled[:, 256:]
        mean_out[rows, :] = mean
        grad_out[rows, :] = grad
        send[256 + 128 * k : 384 + 128 * k, :] = grad

        @pl.when(place[1] == 0)
        def _():
            send[rows, :] = mean

        if k == 0:
            layer_out[...] = (pre_act * sigmoid_val).astype(BF)


def node(place, given, got, feat, self_pre, cot, w_neigh):
    wide = shaped((256, 512), BF)
    half = shaped((256, 256), BF)
    return call(
        node_kernel,
        [shaped((128, 512), BF), wide, wide, half, half, shaped((512, 512), BF)],
        (place, given, got, feat, self_pre, cot, w_neigh),
        [SMEM] + [VMEM] * 6,
        flops=8 * 128 * 512 * 512,
    )


def backward_kernel(count, from_a, from_b, place, vals, *refs):
    parts_a, parts_b, outs = refs[:5], refs[5:10], refs[10:12]
    panel_a, panel_b, total, sems = refs[12:]
    copies = []
    begin = 0
    for k, (part_a, part_b) in enumerate(zip(parts_a, parts_b)):
        rows = pl.ds(begin, part_a.shape[0])
        begin += part_a.shape[0]
        copies.append(pltpu.make_async_copy(part_a, panel_a.at[rows], sems.at[k]))
        copies.append(pltpu.make_async_copy(part_b, panel_b.at[rows], sems.at[5 + k]))
    for copy in copies:
        copy.start()

    def clear(k, carry):
        total[k] = jnp.zeros((128, 512), F32)
        return carry

    lax.fori_loop(0, 9, clear, 0)
    for copy in copies:
        copy.wait()

    def step(i, carry):
        for u in range(TURN):
            s = i * TURN + u
            block = vals[s]
            rows_a = pl.ds(pl.multiple_of(from_a[s] * 128, 128), 128)
            rows_b = pl.ds(pl.multiple_of(from_b[s] * 128, 128), 128)
            first = jnp.dot(block, panel_a[rows_a, :], preferred_element_type=F32)
            second = jnp.dot(block, panel_b[rows_b, :], preferred_element_type=F32)
            total[place[s], :, :256] += first
            total[place[s], :, 256:] += second
        return carry

    lax.fori_loop(0, (count[0] + TURN - 1) // TURN, step, 0)

    def finish(k, carry):
        for part, out in enumerate(outs):
            out[k] = total[part * 4 + k].astype(out.dtype)
        return carry

    lax.fori_loop(0, 4, finish, 0)


def backward(count, from_a, from_b, place, turned, parts_a, parts_b):
    return call(
        backward_kernel,
        [shaped((4, 128, 512), F32), shaped((4, 128, 512), BF)],
        (count, from_a, from_b, place, turned, *parts_a, *parts_b),
        [SMEM] * 4 + [VMEM] + [ANY] * 10,
        [
            pltpu.VMEM((4096, 256), BF),
            pltpu.VMEM((4096, 256), BF),
            pltpu.VMEM((9, 128, 512), F32),
            pltpu.SemaphoreType.DMA((10,)),
        ],
        flops=BACKWARD_COST,
        own=4 * MIB,
    )


def pair_kernel(own, got, *outs):
    for k, out in enumerate(outs):
        out[...] = (own[k] + got[k].astype(F32)).astype(out.dtype)


def pair(own, got):
    piece = own.shape[1:]
    return call(
        pair_kernel,
        [shaped(piece, F32)] + [shaped(piece, BF)] * 3,
        (own, got),
        [VMEM] * 2,
        flops=PAIR_COST,
    )


def total_kernel(product, own, a, b, c, out):
    total = own[...] + a[...].astype(F32) + b[...].astype(F32) + c[...].astype(F32)
    out[...] = product[...] + total


def total(product, own, got):
    return call(
        total_kernel,
        [shaped((128, 512), F32)],
        (product, own, *got),
        [VMEM] * 5,
        flops=TOTAL_COST,
    )[0]


BIAS_ROWS = 16
CHUNK = 128 + BIAS_ROWS


def weights_kernel(place, feat, mean, grad, got, keep_out, give_out):
    nodes = (slice(0, 128), slice(128, 256))
    came = tuple(slice(n.start + 256, n.stop + 256) for n in nodes)
    bias = [jnp.sum(grad[n].astype(F32), axis=0, keepdims=True) for n in nodes]
    bias += [jnp.sum(got[n].astype(F32), axis=0, keepdims=True) for n in came]
    bias = (bias[0] + bias[1]) + (bias[2] + bias[3])
    bias = jnp.broadcast_to(bias, (BIAS_ROWS, 512))

    def emit(lhs):
        for m in range(4):
            begin = pl.multiple_of((place[0] ^ m) * 128, 128)
            columns = pl.ds(begin, 128)
            mine = [
                lax.dot_general(
                    lhs[n, columns], grad[n], CONTRACT_ROWS, preferred_element_type=F32
                )
                for n in nodes
            ]
            theirs = [
                lax.dot_general(got[n, columns], got[g], CONTRACT_ROWS, preferred_element_type=F32)
                for n, g in zip(nodes, came)
            ]
            out = keep_out if m < 2 else give_out
            out[m % 2, :128, :] = ((mine[0] + mine[1]) + (theirs[0] + theirs[1])).astype(out.dtype)
            out[m % 2, 128:, :] = bias.astype(out.dtype)

    @pl.when(place[1] == 0)
    def _():
        emit(feat)

    @pl.when(place[1] != 0)
    def _():
        emit(mean)


def weights(place, feat, mean, grad, got):
    piece = (2, CHUNK, 512)
    return call(
        weights_kernel,
        [shaped(piece, F32), shaped(piece, BF)],
        (place, feat, mean, grad, got),
        [SMEM] + [VMEM] * 4,
        flops=4 * 128 * 512 * 512,
    )


def halve_kernel(own, got, keep, give):
    half = keep.shape[0]
    for k in range(half):
        keep[k] = own[k] + got[k].astype(F32)
        give[k] = (own[half + k] + got[half + k].astype(F32)).astype(BF)


def halve(own, got):
    piece = (own.shape[0] // 2,) + own.shape[1:]
    return call(halve_kernel, [shaped(piece, F32), shaped(piece, BF)], (own, got), [VMEM] * 2)


def arrange_kernel(place, mine, other, self_out, neigh_out):
    def emit(first, second):
        for m in range(4):
            rows = pl.ds(pl.multiple_of((place[0] ^ m) * 128, 128), 128)
            self_out[rows, :] = first[128 * m : 128 * m + 128].astype(F32)
            neigh_out[rows, :] = second[128 * m : 128 * m + 128].astype(F32)

    @pl.when(place[1] == 0)
    def _():
        emit(mine, other)

    @pl.when(place[1] != 0)
    def _():
        emit(other, mine)


def arrange(place, mine, other):
    out = shaped((512, 512), F32)
    return call(arrange_kernel, [out, out], (place, mine, other), [SMEM, VMEM, VMEM])


def ring_sum(value, **axis):
    (name,) = axis
    sent = value.astype(BF)
    got = {k: shift(sent, **{name: k}).astype(F32) for k in others(name)}
    return (sent.astype(F32) + got[2]) + (got[1] + got[3])


def meet_sum(value, **axis):
    sent = value.astype(BF)
    return sent.astype(F32) + meet(sent, **axis).astype(F32)


def local(
    features, cotangent, w_self, w_neigh, out_bias, block_vals, block_rows, block_cols, block_count
):
    device = lax.axis_index("row") * 32 + lax.axis_index("col")
    my_zh, my_core, my_zl, my_x, my_y = coords(device)
    slots = block_vals.shape[0]
    live = jnp.arange(slots, dtype=jnp.int32) < block_count[0]
    rel_z = (block_rows // 16 - my_zl) % ZL
    rel_x = (block_rows // 4 % 4 - my_x) % X
    rel_y = (block_rows % 4 - my_y) % Y
    rows_a = rel_x * 8 + rel_y * 2 + rel_z
    rows_b = rel_y * 8 + rel_x * 2 + rel_z
    place_a = jnp.where(live, rows_a, 32)
    place_b = jnp.where(live, rows_b, 32)
    rel_h = (block_cols // 2 - my_zh) % ZH
    rel_c = (block_cols % 2 - my_core) % CORE
    source = rel_h * 2 + rel_c
    back_place = jnp.where(live, rel_c * 4 + rel_h, 8)

    place = jnp.stack([my_x, my_core]).astype(jnp.int32)

    ahead = {k: shift(features, zh=-k) for k in others("zh")}
    weight, near_vals, ahead[0] = row_weights(block_count, place_a, block_vals, features)
    ahead[1], weight = lax.optimization_barrier((ahead[1], weight))
    pieces = []
    for k in range(4):
        pieces += [ahead[k], shift(ahead[k] if k else features, core=1)]

    total_a, low_a, high_a, total_b, low_b, high_b = forward(
        block_count, place_a, place_b, source, near_vals, weight, pieces
    )
    low_a, high_a = shift(low_a, x=1), shift(high_a, x=-1)
    low_b, high_b = shift(low_b, y=1), shift(high_b, y=-1)
    ahead_a, behind_a = pass_on(True, total_a, weight, low_a, high_a)
    ahead_b, behind_b = pass_on(False, total_b, weight, low_b, high_b)
    got_a = [shift(ahead_a, x=1), shift(behind_a, x=-1)]
    got_b = [shift(ahead_b, y=1), shift(behind_b, y=-1)]

    later, _ = lax.optimization_barrier(((features, cotangent, block_vals), ahead_a))
    feat_late, cot_late, vals_late = later
    late = shift(jnp.concatenate([feat_late, cot_late]), zl=1)
    both_feat = jnp.concatenate([feat_late, late[:128]])
    both_cot = jnp.concatenate([cot_late, late[128:]])
    self_pre = jnp.dot(both_feat, w_self, preferred_element_type=F32) + out_bias
    turned = turn(vals_late)
    (got_a, got_b), self_pre, both_cot, turned = lax.optimization_barrier(
        ((got_a, got_b), self_pre, both_cot, turned)
    )

    parts_a = merge(True, total_a, weight, *got_a)
    got_a = [shift(parts_a[k], y=k) for k in others("y")]
    parts_b = merge(False, total_b, weight, *got_b)
    got_b = [shift(parts_b[k], x=k) for k in others("x")]
    given = join([parts_a[0], *got_a], [parts_b[0], *got_b])
    layer_out, mean_agg, grad_pre, back_a, back_b, send = node(
        place, given, shift(given, zl=1), both_feat, self_pre, both_cot, w_neigh
    )

    near_a, near_b = {0: back_a}, {0: back_b}
    for k in others("y"):
        near_a[k] = shift(back_a, y=-k)
        near_b[k] = shift(back_b, x=-k)
    own_a = jnp.concatenate([near_a[k] for k in range(4)])
    own_b = jnp.concatenate([near_b[k] for k in range(4)])

    got = shift(send, core=1)
    keep_part, give_part = weights(place, both_feat, mean_agg, grad_pre, got)
    came, own_b = lax.optimization_barrier((meet(give_part, x=2), own_b))
    keep_part, give_part = halve(keep_part, came)
    next_a, last_a = shift(own_a, x=-1), shift(own_a, x=1)
    next_b, last_b = shift(own_b, y=-1), shift(own_b, y=1)
    low_a, high_a = shift(last_a[:512], x=1), shift(next_a[512:], x=-1)
    low_b, high_b = shift(last_b[:512], y=1), shift(next_b[512:], y=-1)
    chunk = keep_part[0] + meet(give_part[0], x=1).astype(F32)
    chunk = meet_sum(chunk, zh=1)
    chunk = meet_sum(chunk, zh=2)

    grad_self = lax.dot_general(grad_pre[:128], w_self, CONTRACT_COLS, preferred_element_type=F32)
    own, give = backward(
        block_count,
        rows_a,
        rows_b,
        back_place,
        turned,
        [own_a, next_a, low_a, high_a, last_a],
        [own_b, next_b, low_b, high_b, last_b],
    )
    parts = pair(own, shift(give, core=1))
    chunk = ring_sum(chunk, y=1)
    scale = 1.0 / math.sqrt(128 * DEVICES)
    bias_grad = chunk[128] * scale
    block = (chunk[:128] * scale).astype(BF)
    block, parts = lax.optimization_barrier((block, parts))
    block = jnp.concatenate([block] + [meet(block, x=m) for m in (1, 2, 3)])
    feature_grad = total(grad_self, parts[0], [shift(parts[k], zh=k) for k in others("zh")])
    self_grad, neigh_grad = arrange(place, block, shift(block, core=1))
    return layer_out, feature_grad, self_grad, neigh_grad, bias_grad


def solution(mesh):
    return jax.shard_map(
        local,
        mesh=mesh,
        in_specs=(
            P(("row", "col"), None),
            P(("row", "col"), None),
            P(),
            P(),
            P(),
            P(("row", "col"), None, None),
            P(("row", "col")),
            P(("row", "col")),
            P(("row", "col")),
        ),
        out_specs=(P(("row", "col"), None), P(("row", "col"), None), P(), P(), P()),
        check_vma=False,
    )
```

```python
import functools
import math

import jax
import jax.numpy as jnp
from jax import lax
from jax.experimental import pallas as pl
from jax.experimental.pallas import tpu as pltpu
from jax.sharding import PartitionSpec as P

BF = jnp.bfloat16
F32 = jnp.float32
AXES = ("row", "col")
ZH, CORE, ZL, X, Y = 4, 2, 2, 4, 4
DEVICES = ZH * CORE * ZL * X * Y
VMEM = pl.BlockSpec(memory_space=pltpu.VMEM)
SMEM = pl.BlockSpec(memory_space=pltpu.SMEM)
ANY = pl.BlockSpec(memory_space=pl.ANY)
CONTRACT_ROWS = (((0,), (0,)), ((), ()))
CONTRACT_COLS = (((1,), (1,)), ((), ()))
MIB = 1 << 20


def coords(device):
    y = device % Y
    x = device // Y % X
    zl = device // (Y * X) % ZL
    core = device // (Y * X * ZL) % CORE
    zh = device // (Y * X * ZL * CORE)
    return zh, core, zl, x, y


def shift(value, zh=0, core=0, zl=0, x=0, y=0):
    pairs = []
    for device in range(DEVICES):
        a, b, c, d, e = coords(device)
        a, b, c, d, e = (a + zh) % ZH, (b + core) % CORE, (c + zl) % ZL, (d + x) % X, (e + y) % Y
        pairs.append((device, (((a * CORE + b) * ZL + c) * X + d) * Y + e))
    return lax.ppermute(value, AXES, pairs)


def meet(value, **axis):
    ((name, bit),) = axis.items()
    at = ("zh", "core", "zl", "x", "y").index(name)
    pairs = []
    for device in range(DEVICES):
        place = list(coords(device))
        place[at] ^= bit
        a, b, c, d, e = place
        pairs.append((device, (((a * CORE + b) * ZL + c) * X + d) * Y + e))
    return lax.ppermute(value, AXES, pairs)


def others(axis):
    return (2, 1, 3)


def call(kernel, outs, args, specs, scratch=(), flops=0, own=0):
    size = sum(math.prod(o.shape) * o.dtype.itemsize for o in outs)
    size += sum(math.prod(a.shape) * a.dtype.itemsize for a in args)
    return pl.pallas_call(
        kernel,
        out_shape=tuple(outs),
        in_specs=list(specs),
        out_specs=(VMEM,) * len(outs),
        scratch_shapes=list(scratch),
        compiler_params=pltpu.CompilerParams(vmem_limit_bytes=size + own + 3 * MIB),
        cost_estimate=pl.CostEstimate(flops=flops, bytes_accessed=size, transcendentals=0),
    )(*args)


def shaped(shape, dtype):
    return jax.ShapeDtypeStruct(shape, dtype)


def row_weights_kernel(count, place, vals, feat, weights, vals_out, feat_out):
    feat_out[...] = feat[...]

    def keep(i, carry):
        for u in range(GROUP):
            vals_out[i * GROUP + u] = vals[i * GROUP + u]
        return carry

    lax.fori_loop(0, vals.shape[0] // GROUP, keep, 0)
    weights[...] = jnp.zeros_like(weights)
    ones = jnp.ones((8, 128), BF)

    def step(i, carry):
        slots = [i * GROUP + u for u in range(GROUP)]
        sums = [
            lax.dot_general(ones, vals[s], CONTRACT_COLS, preferred_element_type=F32) for s in slots
        ]
        for s, term in zip(slots, sums):
            weights[place[s]] += term
        return carry

    lax.fori_loop(0, (count[0] + GROUP - 1) // GROUP, step, 0)


def row_weights(count, place, vals, feat):
    return call(
        row_weights_kernel,
        [shaped((33, 8, 128), F32), shaped(vals.shape, BF), shaped(feat.shape, BF)],
        (count, place, vals, feat),
        [SMEM, SMEM, VMEM, VMEM],
    )


def turn_kernel(vals, turned):
    def step(i, carry):
        for u in range(GROUP):
            turned[i * GROUP + u] = vals[i * GROUP + u].T
        return carry

    lax.fori_loop(0, vals.shape[0] // GROUP, step, 0)


def turn(vals):
    return call(turn_kernel, [shaped(vals.shape, BF)], (vals,), [VMEM], flops=6 * 10**9)[0]


GROUP = 4
TURN = 16
BACKWARD_COST = 20 * 10**9
PAIR_COST = 5 * 10**9
TOTAL_COST = 5 * 10**9
PAD = 16


def put_weights(out, rows, value):
    count = value.shape[0]
    if out.dtype == F32:
        out[rows : rows + count, :128] = value
        return
    out[rows:, :] = jnp.zeros((PAD, out.shape[1]), out.dtype)
    lead = value.astype(BF)
    trail = (value - lead.astype(F32)).astype(BF)
    both = jnp.concatenate([lead.astype(F32), trail.astype(F32)], axis=1)
    both = jnp.concatenate([both, jnp.zeros((PAD - count, 256), F32)], axis=0)
    out[rows:, :256] = both.astype(BF)


def get_weights(ref, rows, count):
    got = ref[rows : rows + PAD, :256].astype(F32)[:count]
    if ref.dtype == F32:
        return got[:, :128]
    return got[:, :128] + got[:, 128:]


def forward_kernel(count, place_a, place_b, source, fresh, bare, vals, weights, *refs):
    pieces, (total_a, low_a, high_a, total_b, low_b, high_b), (panel, sems) = (
        refs[:8],
        refs[8:14],
        refs[14:],
    )
    copies = [
        pltpu.make_async_copy(piece, panel.at[k], sems.at[k]) for k, piece in enumerate(pieces)
    ]
    for copy in copies:
        copy.start()

    def clear(k, carry):
        @pl.when(bare[k] != 0)
        def _():
            total_a[k] = jnp.zeros((128, 256), F32)

        @pl.when(bare[32 + k] != 0)
        def _():
            total_b[k] = jnp.zeros((128, 256), F32)

        return carry

    lax.fori_loop(0, 32, clear, 0)
    for copy in copies:
        copy.wait()

    def step(i, carry):
        for u in range(TURN):
            s = i * TURN + u
            term = jnp.dot(vals[s], panel[source[s]], preferred_element_type=F32)
            first = fresh[s] != 0
            old_a, old_b = total_a[place_a[s]], total_b[place_b[s]]
            total_a[place_a[s]] = term[:, :256] + jnp.where(first, 0.0, old_a)
            total_b[place_b[s]] = term[:, 256:] + jnp.where(first, 0.0, old_b)
        return carry

    lax.fori_loop(0, (count[0] + TURN - 1) // TURN, step, 0)

    def finish(k, carry):
        rows = pl.ds(pl.multiple_of(k * 128, 128), 128)
        low_a[rows, :] = total_a[16 + k].astype(BF)
        high_a[rows, :] = total_a[20 + k].astype(BF)
        low_b[rows, :] = total_b[16 + k].astype(BF)
        high_b[rows, :] = total_b[20 + k].astype(BF)
        return carry

    lax.fori_loop(0, 4, finish, 0)
    put_weights(low_a, 512, rows_of(weights, 16, 4))
    put_weights(high_a, 512, rows_of(weights, 20, 4))


def rows_of(weights, begin, count):
    return jnp.concatenate([weights[begin + k, 0:1, :] for k in range(count)], axis=0)


def forward(count, place_a, place_b, source, fresh, bare, vals, weights, pieces):
    full = shaped((33, 128, 256), F32)
    cut = shaped((512 + PAD, 256), BF)
    plain = shaped((512, 256), BF)
    return call(
        forward_kernel,
        [full, cut, cut, full, plain, plain],
        (count, place_a, place_b, source, fresh, bare, vals, weights, *pieces),
        [SMEM] * 6 + [VMEM] * 2 + [ANY] * 8,
        [pltpu.VMEM((8, 128, 512), BF), pltpu.SemaphoreType.DMA((8,))],
        flops=2 * 48 * 128 * 128 * 512,
        own=4 * MIB,
    )


def pass_kernel(carries, total, weights, low, high, ahead_out, behind_out):
    def first(k, carry):
        rows = pl.ds(pl.multiple_of(k * 128, 128), 128)
        later = pl.ds(pl.multiple_of(512 + k * 128, 128), 128)
        ahead_out[rows, :] = (total[8 + k] + low[rows, :].astype(F32)).astype(BF)
        ahead_out[later, :] = total[12 + k].astype(BF)
        behind_out[rows, :] = total[24 + k].astype(BF)
        behind_out[later, :] = (total[28 + k] + high[rows, :].astype(F32)).astype(BF)
        return carry

    lax.fori_loop(0, 4, first, 0)
    if carries:
        none = jnp.zeros((4, 128), F32)
        low_weight = jnp.concatenate([get_weights(low, 512, 4), none], axis=0)
        high_weight = jnp.concatenate([none, get_weights(high, 512, 4)], axis=0)
        put_weights(ahead_out, 1024, rows_of(weights, 8, 8) + low_weight)
        put_weights(behind_out, 1024, rows_of(weights, 24, 8) + high_weight)


def pass_on(carries, total, weights, low, high):
    out = shaped((1024 + (PAD if carries else 0), 256), BF)
    return call(
        functools.partial(pass_kernel, carries),
        [out, out],
        (total, weights, low, high),
        [VMEM] * 4,
    )


def merge_kernel(carries, own, weights, a, b, *outs):
    for part, out in enumerate(outs):
        for k in range(2):
            rows = slice(256 * part + 128 * k, 256 * part + 128 * k + 128)
            total = own[2 * part + k] + a[rows].astype(F32) + b[rows].astype(F32)
            out[128 * k : 128 * k + 128] = total.astype(out.dtype)
    if carries:
        weight = rows_of(weights, 0, 8) + get_weights(a, 1024, 8) + get_weights(b, 1024, 8)
        for part, out in enumerate(outs):
            put_weights(out, 256, weight[2 * part : 2 * part + 2])


def merge(carries, own, weights, a, b):
    rows = 256 + (PAD if carries else 0)
    return call(
        functools.partial(merge_kernel, carries),
        [shaped((rows, 256), F32)] + [shaped((rows, 256), BF)] * 3,
        (own, weights, a, b),
        [VMEM] * 4,
    )


def join_kernel(*refs):
    parts_a, parts_b, give = refs[:4], refs[4:8], refs[8]
    for at, parts in ((0, parts_a), (256, parts_b)):
        total = parts[0][:256]
        for part in parts[1:]:
            total += part[:256].astype(F32)
        give[:256, at : at + 256] = total.astype(BF)
    put_weights(give, 256, sum(get_weights(ref, 256, 2) for ref in parts_a))


def join(parts_a, parts_b):
    return call(
        join_kernel,
        [shaped((256 + PAD, 512), BF)],
        (*parts_a, *parts_b),
        [VMEM] * 8,
    )[0]


def node_kernel(
    place, given, got, feat, self_pre, cot, w_neigh, layer_out, mean_out, grad_out, back_a, back_b, send
):
    @pl.when(place[1] != 0)
    def _():
        send[:256, :] = feat[...]

    weight, came = get_weights(given, 256, 2), get_weights(got, 256, 2)
    for k in range(2):
        rows, back = slice(128 * k, 128 * k + 128), slice(128 - 128 * k, 256 - 128 * k)
        degree = 1.0 + (weight[k : k + 1, :] + came[1 - k : 2 - k, :])
        inverse = 1.0 / jnp.broadcast_to(degree, (128, 128)).T
        inverse = jnp.concatenate([inverse] * 4, axis=1)
        mean = ((given[rows].astype(F32) + got[back].astype(F32)) * inverse).astype(BF)
        pre_act = self_pre[rows] + jnp.dot(mean, w_neigh[...], preferred_element_type=F32)
        sigmoid_val = jax.nn.sigmoid(pre_act)
        grad = cot[rows].astype(F32) * sigmoid_val * (1.0 + pre_act * (1.0 - sigmoid_val))
        grad = grad.astype(BF)
        back_mean = lax.dot_general(
            grad, w_neigh[...], CONTRACT_COLS, preferred_element_type=F32
        )
        scaled = (back_mean * inverse).astype(BF)
        back_a[rows, :] = scaled[:, :256]
        back_b[rows, :] = scaled[:, 256:]
        mean_out[rows, :] = mean
        grad_out[rows, :] = grad
        send[256 + 128 * k : 384 + 128 * k, :] = grad

        @pl.when(place[1] == 0)
        def _():
            send[rows, :] = mean

        if k == 0:
            layer_out[...] = (pre_act * sigmoid_val).astype(BF)


def node(place, given, got, feat, self_pre, cot, w_neigh):
    wide = shaped((256, 512), BF)
    half = shaped((256, 256), BF)
    return call(
        node_kernel,
        [shaped((128, 512), BF), wide, wide, half, half, shaped((512, 512), BF)],
        (place, given, got, feat, self_pre, cot, w_neigh),
        [SMEM] + [VMEM] * 6,
        flops=8 * 128 * 512 * 512,
    )


def backward_kernel(count, from_a, from_b, place, vals, *refs):
    parts_a, parts_b, outs = refs[:5], refs[5:10], refs[10:12]
    panel_a, panel_b, total, sems = refs[12:]
    copies = []
    begin = 0
    for k, (part_a, part_b) in enumerate(zip(parts_a, parts_b)):
        rows = pl.ds(begin, part_a.shape[0])
        begin += part_a.shape[0]
        copies.append(pltpu.make_async_copy(part_a, panel_a.at[rows], sems.at[k]))
        copies.append(pltpu.make_async_copy(part_b, panel_b.at[rows], sems.at[5 + k]))
    for copy in copies:
        copy.start()

    def clear(k, carry):
        total[k] = jnp.zeros((128, 512), F32)
        return carry

    lax.fori_loop(0, 9, clear, 0)
    for copy in copies:
        copy.wait()

    def step(i, carry):
        for u in range(TURN):
            s = i * TURN + u
            block = vals[s]
            rows_a = pl.ds(pl.multiple_of(from_a[s] * 128, 128), 128)
            rows_b = pl.ds(pl.multiple_of(from_b[s] * 128, 128), 128)
            first = jnp.dot(block, panel_a[rows_a, :], preferred_element_type=F32)
            second = jnp.dot(block, panel_b[rows_b, :], preferred_element_type=F32)
            total[place[s], :, :256] += first
            total[place[s], :, 256:] += second
        return carry

    lax.fori_loop(0, (count[0] + TURN - 1) // TURN, step, 0)

    def finish(k, carry):
        for part, out in enumerate(outs):
            out[k] = total[part * 4 + k].astype(out.dtype)
        return carry

    lax.fori_loop(0, 4, finish, 0)


def backward(count, from_a, from_b, place, turned, parts_a, parts_b):
    return call(
        backward_kernel,
        [shaped((4, 128, 512), F32), shaped((4, 128, 512), BF)],
        (count, from_a, from_b, place, turned, *parts_a, *parts_b),
        [SMEM] * 4 + [VMEM] + [ANY] * 10,
        [
            pltpu.VMEM((4096, 256), BF),
            pltpu.VMEM((4096, 256), BF),
            pltpu.VMEM((9, 128, 512), F32),
            pltpu.SemaphoreType.DMA((10,)),
        ],
        flops=BACKWARD_COST,
        own=4 * MIB,
    )


def pair_kernel(own, got, *outs):
    for k, out in enumerate(outs):
        out[...] = (own[k] + got[k].astype(F32)).astype(out.dtype)


def pair(own, got):
    piece = own.shape[1:]
    return call(
        pair_kernel,
        [shaped(piece, F32)] + [shaped(piece, BF)] * 3,
        (own, got),
        [VMEM] * 2,
        flops=PAIR_COST,
    )


def total_kernel(product, own, a, b, c, out):
    total = own[...] + a[...].astype(F32) + b[...].astype(F32) + c[...].astype(F32)
    out[...] = product[...] + total


def total(product, own, got):
    return call(
        total_kernel,
        [shaped((128, 512), F32)],
        (product, own, *got),
        [VMEM] * 5,
        flops=TOTAL_COST,
    )[0]


BIAS_ROWS = 16
CHUNK = 128 + BIAS_ROWS


def weights_kernel(place, feat, mean, grad, got, keep_out, give_out):
    nodes = (slice(0, 128), slice(128, 256))
    came = tuple(slice(n.start + 256, n.stop + 256) for n in nodes)
    bias = [jnp.sum(grad[n].astype(F32), axis=0, keepdims=True) for n in nodes]
    bias += [jnp.sum(got[n].astype(F32), axis=0, keepdims=True) for n in came]
    bias = (bias[0] + bias[1]) + (bias[2] + bias[3])
    bias = jnp.broadcast_to(bias, (BIAS_ROWS, 512))

    def emit(lhs):
        for m in range(4):
            begin = pl.multiple_of((place[0] ^ m) * 128, 128)
            columns = pl.ds(begin, 128)
            mine = [
                lax.dot_general(
                    lhs[n, columns], grad[n], CONTRACT_ROWS, preferred_element_type=F32
                )
                for n in nodes
            ]
            theirs = [
                lax.dot_general(got[n, columns], got[g], CONTRACT_ROWS, preferred_element_type=F32)
                for n, g in zip(nodes, came)
            ]
            out = keep_out if m < 2 else give_out
            out[m % 2, :128, :] = ((mine[0] + mine[1]) + (theirs[0] + theirs[1])).astype(out.dtype)
            out[m % 2, 128:, :] = bias.astype(out.dtype)

    @pl.when(place[1] == 0)
    def _():
        emit(feat)

    @pl.when(place[1] != 0)
    def _():
        emit(mean)


def weights(place, feat, mean, grad, got):
    piece = (2, CHUNK, 512)
    return call(
        weights_kernel,
        [shaped(piece, F32), shaped(piece, BF)],
        (place, feat, mean, grad, got),
        [SMEM] + [VMEM] * 4,
        flops=4 * 128 * 512 * 512,
    )


def halve_kernel(own, got, keep, give):
    half = keep.shape[0]
    for k in range(half):
        keep[k] = own[k] + got[k].astype(F32)
        give[k] = (own[half + k] + got[half + k].astype(F32)).astype(BF)


def halve(own, got):
    piece = (own.shape[0] // 2,) + own.shape[1:]
    return call(halve_kernel, [shaped(piece, F32), shaped(piece, BF)], (own, got), [VMEM] * 2)


def arrange_kernel(place, mine, other, self_out, neigh_out):
    def emit(first, second):
        for m in range(4):
            rows = pl.ds(pl.multiple_of((place[0] ^ m) * 128, 128), 128)
            self_out[rows, :] = first[128 * m : 128 * m + 128].astype(F32)
            neigh_out[rows, :] = second[128 * m : 128 * m + 128].astype(F32)

    @pl.when(place[1] == 0)
    def _():
        emit(mine, other)

    @pl.when(place[1] != 0)
    def _():
        emit(other, mine)


def arrange(place, mine, other):
    out = shaped((512, 512), F32)
    return call(arrange_kernel, [out, out], (place, mine, other), [SMEM, VMEM, VMEM])


def ring_sum(value, **axis):
    (name,) = axis
    sent = value.astype(BF)
    got = {k: shift(sent, **{name: k}).astype(F32) for k in others(name)}
    return (sent.astype(F32) + got[2]) + (got[1] + got[3])


def meet_sum(value, **axis):
    sent = value.astype(BF)
    return sent.astype(F32) + meet(sent, **axis).astype(F32)


def local(
    features, cotangent, w_self, w_neigh, out_bias, block_vals, block_rows, block_cols, block_count
):
    device = lax.axis_index("row") * 32 + lax.axis_index("col")
    my_zh, my_core, my_zl, my_x, my_y = coords(device)
    slots = block_vals.shape[0]
    live = jnp.arange(slots, dtype=jnp.int32) < block_count[0]
    rel_z = (block_rows // 16 - my_zl) % ZL
    rel_x = (block_rows // 4 % 4 - my_x) % X
    rel_y = (block_rows % 4 - my_y) % Y
    rows_a = rel_x * 8 + rel_y * 2 + rel_z
    rows_b = rel_y * 8 + rel_x * 2 + rel_z
    place_a = jnp.where(live, rows_a, 32)
    place_b = jnp.where(live, rows_b, 32)
    rel_h = (block_cols // 2 - my_zh) % ZH
    rel_c = (block_cols % 2 - my_core) % CORE
    source = rel_h * 2 + rel_c
    order = jnp.arange(slots, dtype=jnp.int32)
    same = (block_rows[:, None] == block_rows[None, :]) & live[None, :]
    fresh = 1 - jnp.any(same & (order[None, :] < order[:, None]), axis=1).astype(jnp.int32)
    blocks = jnp.arange(32, dtype=jnp.int32)[:, None]
    bare = [jnp.any(blocks == place[None, :], axis=1) for place in (place_a, place_b)]
    bare = 1 - jnp.concatenate(bare).astype(jnp.int32)
    back_place = jnp.where(live, rel_c * 4 + rel_h, 8)

    place = jnp.stack([my_x, my_core]).astype(jnp.int32)

    ahead = {k: shift(features, zh=-k) for k in others("zh")}
    weight, near_vals, ahead[0] = row_weights(block_count, place_a, block_vals, features)
    ahead[1], weight, fresh, bare, source = lax.optimization_barrier(
        (ahead[1], weight, fresh, bare, source)
    )
    pieces = []
    for k in range(4):
        pieces += [ahead[k], shift(ahead[k] if k else features, core=1)]

    total_a, low_a, high_a, total_b, low_b, high_b = forward(
        block_count, place_a, place_b, source, fresh, bare, near_vals, weight, pieces
    )
    low_a, high_a = shift(low_a, x=1), shift(high_a, x=-1)
    low_b, high_b = shift(low_b, y=1), shift(high_b, y=-1)
    ahead_a, behind_a = pass_on(True, total_a, weight, low_a, high_a)
    low_b, ahead_a = lax.optimization_barrier((low_b, ahead_a))
    ahead_b, behind_b = pass_on(False, total_b, weight, low_b, high_b)
    got_a = [shift(ahead_a, x=1), shift(behind_a, x=-1)]
    got_b = [shift(ahead_b, y=1), shift(behind_b, y=-1)]

    later, _ = lax.optimization_barrier(((features, cotangent, block_vals), ahead_a))
    feat_late, cot_late, vals_late = later
    late = shift(jnp.concatenate([feat_late, cot_late]), zl=1)
    both_feat = jnp.concatenate([feat_late, late[:128]])
    both_cot = jnp.concatenate([cot_late, late[128:]])
    self_pre = jnp.dot(both_feat, w_self, preferred_element_type=F32) + out_bias
    turned = turn(vals_late)
    (got_a, got_b), self_pre, both_cot, turned = lax.optimization_barrier(
        ((got_a, got_b), self_pre, both_cot, turned)
    )

    parts_a = merge(True, total_a, weight, *got_a)
    got_a = [shift(parts_a[k], y=k) for k in others("y")]
    parts_b = merge(False, total_b, weight, *got_b)
    got_b = [shift(parts_b[k], x=k) for k in others("x")]
    given = join([parts_a[0], *got_a], [parts_b[0], *got_b])
    layer_out, mean_agg, grad_pre, back_a, back_b, send = node(
        place, given, shift(given, zl=1), both_feat, self_pre, both_cot, w_neigh
    )

    near_a, near_b = {0: back_a}, {0: back_b}
    for k in others("y"):
        near_a[k] = shift(back_a, y=-k)
        near_b[k] = shift(back_b, x=-k)
    own_a = jnp.concatenate([near_a[k] for k in range(4)])
    own_b = jnp.concatenate([near_b[k] for k in range(4)])

    got = shift(send, core=1)
    keep_part, give_part = weights(place, both_feat, mean_agg, grad_pre, got)
    came, own_b = lax.optimization_barrier((meet(give_part, x=2), own_b))
    keep_part, give_part = halve(keep_part, came)
    next_a, last_a = shift(own_a, x=-1), shift(own_a, x=1)
    next_b, last_b = shift(own_b, y=-1), shift(own_b, y=1)
    low_a, high_a = shift(last_a[:512], x=1), shift(next_a[512:], x=-1)
    low_b, high_b = shift(last_b[:512], y=1), shift(next_b[512:], y=-1)
    chunk = keep_part[0] + meet(give_part[0], x=1).astype(F32)
    chunk = meet_sum(chunk, zh=1)
    chunk = meet_sum(chunk, zh=2)

    grad_self = lax.dot_general(grad_pre[:128], w_self, CONTRACT_COLS, preferred_element_type=F32)
    own, give = backward(
        block_count,
        rows_a,
        rows_b,
        back_place,
        turned,
        [own_a, next_a, low_a, high_a, last_a],
        [own_b, next_b, low_b, high_b, last_b],
    )
    parts = pair(own, shift(give, core=1))
    chunk = ring_sum(chunk, y=1)
    scale = 1.0 / math.sqrt(128 * DEVICES)
    bias_grad = chunk[128] * scale
    block = (chunk[:128] * scale).astype(BF)
    block, parts = lax.optimization_barrier((block, parts))
    block = jnp.concatenate([block] + [meet(block, x=m) for m in (1, 2, 3)])
    feature_grad = total(grad_self, parts[0], [shift(parts[k], zh=k) for k in others("zh")])
    self_grad, neigh_grad = arrange(place, block, shift(block, core=1))
    return layer_out, feature_grad, self_grad, neigh_grad, bias_grad


def solution(mesh):
    return jax.shard_map(
        local,
        mesh=mesh,
        in_specs=(
            P(("row", "col"), None),
            P(("row", "col"), None),
            P(),
            P(),
            P(),
            P(("row", "col"), None, None),
            P(("row", "col")),
            P(("row", "col")),
            P(("row", "col")),
        ),
        out_specs=(P(("row", "col"), None), P(("row", "col"), None), P(), P(), P()),
        check_vma=False,
    )
```

```python
import functools
import math

import jax
import jax.numpy as jnp
from jax import lax
from jax.experimental import pallas as pl
from jax.experimental.pallas import tpu as pltpu
from jax.sharding import PartitionSpec as P

BF = jnp.bfloat16
F32 = jnp.float32
AXES = ("row", "col")
ZH, CORE, ZL, X, Y = 4, 2, 2, 4, 4
DEVICES = ZH * CORE * ZL * X * Y
VMEM = pl.BlockSpec(memory_space=pltpu.VMEM)
SMEM = pl.BlockSpec(memory_space=pltpu.SMEM)
ANY = pl.BlockSpec(memory_space=pl.ANY)
CONTRACT_ROWS = (((0,), (0,)), ((), ()))
CONTRACT_COLS = (((1,), (1,)), ((), ()))
MIB = 1 << 20


def coords(device):
    y = device % Y
    x = device // Y % X
    zl = device // (Y * X) % ZL
    core = device // (Y * X * ZL) % CORE
    zh = device // (Y * X * ZL * CORE)
    return zh, core, zl, x, y


def shift(value, zh=0, core=0, zl=0, x=0, y=0):
    pairs = []
    for device in range(DEVICES):
        a, b, c, d, e = coords(device)
        a, b, c, d, e = (a + zh) % ZH, (b + core) % CORE, (c + zl) % ZL, (d + x) % X, (e + y) % Y
        pairs.append((device, (((a * CORE + b) * ZL + c) * X + d) * Y + e))
    return lax.ppermute(value, AXES, pairs)


def meet(value, **axis):
    ((name, bit),) = axis.items()
    at = ("zh", "core", "zl", "x", "y").index(name)
    pairs = []
    for device in range(DEVICES):
        place = list(coords(device))
        place[at] ^= bit
        a, b, c, d, e = place
        pairs.append((device, (((a * CORE + b) * ZL + c) * X + d) * Y + e))
    return lax.ppermute(value, AXES, pairs)


def others(axis):
    return (2, 1, 3)


def call(kernel, outs, args, specs, scratch=(), flops=0, own=0):
    size = sum(math.prod(o.shape) * o.dtype.itemsize for o in outs)
    size += sum(math.prod(a.shape) * a.dtype.itemsize for a in args)
    return pl.pallas_call(
        kernel,
        out_shape=tuple(outs),
        in_specs=list(specs),
        out_specs=(VMEM,) * len(outs),
        scratch_shapes=list(scratch),
        compiler_params=pltpu.CompilerParams(vmem_limit_bytes=size + own + 3 * MIB),
        cost_estimate=pl.CostEstimate(flops=flops, bytes_accessed=size, transcendentals=0),
    )(*args)


def shaped(shape, dtype):
    return jax.ShapeDtypeStruct(shape, dtype)


def row_weights_kernel(count, place, vals, feat, weights, vals_out, feat_out):
    feat_out[...] = feat[...]

    def keep(i, carry):
        for u in range(GROUP):
            vals_out[i * GROUP + u] = vals[i * GROUP + u]
        return carry

    lax.fori_loop(0, vals.shape[0] // GROUP, keep, 0)
    weights[...] = jnp.zeros_like(weights)
    ones = jnp.ones((8, 128), BF)

    def step(i, carry):
        slots = [i * GROUP + u for u in range(GROUP)]
        sums = [
            lax.dot_general(ones, vals[s], CONTRACT_COLS, preferred_element_type=F32) for s in slots
        ]
        for s, term in zip(slots, sums):
            weights[place[s]] += term
        return carry

    lax.fori_loop(0, (count[0] + GROUP - 1) // GROUP, step, 0)


def row_weights(count, place, vals, feat):
    return call(
        row_weights_kernel,
        [shaped((33, 8, 128), F32), shaped(vals.shape, BF), shaped(feat.shape, BF)],
        (count, place, vals, feat),
        [SMEM, SMEM, VMEM, VMEM],
    )


def turn_kernel(vals, turned):
    def step(i, carry):
        for u in range(GROUP):
            turned[i * GROUP + u] = vals[i * GROUP + u].T
        return carry

    lax.fori_loop(0, vals.shape[0] // GROUP, step, 0)


def turn(vals):
    return call(turn_kernel, [shaped(vals.shape, BF)], (vals,), [VMEM], flops=6 * 10**9)[0]


GROUP = 4
TURN = 16
BACKWARD_COST = 20 * 10**9
PAIR_COST = 5 * 10**9
TOTAL_COST = 5 * 10**9
PAD = 16


def put_weights(out, rows, value):
    count = value.shape[0]
    if out.dtype == F32:
        out[rows : rows + count, :128] = value
        return
    out[rows:, :] = jnp.zeros((PAD, out.shape[1]), out.dtype)
    lead = value.astype(BF)
    trail = (value - lead.astype(F32)).astype(BF)
    both = jnp.concatenate([lead.astype(F32), trail.astype(F32)], axis=1)
    both = jnp.concatenate([both, jnp.zeros((PAD - count, 256), F32)], axis=0)
    out[rows:, :256] = both.astype(BF)


def get_weights(ref, rows, count):
    got = ref[rows : rows + PAD, :256].astype(F32)[:count]
    if ref.dtype == F32:
        return got[:, :128]
    return got[:, :128] + got[:, 128:]


def forward_kernel(count, place_a, place_b, source, vals, weights, *refs):
    pieces, (total_a, low_a, high_a, total_b, low_b, high_b), (panel, sems) = (
        refs[:8],
        refs[8:14],
        refs[14:],
    )
    copies = [
        pltpu.make_async_copy(piece, panel.at[k], sems.at[k]) for k, piece in enumerate(pieces)
    ]
    for copy in copies:
        copy.start()

    def clear(k, carry):
        total_a[k] = jnp.zeros((128, 256), F32)
        total_b[k] = jnp.zeros((128, 256), F32)
        return carry

    lax.fori_loop(0, 33, clear, 0)
    for copy in copies:
        copy.wait()

    def step(i, carry):
        for u in range(TURN):
            s = i * TURN + u
            term = jnp.dot(vals[s], panel[source[s]], preferred_element_type=F32)
            total_a[place_a[s]] += term[:, :256]
            total_b[place_b[s]] += term[:, 256:]
        return carry

    lax.fori_loop(0, (count[0] + TURN - 1) // TURN, step, 0)

    def finish(k, carry):
        rows = pl.ds(pl.multiple_of(k * 128, 128), 128)
        low_a[rows, :] = total_a[16 + k].astype(BF)
        high_a[rows, :] = total_a[20 + k].astype(BF)
        low_b[rows, :] = total_b[16 + k].astype(BF)
        high_b[rows, :] = total_b[20 + k].astype(BF)
        return carry

    lax.fori_loop(0, 4, finish, 0)
    put_weights(low_a, 512, rows_of(weights, 16, 4))
    put_weights(high_a, 512, rows_of(weights, 20, 4))


def rows_of(weights, begin, count):
    return jnp.concatenate([weights[begin + k, 0:1, :] for k in range(count)], axis=0)


def forward(count, place_a, place_b, source, vals, weights, pieces):
    full = shaped((33, 128, 256), F32)
    cut = shaped((512 + PAD, 256), BF)
    plain = shaped((512, 256), BF)
    return call(
        forward_kernel,
        [full, cut, cut, full, plain, plain],
        (count, place_a, place_b, source, vals, weights, *pieces),
        [SMEM] * 4 + [VMEM] * 2 + [ANY] * 8,
        [pltpu.VMEM((8, 128, 512), BF), pltpu.SemaphoreType.DMA((8,))],
        flops=2 * 48 * 128 * 128 * 512,
        own=4 * MIB,
    )


def pass_kernel(carries, total, weights, low, high, ahead_out, behind_out):
    def first(k, carry):
        rows = pl.ds(pl.multiple_of(k * 128, 128), 128)
        later = pl.ds(pl.multiple_of(512 + k * 128, 128), 128)
        ahead_out[rows, :] = (total[8 + k] + low[rows, :].astype(F32)).astype(BF)
        ahead_out[later, :] = total[12 + k].astype(BF)
        behind_out[rows, :] = total[24 + k].astype(BF)
        behind_out[later, :] = (total[28 + k] + high[rows, :].astype(F32)).astype(BF)
        return carry

    lax.fori_loop(0, 4, first, 0)
    if carries:
        none = jnp.zeros((4, 128), F32)
        low_weight = jnp.concatenate([get_weights(low, 512, 4), none], axis=0)
        high_weight = jnp.concatenate([none, get_weights(high, 512, 4)], axis=0)
        put_weights(ahead_out, 1024, rows_of(weights, 8, 8) + low_weight)
        put_weights(behind_out, 1024, rows_of(weights, 24, 8) + high_weight)


def pass_on(carries, total, weights, low, high):
    out = shaped((1024 + (PAD if carries else 0), 256), BF)
    return call(
        functools.partial(pass_kernel, carries),
        [out, out],
        (total, weights, low, high),
        [VMEM] * 4,
    )


def merge_kernel(carries, own, weights, a, b, *outs):
    for part, out in enumerate(outs):
        for k in range(2):
            rows = slice(256 * part + 128 * k, 256 * part + 128 * k + 128)
            total = own[2 * part + k] + a[rows].astype(F32) + b[rows].astype(F32)
            out[128 * k : 128 * k + 128] = total.astype(out.dtype)
    if carries:
        weight = rows_of(weights, 0, 8) + get_weights(a, 1024, 8) + get_weights(b, 1024, 8)
        for part, out in enumerate(outs):
            put_weights(out, 256, weight[2 * part : 2 * part + 2])


def merge(carries, own, weights, a, b):
    rows = 256 + (PAD if carries else 0)
    return call(
        functools.partial(merge_kernel, carries),
        [shaped((rows, 256), F32)] + [shaped((rows, 256), BF)] * 3,
        (own, weights, a, b),
        [VMEM] * 4,
    )


def join_kernel(*refs):
    parts_a, parts_b, give = refs[:4], refs[4:8], refs[8]
    for at, parts in ((0, parts_a), (256, parts_b)):
        total = parts[0][:256]
        for part in parts[1:]:
            total += part[:256].astype(F32)
        give[:256, at : at + 256] = total.astype(BF)
    put_weights(give, 256, sum(get_weights(ref, 256, 2) for ref in parts_a))


def join(parts_a, parts_b):
    return call(
        join_kernel,
        [shaped((256 + PAD, 512), BF)],
        (*parts_a, *parts_b),
        [VMEM] * 8,
    )[0]


def node_kernel(
    place, given, got, feat, self_pre, cot, w_neigh, layer_out, mean_out, grad_out, back_a, back_b, send
):
    @pl.when(place[1] != 0)
    def _():
        send[:256, :] = feat[...]

    def spread(row):
        wide = jnp.broadcast_to(1.0 / row, (128, 128)).T
        return jnp.concatenate([wide] * 4, axis=1)

    weight, came = get_weights(given, 256, 2), get_weights(got, 256, 2)
    inverse = [spread(1.0 + (weight[k : k + 1, :] + came[1 - k : 2 - k, :])) for k in range(2)]
    inverse = jnp.concatenate(inverse, axis=0)
    other = jnp.concatenate([got[128:256], got[0:128]], axis=0)
    mean = ((given[0:256].astype(F32) + other.astype(F32)) * inverse).astype(BF)
    pre_act = self_pre[...] + jnp.dot(mean, w_neigh[...], preferred_element_type=F32)
    sigmoid_val = jax.nn.sigmoid(pre_act)
    grad = cot[...].astype(F32) * sigmoid_val * (1.0 + pre_act * (1.0 - sigmoid_val))
    grad = grad.astype(BF)
    back_mean = lax.dot_general(grad, w_neigh[...], CONTRACT_COLS, preferred_element_type=F32)
    scaled = (back_mean * inverse).astype(BF)
    back_a[...] = scaled[:, :256]
    back_b[...] = scaled[:, 256:]
    mean_out[...] = mean
    grad_out[...] = grad
    send[256:, :] = grad
    layer_out[...] = (pre_act[:128] * sigmoid_val[:128]).astype(BF)

    @pl.when(place[1] == 0)
    def _():
        send[:256, :] = mean


def node(place, given, got, feat, self_pre, cot, w_neigh):
    wide = shaped((256, 512), BF)
    half = shaped((256, 256), BF)
    return call(
        node_kernel,
        [shaped((128, 512), BF), wide, wide, half, half, shaped((512, 512), BF)],
        (place, given, got, feat, self_pre, cot, w_neigh),
        [SMEM] + [VMEM] * 6,
        flops=8 * 128 * 512 * 512,
    )


def backward_kernel(count, from_a, from_b, place, vals, *refs):
    parts_a, parts_b, outs = refs[:5], refs[5:10], refs[10:12]
    panel_a, panel_b, total, sems = refs[12:]
    copies = []
    begin = 0
    for k, (part_a, part_b) in enumerate(zip(parts_a, parts_b)):
        rows = pl.ds(begin, part_a.shape[0])
        begin += part_a.shape[0]
        copies.append(pltpu.make_async_copy(part_a, panel_a.at[rows], sems.at[k]))
        copies.append(pltpu.make_async_copy(part_b, panel_b.at[rows], sems.at[5 + k]))
    for copy in copies:
        copy.start()

    def clear(k, carry):
        total[k] = jnp.zeros((128, 512), F32)
        return carry

    lax.fori_loop(0, 9, clear, 0)
    for copy in copies:
        copy.wait()

    def step(i, carry):
        for u in range(TURN):
            s = i * TURN + u
            block = vals[s]
            rows_a = pl.ds(pl.multiple_of(from_a[s] * 128, 128), 128)
            rows_b = pl.ds(pl.multiple_of(from_b[s] * 128, 128), 128)
            first = jnp.dot(block, panel_a[rows_a, :], preferred_element_type=F32)
            second = jnp.dot(block, panel_b[rows_b, :], preferred_element_type=F32)
            total[place[s], :, :256] += first
            total[place[s], :, 256:] += second
        return carry

    lax.fori_loop(0, (count[0] + TURN - 1) // TURN, step, 0)

    def finish(k, carry):
        for part, out in enumerate(outs):
            out[k] = total[part * 4 + k].astype(out.dtype)
        return carry

    lax.fori_loop(0, 4, finish, 0)


def backward(count, from_a, from_b, place, turned, parts_a, parts_b):
    return call(
        backward_kernel,
        [shaped((4, 128, 512), F32), shaped((4, 128, 512), BF)],
        (count, from_a, from_b, place, turned, *parts_a, *parts_b),
        [SMEM] * 4 + [VMEM] + [ANY] * 10,
        [
            pltpu.VMEM((4096, 256), BF),
            pltpu.VMEM((4096, 256), BF),
            pltpu.VMEM((9, 128, 512), F32),
            pltpu.SemaphoreType.DMA((10,)),
        ],
        flops=BACKWARD_COST,
        own=4 * MIB,
    )


def pair_kernel(own, got, *outs):
    for k, out in enumerate(outs):
        out[...] = (own[k] + got[k].astype(F32)).astype(out.dtype)


def pair(own, got):
    piece = own.shape[1:]
    return call(
        pair_kernel,
        [shaped(piece, F32)] + [shaped(piece, BF)] * 3,
        (own, got),
        [VMEM] * 2,
        flops=PAIR_COST,
    )


def total_kernel(product, own, a, b, c, out):
    total = own[...] + a[...].astype(F32) + b[...].astype(F32) + c[...].astype(F32)
    out[...] = product[...] + total


def total(product, own, got):
    return call(
        total_kernel,
        [shaped((128, 512), F32)],
        (product, own, *got),
        [VMEM] * 5,
        flops=TOTAL_COST,
    )[0]


BIAS_ROWS = 16
CHUNK = 128 + BIAS_ROWS


def weights_kernel(place, feat, mean, grad, got, keep_out, give_out):
    nodes = (slice(0, 128), slice(128, 256))
    came = tuple(slice(n.start + 256, n.stop + 256) for n in nodes)
    bias = [jnp.sum(grad[n].astype(F32), axis=0, keepdims=True) for n in nodes]
    bias += [jnp.sum(got[n].astype(F32), axis=0, keepdims=True) for n in came]
    bias = (bias[0] + bias[1]) + (bias[2] + bias[3])
    bias = jnp.broadcast_to(bias, (BIAS_ROWS, 512))

    def emit(lhs):
        for m in range(4):
            begin = pl.multiple_of((place[0] ^ m) * 128, 128)
            columns = pl.ds(begin, 128)
            mine = [
                lax.dot_general(
                    lhs[n, columns], grad[n], CONTRACT_ROWS, preferred_element_type=F32
                )
                for n in nodes
            ]
            theirs = [
                lax.dot_general(got[n, columns], got[g], CONTRACT_ROWS, preferred_element_type=F32)
                for n, g in zip(nodes, came)
            ]
            out = keep_out if m < 2 else give_out
            out[m % 2, :128, :] = ((mine[0] + mine[1]) + (theirs[0] + theirs[1])).astype(out.dtype)
            out[m % 2, 128:, :] = bias.astype(out.dtype)

    @pl.when(place[1] == 0)
    def _():
        emit(feat)

    @pl.when(place[1] != 0)
    def _():
        emit(mean)


def weights(place, feat, mean, grad, got):
    piece = (2, CHUNK, 512)
    return call(
        weights_kernel,
        [shaped(piece, F32), shaped(piece, BF)],
        (place, feat, mean, grad, got),
        [SMEM] + [VMEM] * 4,
        flops=4 * 128 * 512 * 512,
    )


def halve_kernel(own, got, keep, give):
    half = keep.shape[0]
    for k in range(half):
        keep[k] = own[k] + got[k].astype(F32)
        give[k] = (own[half + k] + got[half + k].astype(F32)).astype(BF)


def halve(own, got):
    piece = (own.shape[0] // 2,) + own.shape[1:]
    return call(halve_kernel, [shaped(piece, F32), shaped(piece, BF)], (own, got), [VMEM] * 2)


def arrange_kernel(own, place, blocks, *refs):
    (self_out, neigh_out), (full, sem) = refs[-4:-2], refs[-2:]
    for m in range(4):
        rows = pl.ds(pl.multiple_of((place[0] ^ m) * 128, 128), 128)
        full[rows, :] = blocks[128 * m : 128 * m + 128].astype(F32)

    @pl.when(place[1] == (0 if own else 1))
    def _():
        copy = pltpu.make_async_copy(full, self_out, sem)
        copy.start()
        copy.wait()

    @pl.when(place[1] == (1 if own else 0))
    def _():
        copy = pltpu.make_async_copy(full, neigh_out, sem)
        copy.start()
        copy.wait()


def arrange(place, blocks, before=()):
    out = shaped((512, 512), F32)
    own = not before
    return pl.pallas_call(
        functools.partial(arrange_kernel, own),
        out_shape=(out, out),
        in_specs=[SMEM, VMEM] + [ANY] * len(before),
        out_specs=(ANY, ANY),
        scratch_shapes=[pltpu.VMEM((512, 512), F32), pltpu.SemaphoreType.DMA],
        input_output_aliases={} if own else {2: 0, 3: 1},
        compiler_params=pltpu.CompilerParams(vmem_limit_bytes=8 * MIB),
        cost_estimate=pl.CostEstimate(flops=0, bytes_accessed=3 * MIB, transcendentals=0),
    )(place, blocks, *before)


def ring_sum(value, **axis):
    (name,) = axis
    sent = value.astype(BF)
    got = {k: shift(sent, **{name: k}).astype(F32) for k in others(name)}
    return (sent.astype(F32) + got[2]) + (got[1] + got[3])


def meet_sum(value, **axis):
    sent = value.astype(BF)
    return sent.astype(F32) + meet(sent, **axis).astype(F32)


def local(
    features, cotangent, w_self, w_neigh, out_bias, block_vals, block_rows, block_cols, block_count
):
    device = lax.axis_index("row") * 32 + lax.axis_index("col")
    my_zh, my_core, my_zl, my_x, my_y = coords(device)
    slots = block_vals.shape[0]
    live = jnp.arange(slots, dtype=jnp.int32) < block_count[0]
    rel_z = (block_rows // 16 - my_zl) % ZL
    rel_x = (block_rows // 4 % 4 - my_x) % X
    rel_y = (block_rows % 4 - my_y) % Y
    rows_a = rel_x * 8 + rel_y * 2 + rel_z
    rows_b = rel_y * 8 + rel_x * 2 + rel_z
    place_a = jnp.where(live, rows_a, 32)
    place_b = jnp.where(live, rows_b, 32)
    rel_h = (block_cols // 2 - my_zh) % ZH
    rel_c = (block_cols % 2 - my_core) % CORE
    source = rel_h * 2 + rel_c
    back_place = jnp.where(live, rel_c * 4 + rel_h, 8)

    place = jnp.stack([my_x, my_core]).astype(jnp.int32)

    ahead = {k: shift(features, zh=-k) for k in others("zh")}
    weight, near_vals, ahead[0] = row_weights(block_count, place_a, block_vals, features)
    ahead[1], weight = lax.optimization_barrier((ahead[1], weight))
    pieces = []
    for k in range(4):
        pieces += [ahead[k], shift(ahead[k] if k else features, core=1)]

    total_a, low_a, high_a, total_b, low_b, high_b = forward(
        block_count, place_a, place_b, source, near_vals, weight, pieces
    )
    low_a, high_a = shift(low_a, x=1), shift(high_a, x=-1)
    low_b, high_b = shift(low_b, y=1), shift(high_b, y=-1)
    ahead_a, behind_a = pass_on(True, total_a, weight, low_a, high_a)
    ahead_b, behind_b = pass_on(False, total_b, weight, low_b, high_b)
    got_a = [shift(ahead_a, x=1), shift(behind_a, x=-1)]
    got_b = [shift(ahead_b, y=1), shift(behind_b, y=-1)]

    later, _ = lax.optimization_barrier(((features, cotangent, block_vals), ahead_a))
    feat_late, cot_late, vals_late = later
    late = shift(jnp.concatenate([feat_late, cot_late]), zl=1)
    both_feat = jnp.concatenate([feat_late, late[:128]])
    both_cot = jnp.concatenate([cot_late, late[128:]])
    self_pre = jnp.dot(both_feat, w_self, preferred_element_type=F32) + out_bias
    turned = turn(vals_late)
    (got_a, got_b), self_pre, both_cot, turned = lax.optimization_barrier(
        ((got_a, got_b), self_pre, both_cot, turned)
    )

    parts_a = merge(True, total_a, weight, *got_a)
    got_a = [shift(parts_a[k], y=k) for k in others("y")]
    parts_b = merge(False, total_b, weight, *got_b)
    got_b = [shift(parts_b[k], x=k) for k in others("x")]
    given = join([parts_a[0], *got_a], [parts_b[0], *got_b])
    layer_out, mean_agg, grad_pre, back_a, back_b, send = node(
        place, given, shift(given, zl=1), both_feat, self_pre, both_cot, w_neigh
    )

    near_a, near_b = {0: back_a}, {0: back_b}
    for k in others("y"):
        near_a[k] = shift(back_a, y=-k)
        near_b[k] = shift(back_b, x=-k)
    own_a = jnp.concatenate([near_a[k] for k in range(4)])
    own_b = jnp.concatenate([near_b[k] for k in range(4)])

    got = shift(send, core=1)
    keep_part, give_part = weights(place, both_feat, mean_agg, grad_pre, got)
    came, own_b = lax.optimization_barrier((meet(give_part, x=2), own_b))
    keep_part, give_part = halve(keep_part, came)
    next_a, last_a = shift(own_a, x=-1), shift(own_a, x=1)
    next_b, last_b = shift(own_b, y=-1), shift(own_b, y=1)
    low_a, high_a = shift(last_a[:512], x=1), shift(next_a[512:], x=-1)
    low_b, high_b = shift(last_b[:512], y=1), shift(next_b[512:], y=-1)
    chunk = keep_part[0] + meet(give_part[0], x=1).astype(F32)
    chunk = meet_sum(chunk, zh=1)
    chunk = meet_sum(chunk, zh=2)

    grad_self = lax.dot_general(grad_pre[:128], w_self, CONTRACT_COLS, preferred_element_type=F32)
    own, give = backward(
        block_count,
        rows_a,
        rows_b,
        back_place,
        turned,
        [own_a, next_a, low_a, high_a, last_a],
        [own_b, next_b, low_b, high_b, last_b],
    )
    parts = pair(own, shift(give, core=1))
    chunk = ring_sum(chunk, y=1)
    scale = 1.0 / math.sqrt(128 * DEVICES)
    bias_grad = chunk[128] * scale
    block = (chunk[:128] * scale).astype(BF)
    block, parts = lax.optimization_barrier((block, parts))
    block = jnp.concatenate([block] + [meet(block, x=m) for m in (1, 2, 3)])
    feature_grad = total(grad_self, parts[0], [shift(parts[k], zh=k) for k in others("zh")])
    self_grad, neigh_grad = arrange(place, shift(block, core=1), arrange(place, block))
    return layer_out, feature_grad, self_grad, neigh_grad, bias_grad


def solution(mesh):
    return jax.shard_map(
        local,
        mesh=mesh,
        in_specs=(
            P(("row", "col"), None),
            P(("row", "col"), None),
            P(),
            P(),
            P(),
            P(("row", "col"), None, None),
            P(("row", "col")),
            P(("row", "col")),
            P(("row", "col")),
        ),
        out_specs=(P(("row", "col"), None), P(("row", "col"), None), P(), P(), P()),
        check_vma=False,
    )
```

```python
import functools
import math

import jax
import jax.numpy as jnp
from jax import lax
from jax.experimental import pallas as pl
from jax.experimental.pallas import tpu as pltpu
from jax.sharding import PartitionSpec as P

BF = jnp.bfloat16
F32 = jnp.float32
AXES = ("row", "col")
ZH, CORE, ZL, X, Y = 4, 2, 2, 4, 4
DEVICES = ZH * CORE * ZL * X * Y
VMEM = pl.BlockSpec(memory_space=pltpu.VMEM)
SMEM = pl.BlockSpec(memory_space=pltpu.SMEM)
ANY = pl.BlockSpec(memory_space=pl.ANY)
CONTRACT_ROWS = (((0,), (0,)), ((), ()))
CONTRACT_COLS = (((1,), (1,)), ((), ()))
MIB = 1 << 20


def coords(device):
    y = device % Y
    x = device // Y % X
    zl = device // (Y * X) % ZL
    core = device // (Y * X * ZL) % CORE
    zh = device // (Y * X * ZL * CORE)
    return zh, core, zl, x, y


def shift(value, zh=0, core=0, zl=0, x=0, y=0):
    pairs = []
    for device in range(DEVICES):
        a, b, c, d, e = coords(device)
        a, b, c, d, e = (a + zh) % ZH, (b + core) % CORE, (c + zl) % ZL, (d + x) % X, (e + y) % Y
        pairs.append((device, (((a * CORE + b) * ZL + c) * X + d) * Y + e))
    return lax.ppermute(value, AXES, pairs)


def meet(value, **axis):
    ((name, bit),) = axis.items()
    at = ("zh", "core", "zl", "x", "y").index(name)
    pairs = []
    for device in range(DEVICES):
        place = list(coords(device))
        place[at] ^= bit
        a, b, c, d, e = place
        pairs.append((device, (((a * CORE + b) * ZL + c) * X + d) * Y + e))
    return lax.ppermute(value, AXES, pairs)


def others(axis):
    return (2, 1, 3)


def call(kernel, outs, args, specs, scratch=(), flops=0, own=0):
    size = sum(math.prod(o.shape) * o.dtype.itemsize for o in outs)
    size += sum(math.prod(a.shape) * a.dtype.itemsize for a in args)
    return pl.pallas_call(
        kernel,
        out_shape=tuple(outs),
        in_specs=list(specs),
        out_specs=(VMEM,) * len(outs),
        scratch_shapes=list(scratch),
        compiler_params=pltpu.CompilerParams(vmem_limit_bytes=size + own + 3 * MIB),
        cost_estimate=pl.CostEstimate(flops=flops, bytes_accessed=size, transcendentals=0),
    )(*args)


def shaped(shape, dtype):
    return jax.ShapeDtypeStruct(shape, dtype)


def row_weights_kernel(count, place, vals, feat, weights, vals_out, feat_out):
    feat_out[...] = feat[...]

    def keep(i, carry):
        for u in range(GROUP):
            vals_out[i * GROUP + u] = vals[i * GROUP + u]
        return carry

    lax.fori_loop(0, vals.shape[0] // GROUP, keep, 0)
    weights[...] = jnp.zeros_like(weights)
    ones = jnp.ones((8, 128), BF)

    def step(i, carry):
        slots = [i * GROUP + u for u in range(GROUP)]
        sums = [
            lax.dot_general(ones, vals[s], CONTRACT_COLS, preferred_element_type=F32) for s in slots
        ]
        for s, term in zip(slots, sums):
            weights[place[s]] += term
        return carry

    lax.fori_loop(0, (count[0] + GROUP - 1) // GROUP, step, 0)


def row_weights(count, place, vals, feat):
    return call(
        row_weights_kernel,
        [shaped((33, 8, 128), F32), shaped(vals.shape, BF), shaped(feat.shape, BF)],
        (count, place, vals, feat),
        [SMEM, SMEM, VMEM, VMEM],
    )


def turn_kernel(vals, turned):
    def step(i, carry):
        for u in range(GROUP):
            turned[i * GROUP + u] = vals[i * GROUP + u].T
        return carry

    lax.fori_loop(0, vals.shape[0] // GROUP, step, 0)


def turn(vals):
    return call(turn_kernel, [shaped(vals.shape, BF)], (vals,), [VMEM], flops=6 * 10**9)[0]


GROUP = 4
TURN = 16
BACKWARD_COST = 20 * 10**9
PAIR_COST = 5 * 10**9
TOTAL_COST = 5 * 10**9
PAD = 16


def put_weights(out, rows, value):
    count = value.shape[0]
    if out.dtype == F32:
        out[rows : rows + count, :128] = value
        return
    out[rows:, :] = jnp.zeros((PAD, out.shape[1]), out.dtype)
    lead = value.astype(BF)
    trail = (value - lead.astype(F32)).astype(BF)
    both = jnp.concatenate([lead.astype(F32), trail.astype(F32)], axis=1)
    both = jnp.concatenate([both, jnp.zeros((PAD - count, 256), F32)], axis=0)
    out[rows:, :256] = both.astype(BF)


def get_weights(ref, rows, count):
    got = ref[rows : rows + PAD, :256].astype(F32)[:count]
    if ref.dtype == F32:
        return got[:, :128]
    return got[:, :128] + got[:, 128:]


def forward_kernel(count, place_a, place_b, source, vals, weights, *refs):
    pieces, (total_a, low_a, high_a, total_b, low_b, high_b), (panel, sems) = (
        refs[:8],
        refs[8:14],
        refs[14:],
    )
    copies = [
        pltpu.make_async_copy(piece, panel.at[k], sems.at[k]) for k, piece in enumerate(pieces)
    ]
    for copy in copies:
        copy.start()

    def clear(k, carry):
        total_a[k] = jnp.zeros((128, 256), F32)
        total_b[k] = jnp.zeros((128, 256), F32)
        return carry

    lax.fori_loop(0, 33, clear, 0)
    for copy in copies:
        copy.wait()

    def step(i, carry):
        for u in range(TURN):
            s = i * TURN + u
            term = jnp.dot(vals[s], panel[source[s]], preferred_element_type=F32)
            total_a[place_a[s]] += term[:, :256]
            total_b[place_b[s]] += term[:, 256:]
        return carry

    lax.fori_loop(0, (count[0] + TURN - 1) // TURN, step, 0)

    def finish(k, carry):
        rows = pl.ds(pl.multiple_of(k * 128, 128), 128)
        low_a[rows, :] = total_a[16 + k].astype(BF)
        high_a[rows, :] = total_a[20 + k].astype(BF)
        low_b[rows, :] = total_b[16 + k].astype(BF)
        high_b[rows, :] = total_b[20 + k].astype(BF)
        return carry

    lax.fori_loop(0, 4, finish, 0)
    put_weights(low_a, 512, rows_of(weights, 16, 4))
    put_weights(high_a, 512, rows_of(weights, 20, 4))


def rows_of(weights, begin, count):
    return jnp.concatenate([weights[begin + k, 0:1, :] for k in range(count)], axis=0)


def forward(count, place_a, place_b, source, vals, weights, pieces):
    full = shaped((33, 128, 256), F32)
    cut = shaped((512 + PAD, 256), BF)
    plain = shaped((512, 256), BF)
    return call(
        forward_kernel,
        [full, cut, cut, full, plain, plain],
        (count, place_a, place_b, source, vals, weights, *pieces),
        [SMEM] * 4 + [VMEM] * 2 + [ANY] * 8,
        [pltpu.VMEM((8, 128, 512), BF), pltpu.SemaphoreType.DMA((8,))],
        flops=2 * 48 * 128 * 128 * 512,
        own=4 * MIB,
    )


def pass_kernel(carries, total, weights, low, high, ahead_out, behind_out):
    def first(k, carry):
        rows = pl.ds(pl.multiple_of(k * 128, 128), 128)
        later = pl.ds(pl.multiple_of(512 + k * 128, 128), 128)
        ahead_out[rows, :] = (total[8 + k] + low[rows, :].astype(F32)).astype(BF)
        ahead_out[later, :] = total[12 + k].astype(BF)
        behind_out[rows, :] = total[24 + k].astype(BF)
        behind_out[later, :] = (total[28 + k] + high[rows, :].astype(F32)).astype(BF)
        return carry

    lax.fori_loop(0, 4, first, 0)
    if carries:
        none = jnp.zeros((4, 128), F32)
        low_weight = jnp.concatenate([get_weights(low, 512, 4), none], axis=0)
        high_weight = jnp.concatenate([none, get_weights(high, 512, 4)], axis=0)
        put_weights(ahead_out, 1024, rows_of(weights, 8, 8) + low_weight)
        put_weights(behind_out, 1024, rows_of(weights, 24, 8) + high_weight)


def pass_on(carries, total, weights, low, high):
    out = shaped((1024 + (PAD if carries else 0), 256), BF)
    return call(
        functools.partial(pass_kernel, carries),
        [out, out],
        (total, weights, low, high),
        [VMEM] * 4,
    )


def merge_kernel(carries, own, weights, a, b, *outs):
    for part, out in enumerate(outs):
        for k in range(2):
            rows = slice(256 * part + 128 * k, 256 * part + 128 * k + 128)
            total = own[2 * part + k] + a[rows].astype(F32) + b[rows].astype(F32)
            out[128 * k : 128 * k + 128] = total.astype(out.dtype)
    if carries:
        weight = rows_of(weights, 0, 8) + get_weights(a, 1024, 8) + get_weights(b, 1024, 8)
        for part, out in enumerate(outs):
            put_weights(out, 256, weight[2 * part : 2 * part + 2])


def merge(carries, own, weights, a, b):
    rows = 256 + (PAD if carries else 0)
    return call(
        functools.partial(merge_kernel, carries),
        [shaped((rows, 256), F32)] + [shaped((rows, 256), BF)] * 3,
        (own, weights, a, b),
        [VMEM] * 4,
    )


def join_kernel(*refs):
    parts_a, parts_b, give = refs[:4], refs[4:8], refs[8]
    for at, parts in ((0, parts_a), (256, parts_b)):
        total = parts[0][:256]
        for part in parts[1:]:
            total += part[:256].astype(F32)
        give[:256, at : at + 256] = total.astype(BF)
    put_weights(give, 256, sum(get_weights(ref, 256, 2) for ref in parts_a))


def join(parts_a, parts_b):
    return call(
        join_kernel,
        [shaped((256 + PAD, 512), BF)],
        (*parts_a, *parts_b),
        [VMEM] * 8,
    )[0]


def node_kernel(
    place, given, got, feat, self_pre, cot, w_neigh, layer_out, mean_out, grad_out, back_a, back_b, send
):
    @pl.when(place[1] != 0)
    def _():
        send[:256, :] = feat[...]

    def spread(row):
        wide = jnp.broadcast_to(1.0 / row, (128, 128)).T
        return jnp.concatenate([wide] * 4, axis=1)

    weight, came = get_weights(given, 256, 2), get_weights(got, 256, 2)
    inverse = [spread(1.0 + (weight[k : k + 1, :] + came[1 - k : 2 - k, :])) for k in range(2)]
    inverse = jnp.concatenate(inverse, axis=0)
    other = jnp.concatenate([got[128:256], got[0:128]], axis=0)
    mean = ((given[0:256].astype(F32) + other.astype(F32)) * inverse).astype(BF)
    pre_act = self_pre[...] + jnp.dot(mean, w_neigh[...], preferred_element_type=F32)
    sigmoid_val = jax.nn.sigmoid(pre_act)
    grad = cot[...].astype(F32) * sigmoid_val * (1.0 + pre_act * (1.0 - sigmoid_val))
    grad = grad.astype(BF)
    back_mean = lax.dot_general(grad, w_neigh[...], CONTRACT_COLS, preferred_element_type=F32)
    scaled = (back_mean * inverse).astype(BF)
    back_a[...] = scaled[:, :256]
    back_b[...] = scaled[:, 256:]
    mean_out[...] = mean
    grad_out[...] = grad
    send[256:, :] = grad
    layer_out[...] = (pre_act[:128] * sigmoid_val[:128]).astype(BF)

    @pl.when(place[1] == 0)
    def _():
        send[:256, :] = mean


def node(place, given, got, feat, self_pre, cot, w_neigh):
    wide = shaped((256, 512), BF)
    half = shaped((256, 256), BF)
    return call(
        node_kernel,
        [shaped((128, 512), BF), wide, wide, half, half, shaped((512, 512), BF)],
        (place, given, got, feat, self_pre, cot, w_neigh),
        [SMEM] + [VMEM] * 6,
        flops=8 * 128 * 512 * 512,
    )


def backward_kernel(count, from_a, from_b, place, vals, *refs):
    parts_a, parts_b, outs = refs[:5], refs[5:10], refs[10:12]
    panel_a, panel_b, total, sems = refs[12:]
    copies = []
    begin = 0
    for k, (part_a, part_b) in enumerate(zip(parts_a, parts_b)):
        rows = pl.ds(begin, part_a.shape[0])
        begin += part_a.shape[0]
        copies.append(pltpu.make_async_copy(part_a, panel_a.at[rows], sems.at[k]))
        copies.append(pltpu.make_async_copy(part_b, panel_b.at[rows], sems.at[5 + k]))
    for copy in copies:
        copy.start()

    def clear(k, carry):
        total[k] = jnp.zeros((128, 512), F32)
        return carry

    lax.fori_loop(0, 9, clear, 0)
    for copy in copies:
        copy.wait()

    def step(i, carry):
        for u in range(TURN):
            s = i * TURN + u
            block = vals[s]
            rows_a = pl.ds(pl.multiple_of(from_a[s] * 128, 128), 128)
            rows_b = pl.ds(pl.multiple_of(from_b[s] * 128, 128), 128)
            first = jnp.dot(block, panel_a[rows_a, :], preferred_element_type=F32)
            second = jnp.dot(block, panel_b[rows_b, :], preferred_element_type=F32)
            total[place[s], :, :256] += first
            total[place[s], :, 256:] += second
        return carry

    lax.fori_loop(0, (count[0] + TURN - 1) // TURN, step, 0)

    def finish(k, carry):
        for part, out in enumerate(outs):
            out[k] = total[part * 4 + k].astype(out.dtype)
        return carry

    lax.fori_loop(0, 4, finish, 0)


def backward(count, from_a, from_b, place, turned, parts_a, parts_b):
    return call(
        backward_kernel,
        [shaped((4, 128, 512), F32), shaped((4, 128, 512), BF)],
        (count, from_a, from_b, place, turned, *parts_a, *parts_b),
        [SMEM] * 4 + [VMEM] + [ANY] * 10,
        [
            pltpu.VMEM((4096, 256), BF),
            pltpu.VMEM((4096, 256), BF),
            pltpu.VMEM((9, 128, 512), F32),
            pltpu.SemaphoreType.DMA((10,)),
        ],
        flops=BACKWARD_COST,
        own=4 * MIB,
    )


def pair_kernel(own, got, *outs):
    for k, out in enumerate(outs):
        out[...] = (own[k] + got[k].astype(F32)).astype(out.dtype)


def pair(own, got):
    piece = own.shape[1:]
    return call(
        pair_kernel,
        [shaped(piece, F32)] + [shaped(piece, BF)] * 3,
        (own, got),
        [VMEM] * 2,
        flops=PAIR_COST,
    )


def total_kernel(product, own, a, b, c, out):
    total = own[...] + a[...].astype(F32) + b[...].astype(F32) + c[...].astype(F32)
    out[...] = product[...] + total


def total(product, own, got):
    return call(
        total_kernel,
        [shaped((128, 512), F32)],
        (product, own, *got),
        [VMEM] * 5,
        flops=TOTAL_COST,
    )[0]


BIAS_ROWS = 16
CHUNK = 128 + BIAS_ROWS


def weights_kernel(place, feat, mean, grad, got, keep_out, give_out):
    nodes = (slice(0, 128), slice(128, 256))
    came = tuple(slice(n.start + 256, n.stop + 256) for n in nodes)
    bias = [jnp.sum(grad[n].astype(F32), axis=0, keepdims=True) for n in nodes]
    bias += [jnp.sum(got[n].astype(F32), axis=0, keepdims=True) for n in came]
    bias = (bias[0] + bias[1]) + (bias[2] + bias[3])
    bias = jnp.broadcast_to(bias, (BIAS_ROWS, 512))

    def emit(lhs):
        for m in range(4):
            begin = pl.multiple_of((place[0] ^ m) * 128, 128)
            columns = pl.ds(begin, 128)
            mine = [
                lax.dot_general(
                    lhs[n, columns], grad[n], CONTRACT_ROWS, preferred_element_type=F32
                )
                for n in nodes
            ]
            theirs = [
                lax.dot_general(got[n, columns], got[g], CONTRACT_ROWS, preferred_element_type=F32)
                for n, g in zip(nodes, came)
            ]
            out = keep_out if m < 2 else give_out
            out[m % 2, :128, :] = ((mine[0] + mine[1]) + (theirs[0] + theirs[1])).astype(out.dtype)
            out[m % 2, 128:, :] = bias.astype(out.dtype)

    @pl.when(place[1] == 0)
    def _():
        emit(feat)

    @pl.when(place[1] != 0)
    def _():
        emit(mean)


def weights(place, feat, mean, grad, got):
    piece = (2, CHUNK, 512)
    return call(
        weights_kernel,
        [shaped(piece, F32), shaped(piece, BF)],
        (place, feat, mean, grad, got),
        [SMEM] + [VMEM] * 4,
        flops=4 * 128 * 512 * 512,
    )


def halve_kernel(own, got, keep, give):
    half = keep.shape[0]
    for k in range(half):
        keep[k] = own[k] + got[k].astype(F32)
        give[k] = (own[half + k] + got[half + k].astype(F32)).astype(BF)


def halve(own, got):
    piece = (own.shape[0] // 2,) + own.shape[1:]
    return call(halve_kernel, [shaped(piece, F32), shaped(piece, BF)], (own, got), [VMEM] * 2)


def arrange_kernel(own, place, blocks, *refs):
    (self_out, neigh_out), (full, sem) = refs[-4:-2], refs[-2:]
    for m in range(4):
        rows = pl.ds(pl.multiple_of((place[0] ^ m) * 128, 128), 128)
        full[rows, :] = blocks[128 * m : 128 * m + 128].astype(F32)

    @pl.when(place[1] == (0 if own else 1))
    def _():
        copy = pltpu.make_async_copy(full, self_out, sem)
        copy.start()
        copy.wait()

    @pl.when(place[1] == (1 if own else 0))
    def _():
        copy = pltpu.make_async_copy(full, neigh_out, sem)
        copy.start()
        copy.wait()


def arrange(place, blocks, before=()):
    out = shaped((512, 512), F32)
    own = not before
    return pl.pallas_call(
        functools.partial(arrange_kernel, own),
        out_shape=(out, out),
        in_specs=[SMEM, VMEM] + [ANY] * len(before),
        out_specs=(ANY, ANY),
        scratch_shapes=[pltpu.VMEM((512, 512), F32), pltpu.SemaphoreType.DMA],
        input_output_aliases={} if own else {2: 0, 3: 1},
        compiler_params=pltpu.CompilerParams(vmem_limit_bytes=8 * MIB),
        cost_estimate=pl.CostEstimate(flops=0, bytes_accessed=3 * MIB, transcendentals=0),
    )(place, blocks, *before)


def ring_sum(value, **axis):
    (name,) = axis
    sent = value.astype(BF)
    got = {k: shift(sent, **{name: k}).astype(F32) for k in others(name)}
    return (sent.astype(F32) + got[2]) + (got[1] + got[3])


def meet_sum(value, **axis):
    sent = value.astype(BF)
    return sent.astype(F32) + meet(sent, **axis).astype(F32)


def local(
    features, cotangent, w_self, w_neigh, out_bias, block_vals, block_rows, block_cols, block_count
):
    device = lax.axis_index("row") * 32 + lax.axis_index("col")
    my_zh, my_core, my_zl, my_x, my_y = coords(device)
    slots = block_vals.shape[0]
    live = jnp.arange(slots, dtype=jnp.int32) < block_count[0]
    rel_z = (block_rows // 16 - my_zl) % ZL
    rel_x = (block_rows // 4 % 4 - my_x) % X
    rel_y = (block_rows % 4 - my_y) % Y
    rows_a = rel_x * 8 + rel_y * 2 + rel_z
    rows_b = rel_y * 8 + rel_x * 2 + rel_z
    place_a = jnp.where(live, rows_a, 32)
    place_b = jnp.where(live, rows_b, 32)
    rel_h = (block_cols // 2 - my_zh) % ZH
    rel_c = (block_cols % 2 - my_core) % CORE
    source = rel_h * 2 + rel_c
    back_place = jnp.where(live, rel_c * 4 + rel_h, 8)

    place = jnp.stack([my_x, my_core]).astype(jnp.int32)

    ahead = {k: shift(features, zh=-k) for k in others("zh")}
    weight, near_vals, ahead[0] = row_weights(block_count, place_a, block_vals, features)
    ahead[1], weight = lax.optimization_barrier((ahead[1], weight))
    pieces = []
    for k in range(4):
        pieces += [ahead[k], shift(ahead[k] if k else features, core=1)]

    total_a, low_a, high_a, total_b, low_b, high_b = forward(
        block_count, place_a, place_b, source, near_vals, weight, pieces
    )
    low_a, high_a = shift(low_a, x=1), shift(high_a, x=-1)
    low_b, high_b = shift(low_b, y=1), shift(high_b, y=-1)
    ahead_a, behind_a = pass_on(True, total_a, weight, low_a, high_a)
    ahead_b, behind_b = pass_on(False, total_b, weight, low_b, high_b)
    got_a = [shift(ahead_a, x=1), shift(behind_a, x=-1)]
    got_b = [shift(ahead_b, y=1), shift(behind_b, y=-1)]

    later, _ = lax.optimization_barrier(((features, cotangent, block_vals), ahead_a))
    feat_late, cot_late, vals_late = later
    late = shift(jnp.concatenate([feat_late, cot_late]), zl=1)
    both_feat = jnp.concatenate([feat_late, late[:128]])
    both_cot = jnp.concatenate([cot_late, late[128:]])
    self_pre = jnp.dot(both_feat, w_self, preferred_element_type=F32) + out_bias
    turned = turn(vals_late)
    (got_a, got_b), self_pre, both_cot, turned = lax.optimization_barrier(
        ((got_a, got_b), self_pre, both_cot, turned)
    )

    parts_a = merge(True, total_a, weight, *got_a)
    got_a = [shift(parts_a[k], y=k) for k in others("y")]
    parts_b = merge(False, total_b, weight, *got_b)
    got_b = [shift(parts_b[k], x=k) for k in others("x")]
    given = join([parts_a[0], *got_a], [parts_b[0], *got_b])
    layer_out, mean_agg, grad_pre, back_a, back_b, send = node(
        place, given, shift(given, zl=1), both_feat, self_pre, both_cot, w_neigh
    )

    near_a, near_b = {0: back_a}, {0: back_b}
    for k in others("y"):
        near_a[k] = shift(back_a, y=-k)
        near_b[k] = shift(back_b, x=-k)
    own_a = jnp.concatenate([near_a[k] for k in range(4)])
    own_b = jnp.concatenate([near_b[k] for k in range(4)])

    got = shift(send, core=1)
    keep_part, give_part = weights(place, both_feat, mean_agg, grad_pre, got)
    came, own_b = lax.optimization_barrier((meet(give_part, x=2), own_b))
    keep_part, give_part = halve(keep_part, came)
    give_part, own_a, own_b = lax.optimization_barrier((give_part, own_a, own_b))
    next_a, last_a = shift(own_a, x=-1), shift(own_a, x=1)
    next_b, last_b = shift(own_b, y=-1), shift(own_b, y=1)
    low_a, high_a = shift(last_a[:512], x=1), shift(next_a[512:], x=-1)
    low_b, high_b = shift(last_b[:512], y=1), shift(next_b[512:], y=-1)
    chunk = keep_part[0] + meet(give_part[0], x=1).astype(F32)
    chunk = meet_sum(chunk, zh=1)
    chunk = meet_sum(chunk, zh=2)

    grad_self = lax.dot_general(grad_pre[:128], w_self, CONTRACT_COLS, preferred_element_type=F32)
    own, give = backward(
        block_count,
        rows_a,
        rows_b,
        back_place,
        turned,
        [own_a, next_a, low_a, high_a, last_a],
        [own_b, next_b, low_b, high_b, last_b],
    )
    parts = pair(own, shift(give, core=1))
    chunk = ring_sum(chunk, y=1)
    scale = 1.0 / math.sqrt(128 * DEVICES)
    bias_grad = chunk[128] * scale
    block = (chunk[:128] * scale).astype(BF)
    block, parts = lax.optimization_barrier((block, parts))
    block = jnp.concatenate([block] + [meet(block, x=m) for m in (1, 2, 3)])
    feature_grad = total(grad_self, parts[0], [shift(parts[k], zh=k) for k in others("zh")])
    self_grad, neigh_grad = arrange(place, shift(block, core=1), arrange(place, block))
    return layer_out, feature_grad, self_grad, neigh_grad, bias_grad


def solution(mesh):
    return jax.shard_map(
        local,
        mesh=mesh,
        in_specs=(
            P(("row", "col"), None),
            P(("row", "col"), None),
            P(),
            P(),
            P(),
            P(("row", "col"), None, None),
            P(("row", "col")),
            P(("row", "col")),
            P(("row", "col")),
        ),
        out_specs=(P(("row", "col"), None), P(("row", "col"), None), P(), P(), P()),
        check_vma=False,
    )
```

```python
import functools
import math

import jax
import jax.numpy as jnp
from jax import lax
from jax.experimental import pallas as pl
from jax.experimental.pallas import tpu as pltpu
from jax.sharding import PartitionSpec as P

BF = jnp.bfloat16
F32 = jnp.float32
AXES = ("row", "col")
ZH, CORE, ZL, X, Y = 4, 2, 2, 4, 4
DEVICES = ZH * CORE * ZL * X * Y
VMEM = pl.BlockSpec(memory_space=pltpu.VMEM)
SMEM = pl.BlockSpec(memory_space=pltpu.SMEM)
ANY = pl.BlockSpec(memory_space=pl.ANY)
CONTRACT_ROWS = (((0,), (0,)), ((), ()))
CONTRACT_COLS = (((1,), (1,)), ((), ()))
MIB = 1 << 20


def coords(device):
    y = device % Y
    x = device // Y % X
    zl = device // (Y * X) % ZL
    core = device // (Y * X * ZL) % CORE
    zh = device // (Y * X * ZL * CORE)
    return zh, core, zl, x, y


def shift(value, zh=0, core=0, zl=0, x=0, y=0):
    pairs = []
    for device in range(DEVICES):
        a, b, c, d, e = coords(device)
        a, b, c, d, e = (a + zh) % ZH, (b + core) % CORE, (c + zl) % ZL, (d + x) % X, (e + y) % Y
        pairs.append((device, (((a * CORE + b) * ZL + c) * X + d) * Y + e))
    return lax.ppermute(value, AXES, pairs)


def meet(value, **axis):
    ((name, bit),) = axis.items()
    at = ("zh", "core", "zl", "x", "y").index(name)
    pairs = []
    for device in range(DEVICES):
        place = list(coords(device))
        place[at] ^= bit
        a, b, c, d, e = place
        pairs.append((device, (((a * CORE + b) * ZL + c) * X + d) * Y + e))
    return lax.ppermute(value, AXES, pairs)


def others(axis):
    return (2, 1, 3)


def call(kernel, outs, args, specs, scratch=(), flops=0, own=0):
    size = sum(math.prod(o.shape) * o.dtype.itemsize for o in outs)
    size += sum(math.prod(a.shape) * a.dtype.itemsize for a in args)
    return pl.pallas_call(
        kernel,
        out_shape=tuple(outs),
        in_specs=list(specs),
        out_specs=(VMEM,) * len(outs),
        scratch_shapes=list(scratch),
        compiler_params=pltpu.CompilerParams(vmem_limit_bytes=size + own + 3 * MIB),
        cost_estimate=pl.CostEstimate(flops=flops, bytes_accessed=size, transcendentals=0),
    )(*args)


def shaped(shape, dtype):
    return jax.ShapeDtypeStruct(shape, dtype)


def row_weights_kernel(count, place, vals, feat, weights, vals_out, feat_out):
    feat_out[...] = feat[...]

    def keep(i, carry):
        for u in range(GROUP):
            vals_out[i * GROUP + u] = vals[i * GROUP + u]
        return carry

    lax.fori_loop(0, vals.shape[0] // GROUP, keep, 0)
    weights[...] = jnp.zeros_like(weights)
    ones = jnp.ones((8, 128), BF)

    def step(i, carry):
        slots = [i * GROUP + u for u in range(GROUP)]
        sums = [
            lax.dot_general(ones, vals[s], CONTRACT_COLS, preferred_element_type=F32) for s in slots
        ]
        for s, term in zip(slots, sums):
            weights[place[s]] += term
        return carry

    lax.fori_loop(0, (count[0] + GROUP - 1) // GROUP, step, 0)


def row_weights(count, place, vals, feat):
    return call(
        row_weights_kernel,
        [shaped((33, 8, 128), F32), shaped(vals.shape, BF), shaped(feat.shape, BF)],
        (count, place, vals, feat),
        [SMEM, SMEM, VMEM, VMEM],
    )


def turn_kernel(vals, turned):
    def step(i, carry):
        for u in range(GROUP):
            turned[i * GROUP + u] = vals[i * GROUP + u].T
        return carry

    lax.fori_loop(0, vals.shape[0] // GROUP, step, 0)


def turn(vals):
    return call(turn_kernel, [shaped(vals.shape, BF)], (vals,), [VMEM], flops=6 * 10**9)[0]


GROUP = 4
TURN = 16
BACKWARD_COST = 20 * 10**9
PAIR_COST = 5 * 10**9
TOTAL_COST = 5 * 10**9
PAD = 16


def put_weights(out, rows, value):
    count = value.shape[0]
    if out.dtype == F32:
        out[rows : rows + count, :128] = value
        return
    out[rows:, :] = jnp.zeros((PAD, out.shape[1]), out.dtype)
    lead = value.astype(BF)
    trail = (value - lead.astype(F32)).astype(BF)
    both = jnp.concatenate([lead.astype(F32), trail.astype(F32)], axis=1)
    both = jnp.concatenate([both, jnp.zeros((PAD - count, 256), F32)], axis=0)
    out[rows:, :256] = both.astype(BF)


def get_weights(ref, rows, count):
    got = ref[rows : rows + PAD, :256].astype(F32)[:count]
    if ref.dtype == F32:
        return got[:, :128]
    return got[:, :128] + got[:, 128:]


def forward_kernel(count, place_a, place_b, source, vals, weights, *refs):
    pieces, (total_a, total_b), (panel, sems) = refs[:8], refs[8:10], refs[10:]
    copies = [
        pltpu.make_async_copy(piece, panel.at[k], sems.at[k]) for k, piece in enumerate(pieces)
    ]
    for copy in copies:
        copy.start()

    def clear(k, carry):
        total_a[k] = jnp.zeros((128, 256), F32)
        total_b[k] = jnp.zeros((128, 256), F32)
        return carry

    lax.fori_loop(0, 33, clear, 0)
    for copy in copies:
        copy.wait()

    def step(i, carry):
        for u in range(TURN):
            s = i * TURN + u
            term = jnp.dot(vals[s], panel[source[s]], preferred_element_type=F32)
            total_a[place_a[s]] += term[:, :256]
            total_b[place_b[s]] += term[:, 256:]
        return carry

    lax.fori_loop(0, (count[0] + TURN - 1) // TURN, step, 0)


def opposite_kernel(count, order, place_a, place_b, source, vals, weights, *refs):
    pieces, (low_a, high_a, low_b, high_b) = refs[:8], refs[8:12]
    panel, total_a, total_b, sems = refs[12:]
    copies = [
        pltpu.make_async_copy(piece, panel.at[k], sems.at[k]) for k, piece in enumerate(pieces)
    ]
    for copy in copies:
        copy.start()

    def clear(k, carry):
        total_a[k] = jnp.zeros((128, 256), F32)
        total_b[k] = jnp.zeros((128, 256), F32)
        return carry

    lax.fori_loop(0, 9, clear, 0)
    for copy in copies:
        copy.wait()

    def step(i, carry):
        for u in range(8):
            s = order[i * 8 + u]
            term = jnp.dot(vals[s], panel[source[s]], preferred_element_type=F32)
            total_a[place_a[s]] += term[:, :256]
            total_b[place_b[s]] += term[:, 256:]
        return carry

    lax.fori_loop(0, (count[0] + 7) // 8, step, 0)

    def finish(k, carry):
        rows = pl.ds(pl.multiple_of(k * 128, 128), 128)
        low_a[rows, :] = total_a[k].astype(BF)
        high_a[rows, :] = total_a[4 + k].astype(BF)
        low_b[rows, :] = total_b[k].astype(BF)
        high_b[rows, :] = total_b[4 + k].astype(BF)
        return carry

    lax.fori_loop(0, 4, finish, 0)
    put_weights(low_a, 512, rows_of(weights, 16, 4))
    put_weights(high_a, 512, rows_of(weights, 20, 4))


def opposite(count, order, place_a, place_b, source, vals, weights, pieces):
    cut = shaped((512 + PAD, 256), BF)
    plain = shaped((512, 256), BF)
    return call(
        opposite_kernel,
        [cut, cut, plain, plain],
        (count, order, place_a, place_b, source, vals, weights, *pieces),
        [SMEM] * 5 + [VMEM] * 2 + [ANY] * 8,
        [
            pltpu.VMEM((8, 128, 512), BF),
            pltpu.VMEM((9, 128, 256), F32),
            pltpu.VMEM((9, 128, 256), F32),
            pltpu.SemaphoreType.DMA((8,)),
        ],
        flops=2 * 24 * 128 * 128 * 512,
        own=4 * MIB,
    )


def rows_of(weights, begin, count):
    return jnp.concatenate([weights[begin + k, 0:1, :] for k in range(count)], axis=0)


def forward(count, place_a, place_b, source, vals, weights, pieces):
    full = shaped((33, 128, 256), F32)
    return call(
        forward_kernel,
        [full, full],
        (count, place_a, place_b, source, vals, weights, *pieces),
        [SMEM] * 4 + [VMEM] * 2 + [ANY] * 8,
        [pltpu.VMEM((8, 128, 512), BF), pltpu.SemaphoreType.DMA((8,))],
        flops=2 * 48 * 128 * 128 * 512,
        own=4 * MIB,
    )


def pass_kernel(carries, total, weights, low, high, ahead_out, behind_out):
    def first(k, carry):
        rows = pl.ds(pl.multiple_of(k * 128, 128), 128)
        later = pl.ds(pl.multiple_of(512 + k * 128, 128), 128)
        ahead_out[rows, :] = (total[8 + k] + low[rows, :].astype(F32)).astype(BF)
        ahead_out[later, :] = total[12 + k].astype(BF)
        behind_out[rows, :] = total[24 + k].astype(BF)
        behind_out[later, :] = (total[28 + k] + high[rows, :].astype(F32)).astype(BF)
        return carry

    lax.fori_loop(0, 4, first, 0)
    if carries:
        none = jnp.zeros((4, 128), F32)
        low_weight = jnp.concatenate([get_weights(low, 512, 4), none], axis=0)
        high_weight = jnp.concatenate([none, get_weights(high, 512, 4)], axis=0)
        put_weights(ahead_out, 1024, rows_of(weights, 8, 8) + low_weight)
        put_weights(behind_out, 1024, rows_of(weights, 24, 8) + high_weight)


def pass_on(carries, total, weights, low, high):
    out = shaped((1024 + (PAD if carries else 0), 256), BF)
    return call(
        functools.partial(pass_kernel, carries),
        [out, out],
        (total, weights, low, high),
        [VMEM] * 4,
    )


def merge_kernel(carries, own, weights, a, b, *outs):
    for part, out in enumerate(outs):
        for k in range(2):
            rows = slice(256 * part + 128 * k, 256 * part + 128 * k + 128)
            total = own[2 * part + k] + a[rows].astype(F32) + b[rows].astype(F32)
            out[128 * k : 128 * k + 128] = total.astype(out.dtype)
    if carries:
        weight = rows_of(weights, 0, 8) + get_weights(a, 1024, 8) + get_weights(b, 1024, 8)
        for part, out in enumerate(outs):
            put_weights(out, 256, weight[2 * part : 2 * part + 2])


def merge(carries, own, weights, a, b):
    rows = 256 + (PAD if carries else 0)
    return call(
        functools.partial(merge_kernel, carries),
        [shaped((rows, 256), F32)] + [shaped((rows, 256), BF)] * 3,
        (own, weights, a, b),
        [VMEM] * 4,
    )


def join_kernel(*refs):
    parts_a, parts_b, give = refs[:4], refs[4:8], refs[8]
    for at, parts in ((0, parts_a), (256, parts_b)):
        total = parts[0][:256]
        for part in parts[1:]:
            total += part[:256].astype(F32)
        give[:256, at : at + 256] = total.astype(BF)
    put_weights(give, 256, sum(get_weights(ref, 256, 2) for ref in parts_a))


def join(parts_a, parts_b):
    return call(
        join_kernel,
        [shaped((256 + PAD, 512), BF)],
        (*parts_a, *parts_b),
        [VMEM] * 8,
    )[0]


def node_kernel(
    place, given, got, feat, self_pre, cot, w_neigh, layer_out, mean_out, grad_out, back_a, back_b, send
):
    @pl.when(place[1] != 0)
    def _():
        send[:256, :] = feat[...]

    def spread(row):
        wide = jnp.broadcast_to(1.0 / row, (128, 128)).T
        return jnp.concatenate([wide] * 4, axis=1)

    weight, came = get_weights(given, 256, 2), get_weights(got, 256, 2)
    inverse = [spread(1.0 + (weight[k : k + 1, :] + came[1 - k : 2 - k, :])) for k in range(2)]
    inverse = jnp.concatenate(inverse, axis=0)
    other = jnp.concatenate([got[128:256], got[0:128]], axis=0)
    mean = ((given[0:256].astype(F32) + other.astype(F32)) * inverse).astype(BF)
    pre_act = self_pre[...] + jnp.dot(mean, w_neigh[...], preferred_element_type=F32)
    sigmoid_val = jax.nn.sigmoid(pre_act)
    grad = cot[...].astype(F32) * sigmoid_val * (1.0 + pre_act * (1.0 - sigmoid_val))
    grad = grad.astype(BF)
    back_mean = lax.dot_general(grad, w_neigh[...], CONTRACT_COLS, preferred_element_type=F32)
    scaled = (back_mean * inverse).astype(BF)
    back_a[...] = scaled[:, :256]
    back_b[...] = scaled[:, 256:]
    mean_out[...] = mean
    grad_out[...] = grad
    send[256:, :] = grad
    layer_out[...] = (pre_act[:128] * sigmoid_val[:128]).astype(BF)

    @pl.when(place[1] == 0)
    def _():
        send[:256, :] = mean


def node(place, given, got, feat, self_pre, cot, w_neigh):
    wide = shaped((256, 512), BF)
    half = shaped((256, 256), BF)
    return call(
        node_kernel,
        [shaped((128, 512), BF), wide, wide, half, half, shaped((512, 512), BF)],
        (place, given, got, feat, self_pre, cot, w_neigh),
        [SMEM] + [VMEM] * 6,
        flops=8 * 128 * 512 * 512,
    )


def backward_kernel(count, from_a, from_b, place, vals, *refs):
    parts_a, parts_b, outs = refs[:5], refs[5:10], refs[10:12]
    panel_a, panel_b, total, sems = refs[12:]
    copies = []
    begin = 0
    for k, (part_a, part_b) in enumerate(zip(parts_a, parts_b)):
        rows = pl.ds(begin, part_a.shape[0])
        begin += part_a.shape[0]
        copies.append(pltpu.make_async_copy(part_a, panel_a.at[rows], sems.at[k]))
        copies.append(pltpu.make_async_copy(part_b, panel_b.at[rows], sems.at[5 + k]))
    for copy in copies:
        copy.start()

    def clear(k, carry):
        total[k] = jnp.zeros((128, 512), F32)
        return carry

    lax.fori_loop(0, 9, clear, 0)
    for copy in copies:
        copy.wait()

    def step(i, carry):
        for u in range(TURN):
            s = i * TURN + u
            block = vals[s]
            rows_a = pl.ds(pl.multiple_of(from_a[s] * 128, 128), 128)
            rows_b = pl.ds(pl.multiple_of(from_b[s] * 128, 128), 128)
            first = jnp.dot(block, panel_a[rows_a, :], preferred_element_type=F32)
            second = jnp.dot(block, panel_b[rows_b, :], preferred_element_type=F32)
            total[place[s], :, :256] += first
            total[place[s], :, 256:] += second
        return carry

    lax.fori_loop(0, (count[0] + TURN - 1) // TURN, step, 0)

    def finish(k, carry):
        for part, out in enumerate(outs):
            out[k] = total[part * 4 + k].astype(out.dtype)
        return carry

    lax.fori_loop(0, 4, finish, 0)


def backward(count, from_a, from_b, place, turned, parts_a, parts_b):
    return call(
        backward_kernel,
        [shaped((4, 128, 512), F32), shaped((4, 128, 512), BF)],
        (count, from_a, from_b, place, turned, *parts_a, *parts_b),
        [SMEM] * 4 + [VMEM] + [ANY] * 10,
        [
            pltpu.VMEM((4096, 256), BF),
            pltpu.VMEM((4096, 256), BF),
            pltpu.VMEM((9, 128, 512), F32),
            pltpu.SemaphoreType.DMA((10,)),
        ],
        flops=BACKWARD_COST,
        own=4 * MIB,
    )


def pair_kernel(own, got, *outs):
    for k, out in enumerate(outs):
        out[...] = (own[k] + got[k].astype(F32)).astype(out.dtype)


def pair(own, got):
    piece = own.shape[1:]
    return call(
        pair_kernel,
        [shaped(piece, F32)] + [shaped(piece, BF)] * 3,
        (own, got),
        [VMEM] * 2,
        flops=PAIR_COST,
    )


def total_kernel(product, own, a, b, c, out):
    total = own[...] + a[...].astype(F32) + b[...].astype(F32) + c[...].astype(F32)
    out[...] = product[...] + total


def total(product, own, got):
    return call(
        total_kernel,
        [shaped((128, 512), F32)],
        (product, own, *got),
        [VMEM] * 5,
        flops=TOTAL_COST,
    )[0]


BIAS_ROWS = 16
CHUNK = 128 + BIAS_ROWS


def weights_kernel(place, feat, mean, grad, got, keep_out, give_out):
    nodes = (slice(0, 128), slice(128, 256))
    came = tuple(slice(n.start + 256, n.stop + 256) for n in nodes)
    bias = [jnp.sum(grad[n].astype(F32), axis=0, keepdims=True) for n in nodes]
    bias += [jnp.sum(got[n].astype(F32), axis=0, keepdims=True) for n in came]
    bias = (bias[0] + bias[1]) + (bias[2] + bias[3])
    bias = jnp.broadcast_to(bias, (BIAS_ROWS, 512))

    def emit(lhs):
        for m in range(4):
            begin = pl.multiple_of((place[0] ^ m) * 128, 128)
            columns = pl.ds(begin, 128)
            mine = [
                lax.dot_general(
                    lhs[n, columns], grad[n], CONTRACT_ROWS, preferred_element_type=F32
                )
                for n in nodes
            ]
            theirs = [
                lax.dot_general(got[n, columns], got[g], CONTRACT_ROWS, preferred_element_type=F32)
                for n, g in zip(nodes, came)
            ]
            out = keep_out if m < 2 else give_out
            out[m % 2, :128, :] = ((mine[0] + mine[1]) + (theirs[0] + theirs[1])).astype(out.dtype)
            out[m % 2, 128:, :] = bias.astype(out.dtype)

    @pl.when(place[1] == 0)
    def _():
        emit(feat)

    @pl.when(place[1] != 0)
    def _():
        emit(mean)


def weights(place, feat, mean, grad, got):
    piece = (2, CHUNK, 512)
    return call(
        weights_kernel,
        [shaped(piece, F32), shaped(piece, BF)],
        (place, feat, mean, grad, got),
        [SMEM] + [VMEM] * 4,
        flops=4 * 128 * 512 * 512,
    )


def halve_kernel(own, got, keep, give):
    half = keep.shape[0]
    for k in range(half):
        keep[k] = own[k] + got[k].astype(F32)
        give[k] = (own[half + k] + got[half + k].astype(F32)).astype(BF)


def halve(own, got):
    piece = (own.shape[0] // 2,) + own.shape[1:]
    return call(halve_kernel, [shaped(piece, F32), shaped(piece, BF)], (own, got), [VMEM] * 2)


def arrange_kernel(own, place, blocks, *refs):
    (self_out, neigh_out), (full, sem) = refs[-4:-2], refs[-2:]
    for m in range(4):
        rows = pl.ds(pl.multiple_of((place[0] ^ m) * 128, 128), 128)
        full[rows, :] = blocks[128 * m : 128 * m + 128].astype(F32)

    @pl.when(place[1] == (0 if own else 1))
    def _():
        copy = pltpu.make_async_copy(full, self_out, sem)
        copy.start()
        copy.wait()

    @pl.when(place[1] == (1 if own else 0))
    def _():
        copy = pltpu.make_async_copy(full, neigh_out, sem)
        copy.start()
        copy.wait()


def arrange(place, blocks, before=()):
    out = shaped((512, 512), F32)
    own = not before
    return pl.pallas_call(
        functools.partial(arrange_kernel, own),
        out_shape=(out, out),
        in_specs=[SMEM, VMEM] + [ANY] * len(before),
        out_specs=(ANY, ANY),
        scratch_shapes=[pltpu.VMEM((512, 512), F32), pltpu.SemaphoreType.DMA],
        input_output_aliases={} if own else {2: 0, 3: 1},
        compiler_params=pltpu.CompilerParams(vmem_limit_bytes=8 * MIB),
        cost_estimate=pl.CostEstimate(flops=0, bytes_accessed=3 * MIB, transcendentals=0),
    )(place, blocks, *before)


def ring_sum(value, **axis):
    (name,) = axis
    sent = value.astype(BF)
    got = {k: shift(sent, **{name: k}).astype(F32) for k in others(name)}
    return (sent.astype(F32) + got[2]) + (got[1] + got[3])


def meet_sum(value, **axis):
    sent = value.astype(BF)
    return sent.astype(F32) + meet(sent, **axis).astype(F32)


def local(
    features, cotangent, w_self, w_neigh, out_bias, block_vals, block_rows, block_cols, block_count
):
    device = lax.axis_index("row") * 32 + lax.axis_index("col")
    my_zh, my_core, my_zl, my_x, my_y = coords(device)
    slots = block_vals.shape[0]
    live = jnp.arange(slots, dtype=jnp.int32) < block_count[0]
    rel_z = (block_rows // 16 - my_zl) % ZL
    rel_x = (block_rows // 4 % 4 - my_x) % X
    rel_y = (block_rows % 4 - my_y) % Y
    rows_a = rel_x * 8 + rel_y * 2 + rel_z
    rows_b = rel_y * 8 + rel_x * 2 + rel_z
    place_a = jnp.where(live, rows_a, 32)
    place_b = jnp.where(live, rows_b, 32)
    rel_h = (block_cols // 2 - my_zh) % ZH
    rel_c = (block_cols % 2 - my_core) % CORE
    source = rel_h * 2 + rel_c
    far_a_place = jnp.where(live & (rel_x == 2), rows_a - 16, 8)
    far_b_place = jnp.where(live & (rel_y == 2), rows_b - 16, 8)
    far = live & ((rel_x == 2) | (rel_y == 2))
    slot = jnp.arange(slots, dtype=jnp.int32)
    ahead_of = (far[None, :] & ~far[:, None]) | (
        (far[None, :] == far[:, None]) & (slot[None, :] < slot[:, None])
    )
    rank = jnp.sum(ahead_of.astype(jnp.int32), axis=1)
    order = jnp.sum(jnp.where(rank[None, :] == slot[:, None], slot[None, :], 0), axis=1)
    far_count = jnp.sum(far.astype(jnp.int32)).reshape(1)
    back_place = jnp.where(live, rel_c * 4 + rel_h, 8)

    place = jnp.stack([my_x, my_core]).astype(jnp.int32)

    ahead = {k: shift(features, zh=-k) for k in others("zh")}
    weight, near_vals, ahead[0] = row_weights(block_count, place_a, block_vals, features)
    ahead[1], weight, order, far_count, far_a_place, far_b_place, source = (
        lax.optimization_barrier(
            (ahead[1], weight, order, far_count, far_a_place, far_b_place, source)
        )
    )
    pieces = []
    for k in range(4):
        pieces += [ahead[k], shift(ahead[k] if k else features, core=1)]

    low_a, high_a, low_b, high_b = opposite(
        far_count, order, far_a_place, far_b_place, source, near_vals, weight, pieces
    )
    later, low_a = lax.optimization_barrier((near_vals, low_a))
    total_a, total_b = forward(block_count, place_a, place_b, source, later, weight, pieces)
    low_a, high_a = shift(low_a, x=1), shift(high_a, x=-1)
    low_b, high_b = shift(low_b, y=1), shift(high_b, y=-1)
    ahead_a, behind_a = pass_on(True, total_a, weight, low_a, high_a)
    ahead_b, behind_b = pass_on(False, total_b, weight, low_b, high_b)
    got_a = [shift(ahead_a, x=1), shift(behind_a, x=-1)]
    got_b = [shift(ahead_b, y=1), shift(behind_b, y=-1)]

    later, _ = lax.optimization_barrier(((features, cotangent, block_vals), ahead_a))
    feat_late, cot_late, vals_late = later
    late = shift(jnp.concatenate([feat_late, cot_late]), zl=1)
    both_feat = jnp.concatenate([feat_late, late[:128]])
    both_cot = jnp.concatenate([cot_late, late[128:]])
    self_pre = jnp.dot(both_feat, w_self, preferred_element_type=F32) + out_bias
    turned = turn(vals_late)
    (got_a, got_b), self_pre, both_cot, turned = lax.optimization_barrier(
        ((got_a, got_b), self_pre, both_cot, turned)
    )

    parts_a = merge(True, total_a, weight, *got_a)
    got_a = [shift(parts_a[k], y=k) for k in others("y")]
    parts_b = merge(False, total_b, weight, *got_b)
    got_b = [shift(parts_b[k], x=k) for k in others("x")]
    given = join([parts_a[0], *got_a], [parts_b[0], *got_b])
    layer_out, mean_agg, grad_pre, back_a, back_b, send = node(
        place, given, shift(given, zl=1), both_feat, self_pre, both_cot, w_neigh
    )

    near_a, near_b = {0: back_a}, {0: back_b}
    for k in others("y"):
        near_a[k] = shift(back_a, y=-k)
        near_b[k] = shift(back_b, x=-k)
    own_a = jnp.concatenate([near_a[k] for k in range(4)])
    own_b = jnp.concatenate([near_b[k] for k in range(4)])

    got = shift(send, core=1)
    keep_part, give_part = weights(place, both_feat, mean_agg, grad_pre, got)
    came, own_b = lax.optimization_barrier((meet(give_part, x=2), own_b))
    keep_part, give_part = halve(keep_part, came)
    give_part, own_a, own_b = lax.optimization_barrier((give_part, own_a, own_b))
    next_a, last_a = shift(own_a, x=-1), shift(own_a, x=1)
    next_b, last_b = shift(own_b, y=-1), shift(own_b, y=1)
    low_a, high_a = shift(last_a[:512], x=1), shift(next_a[512:], x=-1)
    low_b, high_b = shift(last_b[:512], y=1), shift(next_b[512:], y=-1)
    chunk = keep_part[0] + meet(give_part[0], x=1).astype(F32)
    chunk = meet_sum(chunk, zh=1)
    chunk = meet_sum(chunk, zh=2)

    grad_self = lax.dot_general(grad_pre[:128], w_self, CONTRACT_COLS, preferred_element_type=F32)
    own, give = backward(
        block_count,
        rows_a,
        rows_b,
        back_place,
        turned,
        [own_a, next_a, low_a, high_a, last_a],
        [own_b, next_b, low_b, high_b, last_b],
    )
    parts = pair(own, shift(give, core=1))
    chunk = ring_sum(chunk, y=1)
    scale = 1.0 / math.sqrt(128 * DEVICES)
    bias_grad = chunk[128] * scale
    block = (chunk[:128] * scale).astype(BF)
    block, parts = lax.optimization_barrier((block, parts))
    block = jnp.concatenate([block] + [meet(block, x=m) for m in (1, 2, 3)])
    feature_grad = total(grad_self, parts[0], [shift(parts[k], zh=k) for k in others("zh")])
    self_grad, neigh_grad = arrange(place, shift(block, core=1), arrange(place, block))
    return layer_out, feature_grad, self_grad, neigh_grad, bias_grad


def solution(mesh):
    return jax.shard_map(
        local,
        mesh=mesh,
        in_specs=(
            P(("row", "col"), None),
            P(("row", "col"), None),
            P(),
            P(),
            P(),
            P(("row", "col"), None, None),
            P(("row", "col")),
            P(("row", "col")),
            P(("row", "col")),
        ),
        out_specs=(P(("row", "col"), None), P(("row", "col"), None), P(), P(), P()),
        check_vma=False,
    )
```

```python
import functools
import math

import jax
import jax.numpy as jnp
from jax import lax
from jax.experimental import pallas as pl
from jax.experimental.pallas import tpu as pltpu
from jax.sharding import PartitionSpec as P

BF = jnp.bfloat16
F32 = jnp.float32
AXES = ("row", "col")
ZH, CORE, ZL, X, Y = 4, 2, 2, 4, 4
DEVICES = ZH * CORE * ZL * X * Y
VMEM = pl.BlockSpec(memory_space=pltpu.VMEM)
SMEM = pl.BlockSpec(memory_space=pltpu.SMEM)
ANY = pl.BlockSpec(memory_space=pl.ANY)
CONTRACT_ROWS = (((0,), (0,)), ((), ()))
CONTRACT_COLS = (((1,), (1,)), ((), ()))
MIB = 1 << 20


def coords(device):
    y = device % Y
    x = device // Y % X
    zl = device // (Y * X) % ZL
    core = device // (Y * X * ZL) % CORE
    zh = device // (Y * X * ZL * CORE)
    return zh, core, zl, x, y


def shift(value, zh=0, core=0, zl=0, x=0, y=0):
    pairs = []
    for device in range(DEVICES):
        a, b, c, d, e = coords(device)
        a, b, c, d, e = (a + zh) % ZH, (b + core) % CORE, (c + zl) % ZL, (d + x) % X, (e + y) % Y
        pairs.append((device, (((a * CORE + b) * ZL + c) * X + d) * Y + e))
    return lax.ppermute(value, AXES, pairs)


def meet(value, **axis):
    ((name, bit),) = axis.items()
    at = ("zh", "core", "zl", "x", "y").index(name)
    pairs = []
    for device in range(DEVICES):
        place = list(coords(device))
        place[at] ^= bit
        a, b, c, d, e = place
        pairs.append((device, (((a * CORE + b) * ZL + c) * X + d) * Y + e))
    return lax.ppermute(value, AXES, pairs)


def others(axis):
    return (2, 1, 3)


def call(kernel, outs, args, specs, scratch=(), flops=0, own=0):
    size = sum(math.prod(o.shape) * o.dtype.itemsize for o in outs)
    size += sum(math.prod(a.shape) * a.dtype.itemsize for a in args)
    return pl.pallas_call(
        kernel,
        out_shape=tuple(outs),
        in_specs=list(specs),
        out_specs=(VMEM,) * len(outs),
        scratch_shapes=list(scratch),
        compiler_params=pltpu.CompilerParams(vmem_limit_bytes=size + own + 3 * MIB),
        cost_estimate=pl.CostEstimate(flops=flops, bytes_accessed=size, transcendentals=0),
    )(*args)


def shaped(shape, dtype):
    return jax.ShapeDtypeStruct(shape, dtype)


def row_weights_kernel(count, place, vals, feat, weights, vals_out, feat_out):
    feat_out[...] = feat[...]

    def keep(i, carry):
        for u in range(GROUP):
            vals_out[i * GROUP + u] = vals[i * GROUP + u]
        return carry

    lax.fori_loop(0, vals.shape[0] // GROUP, keep, 0)
    weights[...] = jnp.zeros_like(weights)
    ones = jnp.ones((8, 128), BF)

    def step(i, carry):
        slots = [i * GROUP + u for u in range(GROUP)]
        sums = [
            lax.dot_general(ones, vals[s], CONTRACT_COLS, preferred_element_type=F32) for s in slots
        ]
        for s, term in zip(slots, sums):
            weights[place[s]] += term
        return carry

    lax.fori_loop(0, (count[0] + GROUP - 1) // GROUP, step, 0)


def row_weights(count, place, vals, feat):
    return call(
        row_weights_kernel,
        [shaped((33, 8, 128), F32), shaped(vals.shape, BF), shaped(feat.shape, BF)],
        (count, place, vals, feat),
        [SMEM, SMEM, VMEM, VMEM],
    )


def turn_kernel(vals, turned):
    def step(i, carry):
        for u in range(GROUP):
            turned[i * GROUP + u] = vals[i * GROUP + u].T
        return carry

    lax.fori_loop(0, vals.shape[0] // GROUP, step, 0)


def turn(vals):
    return call(turn_kernel, [shaped(vals.shape, BF)], (vals,), [VMEM], flops=6 * 10**9)[0]


GROUP = 4
TURN = 16
BACKWARD_COST = 20 * 10**9
PAIR_COST = 5 * 10**9
TOTAL_COST = 5 * 10**9
PAD = 16


def put_weights(out, rows, value):
    count = value.shape[0]
    if out.dtype == F32:
        out[rows : rows + count, :128] = value
        return
    out[rows:, :] = jnp.zeros((PAD, out.shape[1]), out.dtype)
    lead = value.astype(BF)
    trail = (value - lead.astype(F32)).astype(BF)
    both = jnp.concatenate([lead.astype(F32), trail.astype(F32)], axis=1)
    both = jnp.concatenate([both, jnp.zeros((PAD - count, 256), F32)], axis=0)
    out[rows:, :256] = both.astype(BF)


def get_weights(ref, rows, count):
    got = ref[rows : rows + PAD, :256].astype(F32)[:count]
    if ref.dtype == F32:
        return got[:, :128]
    return got[:, :128] + got[:, 128:]


def forward_kernel(count, place_a, place_b, source, vals, weights, *refs):
    pieces, (total_a, total_b), (panel, sems) = refs[:8], refs[8:10], refs[10:]
    copies = [
        pltpu.make_async_copy(piece, panel.at[k], sems.at[k]) for k, piece in enumerate(pieces)
    ]
    for copy in copies:
        copy.start()

    def clear(k, carry):
        total_a[k] = jnp.zeros((128, 256), F32)
        total_b[k] = jnp.zeros((128, 256), F32)
        return carry

    lax.fori_loop(0, 33, clear, 0)
    for copy in copies:
        copy.wait()

    def step(i, carry):
        for u in range(TURN):
            s = i * TURN + u
            term = jnp.dot(vals[s], panel[source[s]], preferred_element_type=F32)
            total_a[place_a[s]] += term[:, :256]
            total_b[place_b[s]] += term[:, 256:]
        return carry

    lax.fori_loop(0, (count[0] + TURN - 1) // TURN, step, 0)


def opposite_kernel(count, order, place_a, place_b, source, vals, weights, panel, *refs):
    low_a, high_a, low_b, high_b, total_a, total_b = refs

    def clear(k, carry):
        total_a[k] = jnp.zeros((128, 256), F32)
        total_b[k] = jnp.zeros((128, 256), F32)
        return carry

    lax.fori_loop(0, 9, clear, 0)
    def step(i, carry):
        for u in range(8):
            s = order[i * 8 + u]
            rows = pl.ds(pl.multiple_of(source[s] * 128, 128), 128)
            term = jnp.dot(vals[s], panel[rows, :], preferred_element_type=F32)
            total_a[place_a[s]] += term[:, :256]
            total_b[place_b[s]] += term[:, 256:]
        return carry

    lax.fori_loop(0, (count[0] + 7) // 8, step, 0)

    def finish(k, carry):
        rows = pl.ds(pl.multiple_of(k * 128, 128), 128)
        low_a[rows, :] = total_a[k].astype(BF)
        high_a[rows, :] = total_a[4 + k].astype(BF)
        low_b[rows, :] = total_b[k].astype(BF)
        high_b[rows, :] = total_b[4 + k].astype(BF)
        return carry

    lax.fori_loop(0, 4, finish, 0)
    put_weights(low_a, 512, rows_of(weights, 16, 4))
    put_weights(high_a, 512, rows_of(weights, 20, 4))


def opposite(count, order, place_a, place_b, source, vals, weights, panel):
    cut = shaped((512 + PAD, 256), BF)
    plain = shaped((512, 256), BF)
    return call(
        opposite_kernel,
        [cut, cut, plain, plain],
        (count, order, place_a, place_b, source, vals, weights, panel),
        [SMEM] * 5 + [VMEM] * 3,
        [pltpu.VMEM((9, 128, 256), F32), pltpu.VMEM((9, 128, 256), F32)],
        flops=2 * 24 * 128 * 128 * 512,
        own=4 * MIB,
    )


def rows_of(weights, begin, count):
    return jnp.concatenate([weights[begin + k, 0:1, :] for k in range(count)], axis=0)


def forward(count, place_a, place_b, source, vals, weights, pieces):
    full = shaped((33, 128, 256), F32)
    return call(
        forward_kernel,
        [full, full],
        (count, place_a, place_b, source, vals, weights, *pieces),
        [SMEM] * 4 + [VMEM] * 2 + [ANY] * 8,
        [pltpu.VMEM((8, 128, 512), BF), pltpu.SemaphoreType.DMA((8,))],
        flops=2 * 48 * 128 * 128 * 512,
        own=4 * MIB,
    )


def pass_kernel(carries, total, weights, low, high, ahead_out, behind_out):
    def first(k, carry):
        rows = pl.ds(pl.multiple_of(k * 128, 128), 128)
        later = pl.ds(pl.multiple_of(512 + k * 128, 128), 128)
        ahead_out[rows, :] = (total[8 + k] + low[rows, :].astype(F32)).astype(BF)
        ahead_out[later, :] = total[12 + k].astype(BF)
        behind_out[rows, :] = total[24 + k].astype(BF)
        behind_out[later, :] = (total[28 + k] + high[rows, :].astype(F32)).astype(BF)
        return carry

    lax.fori_loop(0, 4, first, 0)
    if carries:
        none = jnp.zeros((4, 128), F32)
        low_weight = jnp.concatenate([get_weights(low, 512, 4), none], axis=0)
        high_weight = jnp.concatenate([none, get_weights(high, 512, 4)], axis=0)
        put_weights(ahead_out, 1024, rows_of(weights, 8, 8) + low_weight)
        put_weights(behind_out, 1024, rows_of(weights, 24, 8) + high_weight)


def pass_on(carries, total, weights, low, high):
    out = shaped((1024 + (PAD if carries else 0), 256), BF)
    return call(
        functools.partial(pass_kernel, carries),
        [out, out],
        (total, weights, low, high),
        [VMEM] * 4,
    )


def merge_kernel(carries, own, weights, a, b, *outs):
    for part, out in enumerate(outs):
        for k in range(2):
            rows = slice(256 * part + 128 * k, 256 * part + 128 * k + 128)
            total = own[2 * part + k] + a[rows].astype(F32) + b[rows].astype(F32)
            out[128 * k : 128 * k + 128] = total.astype(out.dtype)
    if carries:
        weight = rows_of(weights, 0, 8) + get_weights(a, 1024, 8) + get_weights(b, 1024, 8)
        for part, out in enumerate(outs):
            put_weights(out, 256, weight[2 * part : 2 * part + 2])


def merge(carries, own, weights, a, b):
    rows = 256 + (PAD if carries else 0)
    return call(
        functools.partial(merge_kernel, carries),
        [shaped((rows, 256), F32)] + [shaped((rows, 256), BF)] * 3,
        (own, weights, a, b),
        [VMEM] * 4,
    )


def join_kernel(*refs):
    parts_a, parts_b, give = refs[:4], refs[4:8], refs[8]
    for at, parts in ((0, parts_a), (256, parts_b)):
        total = parts[0][:256]
        for part in parts[1:]:
            total += part[:256].astype(F32)
        give[:256, at : at + 256] = total.astype(BF)
    put_weights(give, 256, sum(get_weights(ref, 256, 2) for ref in parts_a))


def join(parts_a, parts_b):
    return call(
        join_kernel,
        [shaped((256 + PAD, 512), BF)],
        (*parts_a, *parts_b),
        [VMEM] * 8,
    )[0]


def node_kernel(
    place, given, got, feat, self_pre, cot, w_neigh, layer_out, mean_out, grad_out, back_a, back_b, send
):
    @pl.when(place[1] != 0)
    def _():
        send[:256, :] = feat[...]

    def spread(row):
        wide = jnp.broadcast_to(1.0 / row, (128, 128)).T
        return jnp.concatenate([wide] * 4, axis=1)

    weight, came = get_weights(given, 256, 2), get_weights(got, 256, 2)
    inverse = [spread(1.0 + (weight[k : k + 1, :] + came[1 - k : 2 - k, :])) for k in range(2)]
    inverse = jnp.concatenate(inverse, axis=0)
    other = jnp.concatenate([got[128:256], got[0:128]], axis=0)
    mean = ((given[0:256].astype(F32) + other.astype(F32)) * inverse).astype(BF)
    pre_act = self_pre[...] + jnp.dot(mean, w_neigh[...], preferred_element_type=F32)
    sigmoid_val = jax.nn.sigmoid(pre_act)
    grad = cot[...].astype(F32) * sigmoid_val * (1.0 + pre_act * (1.0 - sigmoid_val))
    grad = grad.astype(BF)
    back_mean = lax.dot_general(grad, w_neigh[...], CONTRACT_COLS, preferred_element_type=F32)
    scaled = (back_mean * inverse).astype(BF)
    back_a[...] = scaled[:, :256]
    back_b[...] = scaled[:, 256:]
    mean_out[...] = mean
    grad_out[...] = grad
    send[256:, :] = grad
    layer_out[...] = (pre_act[:128] * sigmoid_val[:128]).astype(BF)

    @pl.when(place[1] == 0)
    def _():
        send[:256, :] = mean


def node(place, given, got, feat, self_pre, cot, w_neigh):
    wide = shaped((256, 512), BF)
    half = shaped((256, 256), BF)
    return call(
        node_kernel,
        [shaped((128, 512), BF), wide, wide, half, half, shaped((512, 512), BF)],
        (place, given, got, feat, self_pre, cot, w_neigh),
        [SMEM] + [VMEM] * 6,
        flops=8 * 128 * 512 * 512,
    )


def backward_kernel(count, from_a, from_b, place, vals, *refs):
    parts_a, parts_b, outs = refs[:5], refs[5:10], refs[10:12]
    panel_a, panel_b, total, sems = refs[12:]
    copies = []
    begin = 0
    for k, (part_a, part_b) in enumerate(zip(parts_a, parts_b)):
        rows = pl.ds(begin, part_a.shape[0])
        begin += part_a.shape[0]
        copies.append(pltpu.make_async_copy(part_a, panel_a.at[rows], sems.at[k]))
        copies.append(pltpu.make_async_copy(part_b, panel_b.at[rows], sems.at[5 + k]))
    for copy in copies:
        copy.start()

    def clear(k, carry):
        total[k] = jnp.zeros((128, 512), F32)
        return carry

    lax.fori_loop(0, 9, clear, 0)
    for copy in copies:
        copy.wait()

    def step(i, carry):
        for u in range(TURN):
            s = i * TURN + u
            block = vals[s]
            rows_a = pl.ds(pl.multiple_of(from_a[s] * 128, 128), 128)
            rows_b = pl.ds(pl.multiple_of(from_b[s] * 128, 128), 128)
            first = jnp.dot(block, panel_a[rows_a, :], preferred_element_type=F32)
            second = jnp.dot(block, panel_b[rows_b, :], preferred_element_type=F32)
            total[place[s], :, :256] += first
            total[place[s], :, 256:] += second
        return carry

    lax.fori_loop(0, (count[0] + TURN - 1) // TURN, step, 0)

    def finish(k, carry):
        for part, out in enumerate(outs):
            out[k] = total[part * 4 + k].astype(out.dtype)
        return carry

    lax.fori_loop(0, 4, finish, 0)


def backward(count, from_a, from_b, place, turned, parts_a, parts_b):
    return call(
        backward_kernel,
        [shaped((4, 128, 512), F32), shaped((4, 128, 512), BF)],
        (count, from_a, from_b, place, turned, *parts_a, *parts_b),
        [SMEM] * 4 + [VMEM] + [ANY] * 10,
        [
            pltpu.VMEM((4096, 256), BF),
            pltpu.VMEM((4096, 256), BF),
            pltpu.VMEM((9, 128, 512), F32),
            pltpu.SemaphoreType.DMA((10,)),
        ],
        flops=BACKWARD_COST,
        own=4 * MIB,
    )


def pair_kernel(own, got, *outs):
    for k, out in enumerate(outs):
        out[...] = (own[k] + got[k].astype(F32)).astype(out.dtype)


def pair(own, got):
    piece = own.shape[1:]
    return call(
        pair_kernel,
        [shaped(piece, F32)] + [shaped(piece, BF)] * 3,
        (own, got),
        [VMEM] * 2,
        flops=PAIR_COST,
    )


def total_kernel(product, own, a, b, c, out):
    total = own[...] + a[...].astype(F32) + b[...].astype(F32) + c[...].astype(F32)
    out[...] = product[...] + total


def total(product, own, got):
    return call(
        total_kernel,
        [shaped((128, 512), F32)],
        (product, own, *got),
        [VMEM] * 5,
        flops=TOTAL_COST,
    )[0]


BIAS_ROWS = 16
CHUNK = 128 + BIAS_ROWS


def weights_kernel(place, feat, mean, grad, got, keep_out, give_out):
    nodes = (slice(0, 128), slice(128, 256))
    came = tuple(slice(n.start + 256, n.stop + 256) for n in nodes)
    bias = [jnp.sum(grad[n].astype(F32), axis=0, keepdims=True) for n in nodes]
    bias += [jnp.sum(got[n].astype(F32), axis=0, keepdims=True) for n in came]
    bias = (bias[0] + bias[1]) + (bias[2] + bias[3])
    bias = jnp.broadcast_to(bias, (BIAS_ROWS, 512))

    def emit(lhs):
        for m in range(4):
            begin = pl.multiple_of((place[0] ^ m) * 128, 128)
            columns = pl.ds(begin, 128)
            mine = [
                lax.dot_general(
                    lhs[n, columns], grad[n], CONTRACT_ROWS, preferred_element_type=F32
                )
                for n in nodes
            ]
            theirs = [
                lax.dot_general(got[n, columns], got[g], CONTRACT_ROWS, preferred_element_type=F32)
                for n, g in zip(nodes, came)
            ]
            out = keep_out if m < 2 else give_out
            out[m % 2, :128, :] = ((mine[0] + mine[1]) + (theirs[0] + theirs[1])).astype(out.dtype)
            out[m % 2, 128:, :] = bias.astype(out.dtype)

    @pl.when(place[1] == 0)
    def _():
        emit(feat)

    @pl.when(place[1] != 0)
    def _():
        emit(mean)


def weights(place, feat, mean, grad, got):
    piece = (2, CHUNK, 512)
    return call(
        weights_kernel,
        [shaped(piece, F32), shaped(piece, BF)],
        (place, feat, mean, grad, got),
        [SMEM] + [VMEM] * 4,
        flops=4 * 128 * 512 * 512,
    )


def halve_kernel(own, got, keep, give):
    half = keep.shape[0]
    for k in range(half):
        keep[k] = own[k] + got[k].astype(F32)
        give[k] = (own[half + k] + got[half + k].astype(F32)).astype(BF)


def halve(own, got):
    piece = (own.shape[0] // 2,) + own.shape[1:]
    return call(halve_kernel, [shaped(piece, F32), shaped(piece, BF)], (own, got), [VMEM] * 2)


def arrange_kernel(own, place, blocks, *refs):
    (self_out, neigh_out), (full, sem) = refs[-4:-2], refs[-2:]
    for m in range(4):
        rows = pl.ds(pl.multiple_of((place[0] ^ m) * 128, 128), 128)
        full[rows, :] = blocks[128 * m : 128 * m + 128].astype(F32)

    @pl.when(place[1] == (0 if own else 1))
    def _():
        copy = pltpu.make_async_copy(full, self_out, sem)
        copy.start()
        copy.wait()

    @pl.when(place[1] == (1 if own else 0))
    def _():
        copy = pltpu.make_async_copy(full, neigh_out, sem)
        copy.start()
        copy.wait()


def arrange(place, blocks, before=()):
    out = shaped((512, 512), F32)
    own = not before
    return pl.pallas_call(
        functools.partial(arrange_kernel, own),
        out_shape=(out, out),
        in_specs=[SMEM, VMEM] + [ANY] * len(before),
        out_specs=(ANY, ANY),
        scratch_shapes=[pltpu.VMEM((512, 512), F32), pltpu.SemaphoreType.DMA],
        input_output_aliases={} if own else {2: 0, 3: 1},
        compiler_params=pltpu.CompilerParams(vmem_limit_bytes=8 * MIB),
        cost_estimate=pl.CostEstimate(flops=0, bytes_accessed=3 * MIB, transcendentals=0),
    )(place, blocks, *before)


def ring_sum(value, **axis):
    (name,) = axis
    sent = value.astype(BF)
    got = {k: shift(sent, **{name: k}).astype(F32) for k in others(name)}
    return (sent.astype(F32) + got[2]) + (got[1] + got[3])


def meet_sum(value, **axis):
    sent = value.astype(BF)
    return sent.astype(F32) + meet(sent, **axis).astype(F32)


def local(
    features, cotangent, w_self, w_neigh, out_bias, block_vals, block_rows, block_cols, block_count
):
    device = lax.axis_index("row") * 32 + lax.axis_index("col")
    my_zh, my_core, my_zl, my_x, my_y = coords(device)
    slots = block_vals.shape[0]
    live = jnp.arange(slots, dtype=jnp.int32) < block_count[0]
    rel_z = (block_rows // 16 - my_zl) % ZL
    rel_x = (block_rows // 4 % 4 - my_x) % X
    rel_y = (block_rows % 4 - my_y) % Y
    rows_a = rel_x * 8 + rel_y * 2 + rel_z
    rows_b = rel_y * 8 + rel_x * 2 + rel_z
    place_a = jnp.where(live, rows_a, 32)
    place_b = jnp.where(live, rows_b, 32)
    rel_h = (block_cols // 2 - my_zh) % ZH
    rel_c = (block_cols % 2 - my_core) % CORE
    source = rel_h * 2 + rel_c
    far_a_place = jnp.where(live & (rel_x == 2), rows_a - 16, 8)
    far_b_place = jnp.where(live & (rel_y == 2), rows_b - 16, 8)
    far = live & ((rel_x == 2) | (rel_y == 2))
    slot = jnp.arange(slots, dtype=jnp.int32)
    ahead_of = (far[None, :] & ~far[:, None]) | (
        (far[None, :] == far[:, None]) & (slot[None, :] < slot[:, None])
    )
    rank = jnp.sum(ahead_of.astype(jnp.int32), axis=1)
    order = jnp.sum(jnp.where(rank[None, :] == slot[:, None], slot[None, :], 0), axis=1)
    far_count = jnp.sum(far.astype(jnp.int32)).reshape(1)
    back_place = jnp.where(live, rel_c * 4 + rel_h, 8)

    place = jnp.stack([my_x, my_core]).astype(jnp.int32)

    ahead = {k: shift(features, zh=-k) for k in others("zh")}
    weight, near_vals, ahead[0] = row_weights(block_count, place_a, block_vals, features)
    ahead[1], weight, order, far_count, far_a_place, far_b_place, source = (
        lax.optimization_barrier(
            (ahead[1], weight, order, far_count, far_a_place, far_b_place, source)
        )
    )
    pieces = []
    for k in range(4):
        pieces += [ahead[k], shift(ahead[k] if k else features, core=1)]

    low_a, high_a, low_b, high_b = opposite(
        far_count,
        order,
        far_a_place,
        far_b_place,
        source,
        near_vals,
        weight,
        jnp.concatenate(pieces),
    )
    later, low_a = lax.optimization_barrier((near_vals, low_a))
    total_a, total_b = forward(block_count, place_a, place_b, source, later, weight, pieces)
    low_a, high_a = shift(low_a, x=1), shift(high_a, x=-1)
    low_b, high_b = shift(low_b, y=1), shift(high_b, y=-1)
    ahead_a, behind_a = pass_on(True, total_a, weight, low_a, high_a)
    ahead_b, behind_b = pass_on(False, total_b, weight, low_b, high_b)
    got_a = [shift(ahead_a, x=1), shift(behind_a, x=-1)]
    got_b = [shift(ahead_b, y=1), shift(behind_b, y=-1)]

    later, _ = lax.optimization_barrier(((features, cotangent, block_vals), ahead_a))
    feat_late, cot_late, vals_late = later
    late = shift(jnp.concatenate([feat_late, cot_late]), zl=1)
    both_feat = jnp.concatenate([feat_late, late[:128]])
    both_cot = jnp.concatenate([cot_late, late[128:]])
    self_pre = jnp.dot(both_feat, w_self, preferred_element_type=F32) + out_bias
    turned = turn(vals_late)
    (got_a, got_b), self_pre, both_cot, turned = lax.optimization_barrier(
        ((got_a, got_b), self_pre, both_cot, turned)
    )

    parts_a = merge(True, total_a, weight, *got_a)
    got_a = [shift(parts_a[k], y=k) for k in others("y")]
    parts_b = merge(False, total_b, weight, *got_b)
    got_b = [shift(parts_b[k], x=k) for k in others("x")]
    given = join([parts_a[0], *got_a], [parts_b[0], *got_b])
    layer_out, mean_agg, grad_pre, back_a, back_b, send = node(
        place, given, shift(given, zl=1), both_feat, self_pre, both_cot, w_neigh
    )

    near_a, near_b = {0: back_a}, {0: back_b}
    for k in others("y"):
        near_a[k] = shift(back_a, y=-k)
        near_b[k] = shift(back_b, x=-k)
    own_a = jnp.concatenate([near_a[k] for k in range(4)])
    own_b = jnp.concatenate([near_b[k] for k in range(4)])

    got = shift(send, core=1)
    keep_part, give_part = weights(place, both_feat, mean_agg, grad_pre, got)
    came, own_b = lax.optimization_barrier((meet(give_part, x=2), own_b))
    keep_part, give_part = halve(keep_part, came)
    give_part, own_a, own_b = lax.optimization_barrier((give_part, own_a, own_b))
    next_a, last_a = shift(own_a, x=-1), shift(own_a, x=1)
    next_b, last_b = shift(own_b, y=-1), shift(own_b, y=1)
    low_a, high_a = shift(last_a[:512], x=1), shift(next_a[512:], x=-1)
    low_b, high_b = shift(last_b[:512], y=1), shift(next_b[512:], y=-1)
    chunk = keep_part[0] + meet(give_part[0], x=1).astype(F32)
    chunk = meet_sum(chunk, zh=1)
    chunk = meet_sum(chunk, zh=2)

    grad_self = lax.dot_general(grad_pre[:128], w_self, CONTRACT_COLS, preferred_element_type=F32)
    own, give = backward(
        block_count,
        rows_a,
        rows_b,
        back_place,
        turned,
        [own_a, next_a, low_a, high_a, last_a],
        [own_b, next_b, low_b, high_b, last_b],
    )
    parts = pair(own, shift(give, core=1))
    chunk = ring_sum(chunk, y=1)
    scale = 1.0 / math.sqrt(128 * DEVICES)
    bias_grad = chunk[128] * scale
    block = (chunk[:128] * scale).astype(BF)
    block, parts = lax.optimization_barrier((block, parts))
    block = jnp.concatenate([block] + [meet(block, x=m) for m in (1, 2, 3)])
    feature_grad = total(grad_self, parts[0], [shift(parts[k], zh=k) for k in others("zh")])
    self_grad, neigh_grad = arrange(place, shift(block, core=1), arrange(place, block))
    return layer_out, feature_grad, self_grad, neigh_grad, bias_grad


def solution(mesh):
    return jax.shard_map(
        local,
        mesh=mesh,
        in_specs=(
            P(("row", "col"), None),
            P(("row", "col"), None),
            P(),
            P(),
            P(),
            P(("row", "col"), None, None),
            P(("row", "col")),
            P(("row", "col")),
            P(("row", "col")),
        ),
        out_specs=(P(("row", "col"), None), P(("row", "col"), None), P(), P(), P()),
        check_vma=False,
    )
```
